128 devices in a mesh: rows: 8 (over y_lo, z), cols: 16 (over y_hi, x, core).
Axes of the slice: x: 4, y: 4 (y_hi: 2, y_lo: 2; y = y_hi * 2 + y_lo), z: 4, core: 2. Of those that a mesh axis runs over, the one named last changes fastest.
Arguments:
- features: bfloat16 [128, 1024, 180], P('rows', 'cols'), may hold values from -8 to 8
- gain_one: float32 [180], replicated, may hold values from 0.1 to 1.9
- qkv_weight: bfloat16 [180, 540], replicated, may hold values from -4 to 4
- bias_table: float32 [1521, 6], replicated, may hold values from -4 to 4
- proj_weight: bfloat16 [180, 180], replicated, may hold values from -0.4375 to 0.4375
- gain_two: float32 [180], replicated, may hold values from 0.1 to 1.9
- hidden_weight: bfloat16 [180, 360], replicated, may hold values from -0.4375 to 0.4375
- output_weight: bfloat16 [360, 180], replicated, may hold values from -0.3125 to 0.3125
- group_conv: bfloat16 [3, 3, 180, 180], replicated, may hold values from -0.15625 to 0.15625
- before_conv: bfloat16 [3, 3, 180, 64], replicated, may hold values from -0.15625 to 0.15625
- upsample_conv: bfloat16 [3, 3, 64, 256], replicated, may hold values from -0.25 to 0.25
Outputs:
- upscaled: bfloat16 [64, 256, 2048], P(None, 'rows', 'cols')
The draws below stay inside these ranges and needn't reach their ends.
All inputs are finite; a program needn't handle non-finite values.
Results may differ from the reference program's by a relative error of at most 0.017.
Values may be sent and summed in bfloat16 or wider, within the bound.
A program may use at most 128 MiB of HBM per device.

```python
import jax
import jax.numpy as jnp
import numpy as np
from jax import lax

C = 180
HEADS = 6
MLP = 360
NF = 64
WIN = 16
KWIN = 24
TABLE = 1521
NR = 128
NC = 1024


def draw_features(key, part):
    key = jax.random.fold_in(key, 3)
    noise = jax.random.normal(jax.random.fold_in(key, 1), (NR, NC, C), jnp.float32)
    values = noise
    return jnp.clip(values, -8.0, 8.0).astype(jnp.bfloat16)


def draw_qkv_weight(key, part):
    key = jax.random.fold_in(key, 7)
    weight = jax.random.normal(jax.random.fold_in(key, 1), (C, 3 * C), jnp.float32) / jnp.sqrt(jnp.float32(C))
    return jnp.clip(weight, -4.0, 4.0).astype(jnp.bfloat16)


def normal_values(stream_key, shape, scale, bound, dtype=jnp.bfloat16):
    values = scale * jax.random.normal(stream_key, shape, jnp.float32)
    return jnp.clip(values, min=-bound, max=bound).astype(dtype)


def setup_inputs(seed: int = 0) -> dict:
    streams_of = jax.random.split(jax.random.key(seed), 12)
    return {
        "features": draw_features(jax.random.fold_in(streams_of[11], 71), 0),
        "gain_one": jnp.clip(1.0 + 0.18 * jax.random.normal(streams_of[1], (C,), jnp.float32), 0.1, 1.9),
        "qkv_weight": draw_qkv_weight(jax.random.fold_in(streams_of[11], 71), 0),
        "bias_table": normal_values(streams_of[3], (TABLE, HEADS), 1.0, 4.0, jnp.float32),
        "proj_weight": normal_values(streams_of[4], (C, C), C ** -0.5, 0.4375),
        "gain_two": jnp.clip(1.0 + 0.18 * jax.random.normal(streams_of[5], (C,), jnp.float32), 0.1, 1.9),
        "hidden_weight": normal_values(streams_of[6], (C, MLP), C ** -0.5, 0.4375),
        "output_weight": normal_values(streams_of[7], (MLP, C), MLP ** -0.5, 0.3125),
        "group_conv": normal_values(streams_of[8], (3, 3, C, C), (9 * C) ** -0.5, 0.15625),
        "before_conv": normal_values(streams_of[9], (3, 3, C, NF), (9 * C) ** -0.5, 0.15625),
        "upsample_conv": normal_values(streams_of[10], (3, 3, NF, 4 * NF), (9 * NF) ** -0.5, 0.25),
    }


def layer_norm(values, gain):
    center = values - lax.optimization_barrier(jnp.mean(values, axis=-1, keepdims=True))
    spread = lax.optimization_barrier(jnp.mean(center * center, axis=-1, keepdims=True))
    return center * lax.rsqrt(spread + 1e-05) * gain

def bias_indices():
    query_pos = np.arange(WIN)
    key_pos = np.arange(KWIN)
    offset = key_pos[None, :] - query_pos[:, None] + WIN - 1
    side = WIN + KWIN - 1
    full = offset[:, None, :, None] * side + offset[None, :, None, :]
    return full.reshape(WIN * WIN, KWIN * KWIN).astype(np.int32)

def query_windows(values):
    height, width, chans = values.shape
    blocks = values.reshape(height // WIN, WIN, width // WIN, WIN, chans)
    return blocks.transpose(0, 2, 1, 3, 4).reshape(-1, WIN * WIN, chans)

def undo_windows(values, height, width):
    chans = values.shape[-1]
    blocks = values.reshape(height // WIN, width // WIN, WIN, WIN, chans)
    return blocks.transpose(0, 2, 1, 3, 4).reshape(height, width, chans)

def key_windows(padded):
    span = KWIN - WIN
    height, width, chans = padded.shape
    nbr = height // span
    nbc = width // span
    blocks = padded.reshape(nbr, span, nbc, span, chans)
    stacked = jnp.stack([blocks[0:nbr - 1:2], blocks[1:nbr:2], blocks[2:nbr:2]], axis=1)
    stacked = jnp.stack([stacked[:, :, :, 0:nbc - 1:2], stacked[:, :, :, 1:nbc:2], stacked[:, :, :, 2:nbc:2]], axis=4)
    stacked = stacked.transpose(0, 3, 1, 2, 4, 5, 6)
    return stacked.reshape(-1, KWIN * KWIN, chans)

def attend_group(query_block, keyval_block, bias):
    groups = query_block.shape[0]
    chans = query_block.shape[-1]
    head_size = chans // HEADS
    qs = query_block.reshape(groups, WIN * WIN, HEADS, head_size).astype(jnp.float32)
    keys = keyval_block[..., :chans].reshape(groups, KWIN * KWIN, HEADS, head_size).astype(jnp.float32)
    vals = keyval_block[..., chans:].reshape(groups, KWIN * KWIN, HEADS, head_size).astype(jnp.float32)
    scores = jnp.einsum('gqhd,gkhd->ghqk', qs, keys) / jnp.sqrt(jnp.float32(head_size)) + bias[None]
    probs = jax.nn.softmax(scores, axis=-1).astype(jnp.bfloat16)
    result = jnp.einsum('ghqk,gkhd->gqhd', probs.astype(jnp.float32), vals)
    return result.reshape(groups, WIN * WIN, chans).astype(jnp.bfloat16)

def conv_last(padded, weight):
    height = padded.shape[0] - 2
    width = padded.shape[1] - 2
    total = jnp.zeros((height, width, weight.shape[3]), jnp.float32)
    for tap_r in range(3):
        for tap_c in range(3):
            total = total + jnp.dot(padded[tap_r:tap_r + height, tap_c:tap_c + width], weight[tap_r, tap_c], preferred_element_type=jnp.float32)
    return total

def conv_to_first(padded, weight):
    height = padded.shape[0] - 2
    width = padded.shape[1] - 2
    total = jnp.zeros((weight.shape[3], height, width), jnp.float32)
    for tap_r in range(3):
        for tap_c in range(3):
            total = total + jnp.einsum('hwc,co->ohw', padded[tap_r:tap_r + height, tap_c:tap_c + width].astype(jnp.float32), weight[tap_r, tap_c].astype(jnp.float32))
    return total

def conv_first(padded, weight):
    height = padded.shape[1] - 2
    width = padded.shape[2] - 2
    total = jnp.zeros((weight.shape[3], height, width), jnp.float32)
    for tap_r in range(3):
        for tap_c in range(3):
            total = total + jnp.einsum('chw,co->ohw', padded[:, tap_r:tap_r + height, tap_c:tap_c + width].astype(jnp.float32), weight[tap_r, tap_c].astype(jnp.float32))
    return total

def shuffle(expanded):
    chans4, height, width = expanded.shape
    chans = chans4 // 4
    parts = expanded.reshape(chans, 2, 2, height, width).transpose(0, 3, 1, 4, 2)
    return parts.reshape(chans, 2 * height, 2 * width)

def reference(features, gain_one, qkv_weight, bias_table, proj_weight, gain_two, hidden_weight, output_weight, group_conv, before_conv, upsample_conv):
    height, width, chans = features.shape
    rim = (KWIN - WIN) // 2
    base = features.astype(jnp.float32)
    normed = layer_norm(base, gain_one).astype(jnp.bfloat16)
    projected = jnp.dot(normed, qkv_weight, preferred_element_type=jnp.float32)
    queries = projected[..., :chans].astype(jnp.bfloat16)
    keyvals = projected[..., chans:].astype(jnp.bfloat16)
    padded = jnp.pad(keyvals, ((rim, rim), (rim, rim), (0, 0)))
    bias = jnp.take(bias_table, jnp.asarray(bias_indices()), axis=0).transpose(2, 0, 1)
    query_win = query_windows(queries)
    keyval_win = key_windows(padded)
    count = query_win.shape[0]
    group = 8 if count % 8 == 0 else 1
    attended = lax.map(lambda pair: attend_group(pair[0], pair[1], bias), (query_win.reshape(count // group, group, WIN * WIN, chans), keyval_win.reshape(count // group, group, KWIN * KWIN, 2 * chans)))
    attended = undo_windows(attended.reshape(count, WIN * WIN, chans), height, width)
    first = base + jnp.dot(attended, proj_weight, preferred_element_type=jnp.float32)
    second_norm = layer_norm(first, gain_two).astype(jnp.bfloat16)
    inner = jax.nn.gelu(jnp.dot(second_norm, hidden_weight, preferred_element_type=jnp.float32), approximate=False).astype(jnp.bfloat16)
    mixed = (first + jnp.dot(inner, output_weight, preferred_element_type=jnp.float32)).astype(jnp.bfloat16)
    grouped = (base + conv_last(jnp.pad(mixed, ((1, 1), (1, 1), (0, 0))), group_conv)).astype(jnp.bfloat16)
    lowfeat = jax.nn.leaky_relu(conv_to_first(jnp.pad(grouped, ((1, 1), (1, 1), (0, 0))), before_conv), 0.01).astype(jnp.bfloat16)
    expanded = conv_first(jnp.pad(lowfeat, ((0, 0), (1, 1), (1, 1))), upsample_conv)
    return shuffle(expanded).astype(jnp.bfloat16)
```

```python
import functools
import math

import jax
import jax.numpy as jnp
import numpy as np
from jax import lax
from jax.experimental import pallas as pl
from jax.experimental.pallas import tpu as pltpu
from jax.sharding import PartitionSpec as P

HEADS = 6
HEAD = 30
SLOT = 32
CH = 180
WIN = 16
KWIN = 24
SIDE = WIN + KWIN - 1
TABLE = SIDE * SIDE
TH = 16
TW = 64
PITCH = 80
GP = 72
QSCALE = math.log2(math.e) / math.sqrt(HEAD)
LOG2E = math.log2(math.e)
F32 = jnp.float32
BF16 = jnp.bfloat16
MESH = pl.DeviceIdType.MESH
NT = (((1,), (1,)), ((), ()))


def table_selector():
    out = np.zeros((5, 512, 384), np.float32)
    for tile in range(5):
        start = selector_start(tile)
        for lane in range(128):
            rev = 8 * tile + lane // 16
            if rev >= SIDE:
                continue
            for part in range(3):
                entry = 16 * part + lane % 16
                if entry < SIDE:
                    source = SIDE * (SIDE - 1 - rev) + SIDE - 1 - entry
                    out[tile, source - start, 128 * part + lane] = 1.0
    return out


def selector_start(tile):
    first = max(0, SIDE * (SIDE - 8 - 8 * tile))
    return min(first // 128 * 128, 1536 - 512)


def mm(a, b):
    return jnp.dot(a, b, preferred_element_type=F32)


def mm_nt(a, b):
    return lax.dot_general(a, b, NT, preferred_element_type=F32)


def iota(shape, dim):
    return lax.broadcasted_iota(jnp.int32, shape, dim)


def one_hot(mask):
    return jnp.where(mask, 1.0, 0.0).astype(BF16)


def normalize(x, gain):
    center = x - jnp.sum(x, axis=-1, keepdims=True) * (1.0 / CH)
    spread = jnp.sum(center * center, axis=-1, keepdims=True) * (1.0 / CH)
    return center * lax.rsqrt(spread + 1e-05) * gain


def kernel(
    nr, nc,
    feat, gain1, qkv, table, proj, gain2, hid, outw, gconv, bconv, uconv, selector,
    out,
    feat_v, gain1_v, qkv_v, table_v, proj_v, gain2_v, hid_v, outw_v, gconv_v, bconv_v, upad, sel_v,
    halo_t, halo_b, halo_l, halo_r, halo_c,
    mix_t, mix_b, mix_l, mix_r, mix_c, mix_own,
    fpad, npad, mixpad, gbuf, ybuf, lbuf, l3,
    qpad, wqt, wk, wvt, ppad, pw, hpad, opad, wout, gpad, bpad, w2, w3, bias, wrow, kwin, vwin, attt,
    local_sem, fsend, frecv, msend, mrecv,
):
    row = lax.axis_index("rows")
    col = lax.axis_index("cols")
    up = lax.rem(row + nr - 1, nr)
    down = lax.rem(row + 1, nr)
    left = lax.rem(col + nc - 1, nc)
    right = lax.rem(col + 1, nc)
    neighbours = [
        (up, col), (down, col), (row, left), (row, right),
        (up, left), (up, right), (down, left), (down, right),
    ]
    barrier = pltpu.get_barrier_semaphore()
    for target in neighbours:
        pl.semaphore_signal(barrier, inc=1, device_id=target, device_id_type=MESH)

    local = {}
    pairs = [
        ("feat", feat, feat_v), ("gain1", gain1, gain1_v), ("table", table, table_v),
        ("selector", selector, sel_v), ("qkv", qkv, qkv_v), ("proj", proj, proj_v),
        ("gain2", gain2, gain2_v), ("hid", hid, hid_v), ("outw", outw, outw_v),
        ("gconv", gconv, gconv_v), ("bconv", bconv, bconv_v), ("uconv", uconv, upad.at[:, 0:192, :]),
    ]
    for number, (name, source, target) in enumerate(pairs):
        local[name] = pltpu.make_async_copy(source, target, local_sem.at[number])
        local[name].start()

    def exchange(specs, send_sem, recv_sem):
        copies = []
        for number, (source, target, device) in enumerate(specs):
            copies.append(
                pltpu.make_async_remote_copy(
                    src_ref=source, dst_ref=target, send_sem=send_sem.at[number],
                    recv_sem=recv_sem.at[number], device_id=device, device_id_type=MESH,
                )
            )
        return copies

    fcopies = exchange(
        [
            (feat.at[0:4], halo_b, (up, col)),
            (feat.at[12:16], halo_t, (down, col)),
            (feat.at[:, 0:16], halo_r, (row, left)),
            (feat.at[:, 48:64], halo_l, (row, right)),
            (feat.at[0:4, 0:16], halo_c.at[3], (up, left)),
            (feat.at[0:4, 48:64], halo_c.at[2], (up, right)),
            (feat.at[12:16, 0:16], halo_c.at[1], (down, left)),
            (feat.at[12:16, 48:64], halo_c.at[0], (down, right)),
        ],
        fsend, frecv,
    )
    pl.semaphore_wait(barrier, 8)
    for copy in fcopies:
        copy.start()

    has_up = row > 0
    has_down = row < nr - 1
    has_left = col > 0
    has_right = col < nc - 1

    fpad[1] = jnp.zeros(fpad.shape[1:], F32)
    npad[1] = jnp.zeros(npad.shape[1:], F32)
    for ref in (qpad, ppad, hpad, opad, gpad, bpad):
        ref[...] = jnp.zeros(ref.shape, ref.dtype)
    for a in range(3):
        upad[a, 192:256, :] = jnp.zeros((64, 256), BF16)

    local["gain1"].wait()
    local["feat"].wait()
    g1 = gain1_v[...].reshape(1, CH)

    def store_pixels(start, count, values, valid=None):
        x = values.astype(F32)
        if valid is not None:
            x = jnp.where(valid, x, 0.0)
        n = normalize(x, g1)
        rows = pl.ds(start, count)
        fpad[0, rows, :] = x[:, 0:128]
        fpad[1, rows, 0:52] = x[:, 128:CH]
        npad[0, rows, :] = n[:, 0:128]
        npad[1, rows, 0:52] = n[:, 128:CH]

    def own_rows(h, carry):
        store_pixels(pl.multiple_of((h + 4) * PITCH + 8, 8), TW, feat_v[h])
        return carry

    lax.fori_loop(0, TH, own_rows, 0)

    local["qkv"].wait()
    qpad[0:CH, 0 : 3 * CH] = qkv_v[...]
    r = iota((256, 256), 0)
    c = iota((256, 256), 1)
    identity = one_hot(r == c)
    wqt[...] = (mm_nt(one_hot((r == c) & (r < CH)), qpad[:, 0:256]) * QSCALE).astype(F32)
    wk[...] = mm(qpad[:, 128:384], one_hot((r == c + 52) & (c < CH))).astype(BF16)
    rv = iota((192, 384), 0)
    cv = iota((192, 384), 1)
    slot_source = HEAD * lax.shift_right_logical(rv, 5) + (rv & 31)
    wvt[...] = mm_nt(one_hot((cv == slot_source + 104) & ((rv & 31) < HEAD)), qpad[:, 256:640]).astype(BF16)
    local["proj"].wait()
    ppad[0:CH, 0:CH] = proj_v[...]
    slot_source = HEAD * lax.shift_right_logical(r, 5) + (r & 31)
    pw[...] = mm(one_hot((c == slot_source) & ((r & 31) < HEAD) & (r < 192)), ppad[...]).astype(BF16)
    local["gain2"].wait()
    local["hid"].wait()
    hpad[0:CH, 0 : 2 * CH] = hid_v[...]
    local["outw"].wait()
    opad[0:CH, 0 : 2 * CH] = outw_v[...]
    wout[...] = mm_nt(one_hot(iota((384, 384), 0) == iota((384, 384), 1)), opad[...]).astype(BF16)
    local["gconv"].wait()
    for tap in range(9):
        gpad[tap, 0:CH, 0:CH] = gconv_v[tap // 3, tap % 3]
    local["bconv"].wait()
    local["uconv"].wait()
    order = 4 * (r & 63) + 2 * (lax.shift_right_logical(r, 6) & 1) + lax.shift_right_logical(r, 7)
    shuffle_rows = one_hot(c == order)
    for a in range(3):
        for b in range(3):
            bpad[a, 64 * b : 64 * (b + 1), 0:CH] = bconv_v[a, b]
        w2[a] = mm_nt(identity, bpad[a]).astype(BF16)
        w3[a] = mm_nt(shuffle_rows, upad[a]).astype(BF16)

    local["table"].wait()
    local["selector"].wait()
    whole = table_v[...] * LOG2E
    lane8 = iota((8, 128), 1)
    sub8 = iota((8, 128), 0)
    for tile in range(5):
        start = selector_start(tile)
        piece = whole[:, start : min(start + 512, TABLE)]
        sel = sel_v[tile, 0 : piece.shape[1], :]
        hi = piece.astype(BF16)
        rest = piece - hi.astype(F32)
        mid = rest.astype(BF16)
        low = (rest - mid.astype(F32)).astype(BF16)
        z = mm(hi, sel) + mm(mid, sel) + mm(low, sel)
        for group, (part, base) in enumerate(((1, 7), (0, 15), (0, 7))):
            use_first = (lane8 & 15) + base - sub8 < 16
            for head in range(HEADS):
                first = jnp.broadcast_to(z[head : head + 1, 128 * part : 128 * part + 128], (8, 128))
                second = jnp.broadcast_to(z[head : head + 1, 128 * part + 128 : 128 * part + 256], (8, 128))
                first = pltpu.roll(first, 128 - base, 1, stride=1, stride_axis=0)
                second = pltpu.roll(second, 16 - base, 1, stride=1, stride_axis=0)
                wrow[head, 8 * group : 8 * group + 8, 128 * tile : 128 * tile + 128] = jnp.where(
                    use_first, first, second
                )
    lane24 = iota((KWIN, 128), 1)

    def build_bias(head, carry):
        tiles = [wrow[head, :, 128 * k : 128 * k + 128] for k in range(5)]
        for shift in range(8):
            amount = 16 * shift
            if shift:
                rolled = [pltpu.roll(t, 128 - amount, 1) for t in tiles]
                joined = [
                    jnp.where(lane24 < 128 - amount, rolled[k], rolled[k + 1]) for k in range(4)
                ]
            else:
                joined = tiles
            for block in range(3):
                p = KWIN - 1 - 8 * block - shift
                for half in range(2):
                    bias[head, KWIN * p : KWIN * (p + 1), 128 * half : 128 * half + 128] = joined[
                        block + half
                    ]
        return carry

    lax.fori_loop(0, HEADS, build_bias, 0)

    for copy in fcopies:
        copy.wait_recv()

    def halo_rows(h, carry):
        for ref, first, valid, kinds in ((halo_t, 0, has_up, (0, 1)), (halo_b, 20, has_down, (2, 3))):
            start = (first + h) * PITCH
            store_pixels(pl.multiple_of(start + 8, 8), TW, ref[h], valid)
            lo = halo_c[kinds[0], h].astype(F32)[8:16]
            hi = halo_c[kinds[1], h].astype(F32)[0:8]
            store_pixels(pl.multiple_of(start, 8), 8, lo, valid & has_left)
            store_pixels(pl.multiple_of(start + 72, 8), 8, hi, valid & has_right)
        return carry

    lax.fori_loop(0, 4, halo_rows, 0)

    def halo_cols(h, carry):
        start = (4 + h) * PITCH
        store_pixels(pl.multiple_of(start, 8), 8, halo_l[h].astype(F32)[8:16], has_left)
        store_pixels(pl.multiple_of(start + 72, 8), 8, halo_r[h].astype(F32)[0:8], has_right)
        return carry

    lax.fori_loop(0, TH, halo_cols, 0)

    g2 = jnp.concatenate([gain2_v[...].reshape(1, CH), jnp.zeros((1, 256 - CH), F32)], axis=1)
    chan = iota((256, 256), 1)
    inside = chan < CH
    ones_row = (iota((192, KWIN * KWIN), 0) & 31) == HEAD

    def window(w, carry):
        def pixels(ref, half, first_row, count_rows, first_col, count_cols):
            return jnp.concatenate(
                [
                    ref[half, pl.ds((first_row + p) * PITCH + first_col + w * WIN, count_cols), :]
                    for p in range(count_rows)
                ],
                axis=0,
            )

        keys_in = jnp.concatenate(
            [pixels(npad, half, 0, KWIN, 4, KWIN).astype(BF16) for half in range(2)], axis=1
        )
        kwin[...] = mm(keys_in, wk[...]).astype(BF16)
        values = mm_nt(wvt[...], keys_in)
        vwin[...] = jnp.where(ones_row, 1.0, values).astype(BF16)
        query_in = jnp.concatenate(
            [pixels(npad, half, 4, WIN, 8, WIN).astype(BF16) for half in range(2)], axis=1
        )
        queries = mm_nt(wqt[...].astype(BF16), query_in)
        for head in range(HEADS):
            mine = (r >= HEAD * head) & (r < HEAD * (head + 1))
            q = jnp.where(mine, queries, 0.0).astype(BF16)
            scores = mm(kwin[...], q) + bias[head]
            top = jnp.max(scores, axis=0, keepdims=True)
            probs = jnp.exp2(scores - top).astype(BF16)
            mixed_values = mm(vwin[SLOT * head : SLOT * (head + 1), :], probs)
            total = mixed_values[HEAD : HEAD + 1, :]
            attt[SLOT * head : SLOT * (head + 1), :] = (mixed_values / total).astype(BF16)
        attended = mm_nt(identity, attt[...]).astype(BF16)
        base = jnp.concatenate([pixels(fpad, half, 4, WIN, 8, WIN) for half in range(2)], axis=1)
        first = base + mm(attended, pw[0:192, :])
        center = first - jnp.sum(first, axis=-1, keepdims=True) * (1.0 / CH)
        center = jnp.where(inside, center, 0.0)
        spread = jnp.sum(center * center, axis=-1, keepdims=True) * (1.0 / CH)
        second = (center * lax.rsqrt(spread + 1e-05) * g2).astype(BF16)
        inner = mm(second, hpad[...])
        inner = (0.5 * inner * (1.0 + lax.erf(inner * math.sqrt(0.5)))).astype(BF16)
        mixed = first + mm(inner, wout[...])
        for i in range(WIN):
            block = mixed[WIN * i : WIN * (i + 1), :]
            rows = pl.ds(pl.multiple_of((3 + i) * PITCH + 8 + w * WIN, 8), WIN)
            mixpad[0, rows, :] = block[:, 0:128]
            mixpad[1, rows, :] = block[:, 128:256]
            mix_own[i, pl.ds(pl.multiple_of(w * WIN, WIN), WIN), :] = block.astype(BF16)
        return carry

    lax.fori_loop(0, TW // WIN, window, 0)

    mcopies = exchange(
        [
            (mix_own.at[0:3], mix_b, (up, col)),
            (mix_own.at[13:16], mix_t, (down, col)),
            (mix_own.at[:, 0:16], mix_r, (row, left)),
            (mix_own.at[:, 48:64], mix_l, (row, right)),
            (mix_own.at[0:3, 0:16], mix_c.at[3], (up, left)),
            (mix_own.at[0:3, 48:64], mix_c.at[2], (up, right)),
            (mix_own.at[13:16, 0:16], mix_c.at[1], (down, left)),
            (mix_own.at[13:16, 48:64], mix_c.at[0], (down, right)),
        ],
        msend, mrecv,
    )
    for copy in mcopies:
        copy.start()
    for copy in mcopies:
        copy.wait_recv()

    def store_mixed(start, count, values, valid):
        x = jnp.where(valid, values.astype(F32), 0.0)
        rows = pl.ds(start, count)
        mixpad[0, rows, :] = x[:, 0:128]
        mixpad[1, rows, :] = x[:, 128:256]

    for h in range(3):
        for ref, first, valid, kinds in ((mix_t, 0, has_up, (0, 1)), (mix_b, 19, has_down, (2, 3))):
            start = (first + h) * PITCH
            store_mixed(start + 8, TW, ref[h], valid)
            store_mixed(start, 8, mix_c[kinds[0], h].astype(F32)[8:16], valid & has_left)
            store_mixed(start + 72, 8, mix_c[kinds[1], h].astype(F32)[0:8], valid & has_right)
    for h in range(TH):
        start = (3 + h) * PITCH
        store_mixed(start, 8, mix_l[h].astype(F32)[8:16], has_left)
        store_mixed(start + 72, 8, mix_r[h].astype(F32)[0:8], has_right)

    cols72 = iota((GP, 128), 0)
    gcols = ((cols72 >= 2) | has_left) & ((cols72 < 66) | has_right)

    def conv_group(step, carry):
        h0 = step * 4
        acc = None
        for a in range(3):
            for b in range(3):
                halves = []
                for half in range(2):
                    rows = [
                        mixpad[half, pl.ds((h0 + k + a) * PITCH + 5 + b, GP), :] for k in range(4)
                    ]
                    halves.append(jnp.concatenate(rows, axis=0).astype(BF16))
                term = mm(jnp.concatenate(halves, axis=1), gpad[3 * a + b])
                acc = term if acc is None else acc + term
        for k in range(4):
            h = h0 + k
            keep = gcols & ((h >= 2) | has_up) & ((h < 18) | has_down)
            for half in range(2):
                base = fpad[half, pl.ds((h + 2) * PITCH + 6, GP), :]
                value = base + acc[GP * k : GP * (k + 1), 128 * half : 128 * half + 128]
                gbuf[half, pl.ds(pl.multiple_of(h * GP, 8), GP), :] = jnp.where(keep, value, 0.0)
        return carry

    lax.fori_loop(0, 5, conv_group, 0)

    def conv_before(step, carry):
        start = pl.multiple_of(step * (6 * GP), 16)
        acc = None
        for a in range(3):
            rows = pl.ds(pl.multiple_of(start + a * GP, 8), 6 * GP)
            lhs = jnp.concatenate([gbuf[half, rows, :].astype(BF16) for half in range(2)], axis=1)
            term = mm(lhs, w2[a])
            acc = term if acc is None else acc + term
        rows = pl.ds(start, 6 * GP)
        ybuf[0, rows, :] = acc[:, 0:128]
        ybuf[1, rows, :] = acc[:, 128:256]
        return carry

    ybuf[:, 18 * GP :, :] = jnp.zeros((2, 8, 128), F32)
    lbuf[18 * GP :, :] = jnp.zeros((8, 128), F32)
    lax.fori_loop(0, 3, conv_before, 0)
    lcols = ((cols72 >= 1) | has_left) & ((cols72 < 65) | has_right)
    low_lanes = iota((GP, 128), 1) < 64

    def finish_before(h, carry):
        start = h * GP
        value = (
            ybuf[0, pl.ds(pl.multiple_of(start, 8), GP), :]
            + pltpu.roll(ybuf[0, pl.ds(start + 1, GP), :], 64, 1)
            + ybuf[1, pl.ds(start + 2, GP), :]
        )
        value = jnp.where(value >= 0, value, 0.01 * value)
        value = jnp.where(lcols & ((h >= 1) | has_up) & ((h < 17) | has_down), value, 0.0)
        lbuf[pl.ds(pl.multiple_of(start, 8), GP), :] = jnp.where(
            low_lanes, value, pltpu.roll(value, 64, 1)
        )
        return carry

    lax.fori_loop(0, 18, finish_before, 0)
    low64 = iota((TW, 128), 1) < 64

    def gather_taps(h, carry):
        start = h * GP
        zero = lbuf[pl.ds(pl.multiple_of(start, 8), TW), :]
        one = lbuf[pl.ds(start + 1, TW), :]
        two = lbuf[pl.ds(start + 2, TW), :]
        l3[h, :, 0:128] = jnp.where(low64, zero, one).astype(BF16)
        l3[h, :, 128:256] = jnp.where(low64, two, 0.0).astype(BF16)
        return carry

    lax.fori_loop(0, 18, gather_taps, 0)

    target = 128 * (lax.shift_right_logical(r, 6) & 1) + 2 * (r & 63) + lax.shift_right_logical(r, 7)
    weave = one_hot(c == target)

    def conv_up(step, carry):
        acc = None
        for a in range(3):
            rhs = jnp.concatenate([l3[4 * step + a + k] for k in range(4)], axis=0)
            term = mm_nt(w3[a], rhs)
            acc = term if acc is None else acc + term
        acc = acc.astype(BF16)
        for pair in range(2):
            lanes = slice(128 * pair, 128 * pair + 128)
            both = jnp.concatenate([acc[0:128, lanes], acc[128:256, lanes]], axis=1)
            woven = mm(both, weave).astype(BF16)
            for k in range(2):
                for a in range(2):
                    out[2 * (4 * step + 2 * pair + k) + a] = woven[
                        64 * a : 64 * (a + 1), 128 * k : 128 * k + 128
                    ]
        return carry

    lax.fori_loop(0, 4, conv_up, 0)
    for copy in fcopies + mcopies:
        copy.wait_send()


def on_device(
    nr, nc, features, gain_one, qkv_weight, bias_table, proj_weight, gain_two,
    hidden_weight, output_weight, group_conv, before_conv, upsample_conv,
):
    selector = jnp.asarray(table_selector(), BF16)
    operands = (
        features, gain_one, qkv_weight, bias_table.T, proj_weight, gain_two, hidden_weight,
        output_weight.T, group_conv, before_conv.transpose(0, 1, 3, 2),
        upsample_conv.reshape(3, 192, 256), selector,
    )
    any_space = pl.BlockSpec(memory_space=pl.ANY)
    staged = [pltpu.VMEM(x.shape, x.dtype) for x in operands]
    staged[10] = pltpu.VMEM((3, 256, 256), BF16)
    scratch = staged + [
        pltpu.VMEM((4, TW, CH), BF16), pltpu.VMEM((4, TW, CH), BF16),
        pltpu.VMEM((TH, 16, CH), BF16), pltpu.VMEM((TH, 16, CH), BF16),
        pltpu.VMEM((4, 4, 16, CH), BF16),
        pltpu.VMEM((3, TW, 256), BF16), pltpu.VMEM((3, TW, 256), BF16),
        pltpu.VMEM((TH, 16, 256), BF16), pltpu.VMEM((TH, 16, 256), BF16),
        pltpu.VMEM((4, 3, 16, 256), BF16), pltpu.VMEM((TH, TW, 256), BF16),
        pltpu.VMEM((2, 24 * PITCH, 128), F32), pltpu.VMEM((2, 24 * PITCH, 128), F32),
        pltpu.VMEM((2, 22 * PITCH, 128), F32), pltpu.VMEM((2, 20 * GP, 128), F32),
        pltpu.VMEM((2, 18 * GP + 8, 128), F32), pltpu.VMEM((18 * GP + 8, 128), F32),
        pltpu.VMEM((18, TW, 256), BF16),
        pltpu.VMEM((256, 640), BF16), pltpu.VMEM((256, 256), F32), pltpu.VMEM((256, 256), BF16),
        pltpu.VMEM((192, 256), BF16), pltpu.VMEM((256, 256), BF16), pltpu.VMEM((256, 256), BF16),
        pltpu.VMEM((256, 384), BF16), pltpu.VMEM((256, 384), BF16), pltpu.VMEM((384, 256), BF16),
        pltpu.VMEM((9, 256, 256), BF16), pltpu.VMEM((3, 256, 256), BF16),
        pltpu.VMEM((3, 256, 256), BF16), pltpu.VMEM((3, 256, 256), BF16),
        pltpu.VMEM((HEADS, KWIN * KWIN, 256), F32), pltpu.VMEM((HEADS, KWIN, 640), F32),
        pltpu.VMEM((KWIN * KWIN, 256), BF16), pltpu.VMEM((192, KWIN * KWIN), BF16),
        pltpu.VMEM((192, 256), BF16),
        pltpu.SemaphoreType.DMA((12,)), pltpu.SemaphoreType.DMA((8,)), pltpu.SemaphoreType.DMA((8,)),
        pltpu.SemaphoreType.DMA((8,)), pltpu.SemaphoreType.DMA((8,)),
    ]
    result = pl.pallas_call(
        functools.partial(kernel, nr, nc),
        out_shape=jax.ShapeDtypeStruct((2 * TH, 64, 2 * TW), BF16),
        in_specs=[any_space] * len(operands),
        out_specs=pl.BlockSpec(memory_space=pltpu.VMEM),
        scratch_shapes=scratch,
        compiler_params=pltpu.CompilerParams(
            collective_id=0, has_side_effects=True, vmem_limit_bytes=48 * 1024 * 1024
        ),
    )(*operands)
    return result.transpose(1, 0, 2)


def solution(mesh):
    placed = (P("rows", "cols", None),) + (P(),) * 10
    body = functools.partial(on_device, mesh.shape["rows"], mesh.shape["cols"])
    return jax.shard_map(
        body, mesh=mesh, in_specs=placed, out_specs=P(None, "rows", "cols"), check_vma=False
    )
```

```python
import functools
import math

import jax
import jax.numpy as jnp
import numpy as np
from jax import lax
from jax.experimental import pallas as pl
from jax.experimental.pallas import tpu as pltpu
from jax.sharding import PartitionSpec as P

HEADS = 6
HEAD = 30
SLOT = 32
CH = 180
WIN = 16
KWIN = 24
SIDE = WIN + KWIN - 1
TABLE = SIDE * SIDE
TH = 16
TW = 64
PITCH = 80
GP = 72
QSCALE = math.log2(math.e) / math.sqrt(HEAD)
LOG2E = math.log2(math.e)
F32 = jnp.float32
BF16 = jnp.bfloat16
MESH = pl.DeviceIdType.MESH
NT = (((1,), (1,)), ((), ()))


def table_selector():
    out = np.zeros((5, 512, 384), np.float32)
    for tile in range(5):
        start = selector_start(tile)
        for lane in range(128):
            rev = 8 * tile + lane // 16
            if rev >= SIDE:
                continue
            for part in range(3):
                entry = 16 * part + lane % 16
                if entry < SIDE:
                    source = SIDE * (SIDE - 1 - rev) + SIDE - 1 - entry
                    out[tile, source - start, 128 * part + lane] = 1.0
    return out


def selector_start(tile):
    first = max(0, SIDE * (SIDE - 8 - 8 * tile))
    return min(first // 128 * 128, 1536 - 512)


def mm(a, b):
    return jnp.dot(a, b, preferred_element_type=F32)


def mm_nt(a, b):
    return lax.dot_general(a, b, NT, preferred_element_type=F32)


def iota(shape, dim):
    return lax.broadcasted_iota(jnp.int32, shape, dim)


def one_hot(mask):
    return jnp.where(mask, 1.0, 0.0).astype(BF16)


def normalize(x, gain):
    center = x - jnp.sum(x, axis=-1, keepdims=True) * (1.0 / CH)
    spread = jnp.sum(center * center, axis=-1, keepdims=True) * (1.0 / CH)
    return center * lax.rsqrt(spread + 1e-05) * gain


def kernel(
    nr, nc,
    feat, gain1, qkv, table, proj, gain2, hid, outw, gconv, bconv, uconv, selector,
    out,
    feat_v, gain1_v, qkv_v, table_v, proj_v, gain2_v, hid_v, outw_v, gconv_v, bconv_v, upad, sel_v,
    halo_t, halo_b, halo_l, halo_r, halo_c,
    mix_t, mix_b, mix_l, mix_r, mix_c, mix_own,
    fpad, npad, mixpad, gbuf, ybuf, lbuf, l3,
    qpad, wqt, wk, wvt, ppad, pw, hpad, opad, wout, gpad, bpad, w2, w3, bias, wrow, kwin, vwin, qwin, sbuf, pbuf, attt, obuf,
    local_sem, fsend, frecv, msend, mrecv,
):
    row = lax.axis_index("rows")
    col = lax.axis_index("cols")
    up = lax.rem(row + nr - 1, nr)
    down = lax.rem(row + 1, nr)
    left = lax.rem(col + nc - 1, nc)
    right = lax.rem(col + 1, nc)
    neighbours = [
        (up, col), (down, col), (row, left), (row, right),
        (up, left), (up, right), (down, left), (down, right),
    ]
    barrier = pltpu.get_barrier_semaphore()
    for target in neighbours:
        pl.semaphore_signal(barrier, inc=1, device_id=target, device_id_type=MESH)

    local = {}
    pairs = [
        ("feat", feat, feat_v), ("gain1", gain1, gain1_v), ("table", table, table_v),
        ("selector", selector, sel_v), ("qkv", qkv, qkv_v), ("proj", proj, proj_v),
        ("gain2", gain2, gain2_v), ("hid", hid, hid_v), ("outw", outw, outw_v),
        ("gconv", gconv, gconv_v), ("bconv", bconv, bconv_v), ("uconv", uconv, upad.at[:, 0:192, :]),
    ]
    for number, (name, source, target) in enumerate(pairs):
        local[name] = pltpu.make_async_copy(source, target, local_sem.at[number])
        local[name].start()

    def arrive(*names):
        for name in names:
            local[name].wait()

    def exchange(specs, send_sem, recv_sem):
        copies = []
        for number, (source, target, device) in enumerate(specs):
            copies.append(
                pltpu.make_async_remote_copy(
                    src_ref=source, dst_ref=target, send_sem=send_sem.at[number],
                    recv_sem=recv_sem.at[number], device_id=device, device_id_type=MESH,
                )
            )
        return copies

    fcopies = exchange(
        [
            (feat.at[0:4], halo_b, (up, col)),
            (feat.at[12:16], halo_t, (down, col)),
            (feat.at[:, 0:16], halo_r, (row, left)),
            (feat.at[:, 48:64], halo_l, (row, right)),
            (feat.at[0:4, 0:16], halo_c.at[3], (up, left)),
            (feat.at[0:4, 48:64], halo_c.at[2], (up, right)),
            (feat.at[12:16, 0:16], halo_c.at[1], (down, left)),
            (feat.at[12:16, 48:64], halo_c.at[0], (down, right)),
        ],
        fsend, frecv,
    )
    pl.semaphore_wait(barrier, 8)
    for copy in fcopies:
        copy.start()

    has_up = row > 0
    has_down = row < nr - 1
    has_left = col > 0
    has_right = col < nc - 1

    fpad[1] = jnp.zeros(fpad.shape[1:], F32)
    npad[1] = jnp.zeros(npad.shape[1:], F32)
    for ref in (qpad, ppad, hpad, opad, gpad, bpad):
        ref[...] = jnp.zeros(ref.shape, ref.dtype)
    for a in range(3):
        upad[a, 192:256, :] = jnp.zeros((64, 256), BF16)

    arrive("gain1", "feat")
    g1 = gain1_v[...].reshape(1, CH)

    def store_pixels(x, starts):
        n = normalize(x, g1)
        width = x.shape[0] // len(starts)
        for k, start in enumerate(starts):
            part = slice(k * width, (k + 1) * width)
            rows = pl.ds(start, width)
            fpad[0, rows, :] = x[part, 0:128]
            fpad[1, rows, 0:52] = x[part, 128:CH]
            npad[0, rows, :] = n[part, 0:128]
            npad[1, rows, 0:52] = n[part, 128:CH]

    def own_pixels():
        for h in range(0, TH, 4):
            x = feat_v[h : h + 4].astype(F32).reshape(4 * TW, CH)
            store_pixels(x, [(h + k + 4) * PITCH + 8 for k in range(4)])

    own_pixels()
    r = iota((256, 256), 0)
    c = iota((256, 256), 1)
    identity = one_hot(r == c)

    def prepare_weights():
        qpad[0:CH, 0 : 3 * CH] = qkv_v[...]
        wqt[...] = mm_nt(one_hot((r == c) & (r < CH)), qpad[:, 0:256]).astype(BF16)
        wk[...] = mm(qpad[:, 128:384], one_hot((r == c + 52) & (c < CH))).astype(BF16)
        rv = iota((192, 384), 0)
        cv = iota((192, 384), 1)
        slot_source = HEAD * lax.shift_right_logical(rv, 5) + (rv & 31)
        wvt[...] = mm_nt(one_hot((cv == slot_source + 104) & ((rv & 31) < HEAD)), qpad[:, 256:640]).astype(BF16)
        ppad[0:CH, 0:CH] = proj_v[...]
        slot_source = HEAD * lax.shift_right_logical(r, 5) + (r & 31)
        pw[...] = mm(one_hot((c == slot_source) & ((r & 31) < HEAD) & (r < 192)), ppad[...]).astype(BF16)
        hpad[0:CH, 0 : 2 * CH] = hid_v[...]
        opad[0:CH, 0 : 2 * CH] = outw_v[...]
        wout[...] = mm_nt(one_hot(iota((384, 384), 0) == iota((384, 384), 1)), opad[...]).astype(BF16)
        for tap in range(9):
            gpad[tap, 0:CH, 0:CH] = gconv_v[tap // 3, tap % 3]
        order = 4 * (r & 63) + 2 * (lax.shift_right_logical(r, 6) & 1) + lax.shift_right_logical(r, 7)
        shuffle_rows = one_hot(c == order)
        for a in range(3):
            for b in range(3):
                bpad[a, 64 * b : 64 * (b + 1), 0:CH] = bconv_v[a, b]
            w2[a] = mm_nt(identity, bpad[a]).astype(BF16)
            w3[a] = mm_nt(shuffle_rows, upad[a]).astype(BF16)

    arrive("qkv", "proj", "gain2", "hid", "outw", "gconv", "bconv", "uconv")
    prepare_weights()
    def prepare_bias():
        whole = table_v[...] * LOG2E
        lane8 = iota((8, 128), 1)
        sub8 = iota((8, 128), 0)
        for tile in range(5):
            start = selector_start(tile)
            piece = whole[:, start : min(start + 512, TABLE)]
            sel = sel_v[tile, 0 : piece.shape[1], :]
            hi = piece.astype(BF16)
            rest = piece - hi.astype(F32)
            mid = rest.astype(BF16)
            low = (rest - mid.astype(F32)).astype(BF16)
            z = mm(hi, sel) + mm(mid, sel) + mm(low, sel)
            for group, (part, base) in enumerate(((1, 7), (0, 15), (0, 7))):
                use_first = (lane8 & 15) + base - sub8 < 16
                for head in range(HEADS):
                    first = jnp.broadcast_to(z[head : head + 1, 128 * part : 128 * part + 128], (8, 128))
                    second = jnp.broadcast_to(z[head : head + 1, 128 * part + 128 : 128 * part + 256], (8, 128))
                    first = pltpu.roll(first, 128 - base, 1, stride=1, stride_axis=0)
                    second = pltpu.roll(second, 16 - base, 1, stride=1, stride_axis=0)
                    wrow[head, 8 * group : 8 * group + 8, 128 * tile : 128 * tile + 128] = jnp.where(
                        use_first, first, second
                    )
        lane24 = iota((KWIN, 128), 1)

        def build_bias(head, carry):
            tiles = [wrow[head, :, 128 * k : 128 * k + 128] for k in range(5)]
            for shift in range(8):
                amount = 16 * shift
                if shift:
                    rolled = [pltpu.roll(t, 128 - amount, 1) for t in tiles]
                    joined = [
                        jnp.where(lane24 < 128 - amount, rolled[k], rolled[k + 1]) for k in range(4)
                    ]
                else:
                    joined = tiles
                for block in range(3):
                    p = KWIN - 1 - 8 * block - shift
                    for half in range(2):
                        bias[head, KWIN * p : KWIN * (p + 1), 128 * half : 128 * half + 128] = joined[
                            block + half
                        ]
            return carry

        lax.fori_loop(0, HEADS, build_bias, 0)

    arrive("table", "selector")
    prepare_bias()
    def halo_pixels():
        for ref, first, valid, kinds in ((halo_t, 0, has_up, (0, 1)), (halo_b, 20, has_down, (2, 3))):
            x = jnp.where(valid, ref[...].astype(F32).reshape(4 * TW, CH), 0.0)
            store_pixels(x, [(first + h) * PITCH + 8 for h in range(4)])
            lo = halo_c[kinds[0]].astype(F32)[:, 8:16, :].reshape(32, CH)
            hi = halo_c[kinds[1]].astype(F32)[:, 0:8, :].reshape(32, CH)
            store_pixels(
                jnp.where(valid & has_left, lo, 0.0), [(first + h) * PITCH for h in range(4)]
            )
            store_pixels(
                jnp.where(valid & has_right, hi, 0.0), [(first + h) * PITCH + 72 for h in range(4)]
            )
        lo = halo_l[...].astype(F32)[:, 8:16, :].reshape(8 * TH, CH)
        hi = halo_r[...].astype(F32)[:, 0:8, :].reshape(8 * TH, CH)
        store_pixels(jnp.where(has_left, lo, 0.0), [(4 + h) * PITCH for h in range(TH)])
        store_pixels(jnp.where(has_right, hi, 0.0), [(4 + h) * PITCH + 72 for h in range(TH)])

    for copy in fcopies:
        copy.wait_recv()
    halo_pixels()

    g2 = jnp.concatenate([gain2_v[...].reshape(1, CH), jnp.zeros((1, 256 - CH), F32)], axis=1)
    inside = c < CH
    ones_row = (iota((192, KWIN * KWIN), 0) & 31) == HEAD
    tops = {}

    def pixels(ref, half, w, first_row, count_rows, first_col, count_cols):
        return jnp.concatenate(
            [
                ref[half, pl.ds((first_row + p) * PITCH + first_col + w * WIN, count_cols), :]
                for p in range(count_rows)
            ],
            axis=0,
        )

    def project(w):
        keys_in = jnp.concatenate(
            [pixels(npad, half, w, 0, KWIN, 4, KWIN).astype(BF16) for half in range(2)], axis=1
        )
        kwin[w] = mm(keys_in, wk[...]).astype(BF16)
        vwin[w] = jnp.where(ones_row, 1.0, mm_nt(wvt[...], keys_in)).astype(BF16)
        query_in = jnp.concatenate(
            [pixels(npad, half, w, 4, WIN, 8, WIN).astype(BF16) for half in range(2)], axis=1
        )
        qwin[w] = mm_nt(wqt[...], query_in) * QSCALE

    def score(number, w, head):
        mine = (r >= HEAD * head) & (r < HEAD * (head + 1))
        q = jnp.where(mine, qwin[w], 0.0).astype(BF16)
        top = None
        for part in (slice(0, 288), slice(288, 576)):
            scores = mm(kwin[w, part, :], q) + bias[head, part, :]
            sbuf[number % 2, part, :] = scores
            best = jnp.max(scores, axis=0, keepdims=True)
            top = best if top is None else jnp.maximum(top, best)
        tops[number] = top

    def exponent(number):
        pbuf[number % 2] = jnp.exp2(sbuf[number % 2] - tops[number]).astype(BF16)

    def combine(number, w, head):
        rows = slice(SLOT * head, SLOT * (head + 1))
        mixed_values = mm(vwin[w, rows, :], pbuf[number % 2])
        attt[w, rows, :] = (mixed_values / mixed_values[HEAD : HEAD + 1, :]).astype(BF16)

    def feed_forward(w):
        attended = mm_nt(identity, attt[w]).astype(BF16)
        base = jnp.concatenate([pixels(fpad, half, w, 4, WIN, 8, WIN) for half in range(2)], axis=1)
        first = base + mm(attended, pw[0:192, :])
        center = first - jnp.sum(first, axis=-1, keepdims=True) * (1.0 / CH)
        center = jnp.where(inside, center, 0.0)
        spread = jnp.sum(center * center, axis=-1, keepdims=True) * (1.0 / CH)
        second = (center * lax.rsqrt(spread + 1e-05) * g2).astype(BF16)
        inner = mm(second, hpad[...])
        inner = (0.5 * inner * (1.0 + lax.erf(inner * math.sqrt(0.5)))).astype(BF16)
        mixed = first + mm(inner, wout[...])
        for i in range(WIN):
            block = mixed[WIN * i : WIN * (i + 1), :]
            rows = pl.ds((3 + i) * PITCH + 8 + w * WIN, WIN)
            mixpad[0, rows, :] = block[:, 0:128]
            mixpad[1, rows, :] = block[:, 128:256]
            mix_own[i, w * WIN : (w + 1) * WIN, :] = block.astype(BF16)

    mcopies = exchange(
        [
            (mix_own.at[:, 0:16], mix_r, (row, left)),
            (mix_own.at[:, 48:64], mix_l, (row, right)),
            (mix_own.at[0:3, 0:16], mix_c.at[3], (up, left)),
            (mix_own.at[0:3, 48:64], mix_c.at[2], (up, right)),
            (mix_own.at[13:16, 0:16], mix_c.at[1], (down, left)),
            (mix_own.at[13:16, 48:64], mix_c.at[0], (down, right)),
            (mix_own.at[0:3, 0:16], mix_b.at[:, 0:16], (up, col)),
            (mix_own.at[0:3, 48:64], mix_b.at[:, 48:64], (up, col)),
            (mix_own.at[13:16, 0:16], mix_t.at[:, 0:16], (down, col)),
            (mix_own.at[13:16, 48:64], mix_t.at[:, 48:64], (down, col)),
            (mix_own.at[0:3, 16:48], mix_b.at[:, 16:48], (up, col)),
            (mix_own.at[13:16, 16:48], mix_t.at[:, 16:48], (down, col)),
        ],
        msend, mrecv,
    )
    windows = (0, 3, 1, 2)
    steps = [(w, head) for w in windows for head in range(HEADS)]

    def attend(first, last):
        for number in range(first, last + 2):
            if number < last:
                w, head = steps[number]
                if head == 0:
                    project(w)
                score(number, w, head)
            if first <= number - 1 < last:
                exponent(number - 1)
            if first <= number - 2 < last:
                combine(number - 2, *steps[number - 2])
                if number - 2 == first + 5:
                    feed_forward(steps[number - 2][0])
        feed_forward(steps[last - 1][0])

    def edge_windows():
        attend(0, 12)

    def inner_windows():
        attend(12, 24)

    edge_windows()
    for copy in mcopies[0:10]:
        copy.start()
    inner_windows()
    for copy in mcopies[10:12]:
        copy.start()

    def store_mixed(start, count, values, valid):
        x = jnp.where(valid, values, 0.0)
        rows = pl.ds(start, count)
        mixpad[0, rows, :] = x[:, 0:128]
        mixpad[1, rows, :] = x[:, 128:256]

    def side_mixed():
        for h in range(TH):
            start = (3 + h) * PITCH
            store_mixed(start, 8, mix_l[h].astype(F32)[8:16], has_left)
            store_mixed(start + 72, 8, mix_r[h].astype(F32)[0:8], has_right)

    def ends_mixed():
        for h in range(3):
            for ref, first, valid, kinds in ((mix_t, 0, has_up, (0, 1)), (mix_b, 19, has_down, (2, 3))):
                start = (first + h) * PITCH
                store_mixed(start + 8, TW, ref[h].astype(F32), valid)
                store_mixed(start, 8, mix_c[kinds[0], h].astype(F32)[8:16], valid & has_left)
                store_mixed(start + 72, 8, mix_c[kinds[1], h].astype(F32)[0:8], valid & has_right)

    def conv_group(h0, count):
        acc = None
        for a in range(3):
            for b in range(3):
                halves = []
                for half in range(2):
                    rows = [
                        mixpad[half, pl.ds((h0 + k + a) * PITCH + 5 + b, GP), :] for k in range(count)
                    ]
                    halves.append(jnp.concatenate(rows, axis=0).astype(BF16))
                term = mm(jnp.concatenate(halves, axis=1), gpad[3 * a + b])
                acc = term if acc is None else acc + term
        for k in range(count):
            h = h0 + k
            for half in range(2):
                base = fpad[half, pl.ds((h + 2) * PITCH + 6, GP), :]
                value = base + acc[GP * k : GP * (k + 1), 128 * half : 128 * half + 128]
                gbuf[half, pl.ds(h * GP, GP), :] = value

    def group_inner():
        for h0 in range(3, 17, 2):
            conv_group(h0, 2)

    def group_ends():
        for h0 in (0, 17):
            conv_group(h0, 2)
            conv_group(h0 + 2, 1)

    for copy in mcopies[0:2]:
        copy.wait_recv()
    side_mixed()
    group_inner()
    for copy in mcopies[2:12]:
        copy.wait_recv()
    ends_mixed()
    group_ends()

    def clear_rim(ref, lead, count, rim):
        def clear(start, size):
            if lead:
                ref[:, pl.ds(start, size), :] = jnp.zeros((2, size, 128), F32)
            else:
                ref[pl.ds(start, size), :] = jnp.zeros((size, 128), F32)

        @pl.when(jnp.logical_not(has_up))
        def _():
            clear(0, rim * GP)

        @pl.when(jnp.logical_not(has_down))
        def _():
            clear((count - rim) * GP, rim * GP)

        @pl.when(jnp.logical_not(has_left))
        def _():
            for h in range(count):
                clear(h * GP, rim)

        @pl.when(jnp.logical_not(has_right))
        def _():
            for h in range(count):
                clear(h * GP + TW + rim, rim)

    clear_rim(gbuf, True, 20, 2)

    low_lanes = iota((6 * GP, 128), 1) < 64
    low64 = iota((TW, 128), 1) < 64

    def before():
        ybuf[:, 18 * GP :, :] = jnp.zeros((2, 8, 128), F32)
        lbuf[18 * GP :, :] = jnp.zeros((8, 128), F32)
        for step in range(3):
            start = step * (6 * GP)
            acc = None
            for a in range(3):
                rows = pl.ds(start + a * GP, 6 * GP)
                lhs = jnp.concatenate([gbuf[half, rows, :].astype(BF16) for half in range(2)], axis=1)
                term = mm(lhs, w2[a])
                acc = term if acc is None else acc + term
            rows = pl.ds(start, 6 * GP)
            ybuf[0, rows, :] = acc[:, 0:128]
            ybuf[1, rows, :] = acc[:, 128:256]
        for step in range(3):
            start = step * (6 * GP)
            value = (
                ybuf[0, pl.ds(start, 6 * GP), :]
                + pltpu.roll(ybuf[0, pl.ds(start + 1, 6 * GP), :], 64, 1)
                + ybuf[1, pl.ds(start + 2, 6 * GP), :]
            )
            value = jnp.where(value >= 0, value, 0.01 * value)
            lbuf[pl.ds(start, 6 * GP), :] = jnp.where(low_lanes, value, pltpu.roll(value, 64, 1))

    before()
    clear_rim(lbuf, False, 18, 1)

    def gather_taps():
        for h in range(18):
            start = h * GP
            zero = lbuf[pl.ds(start, TW), :]
            one = lbuf[pl.ds(start + 1, TW), :]
            two = lbuf[pl.ds(start + 2, TW), :]
            l3[h, :, 0:128] = jnp.where(low64, zero, one).astype(BF16)
            l3[h, :, 128:256] = jnp.where(low64, two, 0.0).astype(BF16)

    gather_taps()

    target = 128 * (lax.shift_right_logical(r, 6) & 1) + 2 * (r & 63) + lax.shift_right_logical(r, 7)
    weave = one_hot(c == target)

    def conv_up():
        for step in range(4):
            acc = None
            for a in range(3):
                rhs = jnp.concatenate([l3[4 * step + a + k] for k in range(4)], axis=0)
                term = mm_nt(w3[a], rhs)
                acc = term if acc is None else acc + term
            acc = acc.astype(BF16)
            for pair in range(2):
                lanes = slice(128 * pair, 128 * pair + 128)
                both = jnp.concatenate([acc[0:128, lanes], acc[128:256, lanes]], axis=1)
                woven = mm(both, weave)
                for k in range(2):
                    for a in range(2):
                        line = (2 * (4 * step + 2 * pair + k) + a) % 16
                        obuf[step // 2, pl.ds(line, 64, stride=16), :] = woven[
                            64 * a : 64 * (a + 1), 128 * k : 128 * k + 128
                        ]
            if step % 2:
                half = step // 2
                out[:, 16 * half : 16 * half + 16, :] = (
                    obuf[half].reshape(64, 16, 128).astype(BF16)
                )

    conv_up()
    for copy in fcopies + mcopies:
        copy.wait_send()


def on_device(
    nr, nc, features, gain_one, qkv_weight, bias_table, proj_weight, gain_two,
    hidden_weight, output_weight, group_conv, before_conv, upsample_conv,
):
    selector = jnp.asarray(table_selector(), BF16)
    operands = (
        features, gain_one, qkv_weight, bias_table.T, proj_weight, gain_two, hidden_weight,
        output_weight.T, group_conv, before_conv.transpose(0, 1, 3, 2),
        upsample_conv.reshape(3, 192, 256), selector,
    )
    any_space = pl.BlockSpec(memory_space=pltpu.HBM)
    staged = [pltpu.VMEM(x.shape, x.dtype) for x in operands]
    staged[10] = pltpu.VMEM((3, 256, 256), BF16)
    scratch = staged + [
        pltpu.VMEM((4, TW, CH), BF16), pltpu.VMEM((4, TW, CH), BF16),
        pltpu.VMEM((TH, 16, CH), BF16), pltpu.VMEM((TH, 16, CH), BF16),
        pltpu.VMEM((4, 4, 16, CH), BF16),
        pltpu.VMEM((3, TW, 256), BF16), pltpu.VMEM((3, TW, 256), BF16),
        pltpu.VMEM((TH, 16, 256), BF16), pltpu.VMEM((TH, 16, 256), BF16),
        pltpu.VMEM((4, 3, 16, 256), BF16), pltpu.VMEM((TH, TW, 256), BF16),
        pltpu.VMEM((2, 24 * PITCH, 128), F32), pltpu.VMEM((2, 24 * PITCH, 128), F32),
        pltpu.VMEM((2, 22 * PITCH, 128), F32), pltpu.VMEM((2, 20 * GP, 128), F32),
        pltpu.VMEM((2, 18 * GP + 8, 128), F32), pltpu.VMEM((18 * GP + 8, 128), F32),
        pltpu.VMEM((18, TW, 256), BF16),
        pltpu.VMEM((256, 640), BF16), pltpu.VMEM((256, 256), BF16), pltpu.VMEM((256, 256), BF16),
        pltpu.VMEM((192, 256), BF16), pltpu.VMEM((256, 256), BF16), pltpu.VMEM((256, 256), BF16),
        pltpu.VMEM((256, 384), BF16), pltpu.VMEM((256, 384), BF16), pltpu.VMEM((384, 256), BF16),
        pltpu.VMEM((9, 256, 256), BF16), pltpu.VMEM((3, 256, 256), BF16),
        pltpu.VMEM((3, 256, 256), BF16), pltpu.VMEM((3, 256, 256), BF16),
        pltpu.VMEM((HEADS, KWIN * KWIN, 256), F32), pltpu.VMEM((HEADS, KWIN, 640), F32),
        pltpu.VMEM((4, KWIN * KWIN, 256), BF16), pltpu.VMEM((4, 192, KWIN * KWIN), BF16),
        pltpu.VMEM((4, 256, 256), F32), pltpu.VMEM((2, KWIN * KWIN, 256), F32),
        pltpu.VMEM((2, KWIN * KWIN, 256), BF16), pltpu.VMEM((4, 192, 256), BF16),
        pltpu.VMEM((2, 64 * 16, 128), F32),
        pltpu.SemaphoreType.DMA((12,)), pltpu.SemaphoreType.DMA((8,)), pltpu.SemaphoreType.DMA((8,)),
        pltpu.SemaphoreType.DMA((12,)), pltpu.SemaphoreType.DMA((12,)),
    ]
    result = pl.pallas_call(
        functools.partial(kernel, nr, nc),
        out_shape=jax.ShapeDtypeStruct((64, 2 * TH, 2 * TW), BF16),
        in_specs=[any_space] * len(operands),
        out_specs=pl.BlockSpec(memory_space=pltpu.VMEM),
        scratch_shapes=scratch,
        compiler_params=pltpu.CompilerParams(
            collective_id=0, has_side_effects=True, vmem_limit_bytes=62 * 1024 * 1024
        ),
    )(*operands)
    return result


def solution(mesh):
    placed = (P("rows", "cols", None),) + (P(),) * 10
    body = functools.partial(on_device, mesh.shape["rows"], mesh.shape["cols"])
    return jax.shard_map(
        body, mesh=mesh, in_specs=placed, out_specs=P(None, "rows", "cols"), check_vma=False
    )
```

```python
import functools
import math

import jax
import jax.numpy as jnp
import numpy as np
from jax import lax
from jax.experimental import pallas as pl
from jax.experimental.pallas import tpu as pltpu
from jax.sharding import PartitionSpec as P

HEADS = 6
HEAD = 30
SLOT = 32
CH = 180
WIN = 16
KWIN = 24
SIDE = WIN + KWIN - 1
TABLE = SIDE * SIDE
TH = 16
TW = 64
PITCH = 80
GP = 72
QSCALE = math.log2(math.e) / math.sqrt(HEAD)
LOG2E = math.log2(math.e)
F32 = jnp.float32
BF16 = jnp.bfloat16
MESH = pl.DeviceIdType.MESH
NT = (((1,), (1,)), ((), ()))


def table_selector():
    out = np.zeros((384, 384), np.float32)
    for lane in range(128):
        for part in range(3):
            entry = 16 * part + lane % 16
            if entry < SIDE:
                out[SIDE * (7 - lane // 16) + SIDE - 1 - entry, 128 * part + lane] = 1.0
    return out


def mm(a, b):
    return jnp.dot(a, b, preferred_element_type=F32)


def mm_nt(a, b):
    return lax.dot_general(a, b, NT, preferred_element_type=F32)


def iota(shape, dim):
    return lax.broadcasted_iota(jnp.int32, shape, dim)


def one_hot(mask):
    return jnp.where(mask, 1.0, 0.0).astype(BF16)


def normalize(x, gain):
    lane = iota(x[1].shape, 1)
    mean = jnp.sum(x[0] + x[1], axis=-1, keepdims=True) * (1.0 / CH)
    low = x[0] - mean
    high = jnp.where(lane < CH - 128, x[1] - mean, 0.0)
    spread = jnp.sum(low * low + high * high, axis=-1, keepdims=True) * (1.0 / CH)
    scale = lax.rsqrt(spread + 1e-05)
    return low * scale * gain[:, 0:128], high * scale * gain[:, 128:256]


def pack_pixels(low, high):
    half = low.shape[0] // 2
    lane = iota((half, 128), 1)
    joined = jnp.where(lane < 64, high[:half], pltpu.roll(high[half:], 64, 1))
    return jnp.concatenate([low, joined], axis=0).astype(BF16)


def unpack_pixels(packed, valid):
    count = packed.shape[0] * 2 // 3
    x = jnp.where(valid, packed.astype(F32), 0.0)
    joined = x[count:]
    high = jnp.concatenate([joined, pltpu.roll(joined, 64, 1)], axis=0)
    return x[:count], jnp.where(iota(high.shape, 1) < CH - 128, high, 0.0)


def kernel(
    nr, nc,
    feat, gain1, qkv, table, proj, gain2, hid, outw, gconv, bconv, uconv, selector,
    out,
    feat_v, gain1_v, qkv_v, table_v, proj_v, gain2_v, hid_v, outw_v, gconv_v, bconv_v, upad, sel_v,
    send_t, send_b, send_l, send_r, send_c, halo_t, halo_b, halo_l, halo_r, halo_c,
    mix_t, mix_b, mix_l, mix_r, mix_c, mix_own,
    fpad, npad, mixpad, gbuf, ybuf, lbuf, l3,
    qpad, wqt, wk, wvt, ppad, pw, hpad, opad, wout, gpad, bpad, w2, w3, bias, xwin, kwin, vwin, qwin, sbuf, pbuf, attt, fbuf, second, inner, obuf,
    local_sem, fsend, frecv, msend, mrecv,
):
    row = lax.axis_index("rows")
    col = lax.axis_index("cols")
    up = lax.rem(row + nr - 1, nr)
    down = lax.rem(row + 1, nr)
    left = lax.rem(col + nc - 1, nc)
    right = lax.rem(col + 1, nc)
    neighbours = [
        (up, col), (down, col), (row, left), (row, right),
        (up, left), (up, right), (down, left), (down, right),
    ]
    barrier = pltpu.get_barrier_semaphore()
    for target in neighbours:
        pl.semaphore_signal(barrier, inc=1, device_id=target, device_id_type=MESH)

    local = {}
    pairs = [
        ("feat", feat, feat_v), ("gain1", gain1, gain1_v), ("table", table, table_v),
        ("selector", selector, sel_v), ("qkv", qkv, qkv_v), ("proj", proj, proj_v),
        ("gain2", gain2, gain2_v), ("hid", hid, hid_v), ("outw", outw, outw_v),
        ("gconv", gconv, gconv_v), ("bconv", bconv, bconv_v), ("uconv", uconv, upad.at[:, 0:192, :]),
    ]
    for number, (name, source, target) in enumerate(pairs):
        local[name] = pltpu.make_async_copy(source, target, local_sem.at[number])
    for name in ("feat", "gain1", "table", "selector"):
        local[name].start()

    def arrive(*names):
        for name in names:
            local[name].wait()

    def exchange(specs, send_sem, recv_sem):
        copies = []
        for number, (source, target, device) in enumerate(specs):
            copies.append(
                pltpu.make_async_remote_copy(
                    src_ref=source, dst_ref=target, send_sem=send_sem.at[number],
                    recv_sem=recv_sem.at[number], device_id=device, device_id_type=MESH,
                )
            )
        return copies

    fcopies = exchange(
        [
            (send_t, halo_b, (up, col)),
            (send_b, halo_t, (down, col)),
            (send_l, halo_r, (row, left)),
            (send_r, halo_l, (row, right)),
            (send_c.at[0], halo_c.at[3], (up, left)),
            (send_c.at[1], halo_c.at[2], (up, right)),
            (send_c.at[2], halo_c.at[1], (down, left)),
            (send_c.at[3], halo_c.at[0], (down, right)),
        ],
        fsend, frecv,
    )

    has_up = row > 0
    has_down = row < nr - 1
    has_left = col > 0
    has_right = col < nc - 1

    fpad[1] = jnp.zeros(fpad.shape[1:], F32)
    arrive("feat", "gain1")
    for h in range(0, TH, 4):
        x = feat_v[h : h + 4].astype(F32).reshape(4 * TW, CH)
        for k in range(4):
            rows = pl.ds((h + k + 4) * PITCH + 8, TW)
            fpad[0, rows, :] = x[k * TW : (k + 1) * TW, 0:128]
            fpad[1, rows, 0 : CH - 128] = x[k * TW : (k + 1) * TW, 128:CH]

    def region(ref, first_row, count_rows, first_col, count_cols):
        return [
            jnp.concatenate(
                [
                    ref[half, pl.ds((first_row + k) * PITCH + first_col, count_cols), :]
                    for k in range(count_rows)
                ],
                axis=0,
            )
            for half in range(2)
        ]

    send_t[...] = pack_pixels(*region(fpad, 4, 4, 8, TW))
    send_b[...] = pack_pixels(*region(fpad, 16, 4, 8, TW))
    send_l[...] = pack_pixels(*region(fpad, 4, TH, 8, 8))
    send_r[...] = pack_pixels(*region(fpad, 4, TH, 64, 8))
    for corner, (first_row, first_col) in enumerate(((4, 8), (4, 64), (16, 8), (16, 64))):
        send_c[corner] = pack_pixels(*region(fpad, first_row, 4, first_col, 8))
    pl.semaphore_wait(barrier, 8)
    for copy in fcopies:
        copy.start()
    for name in ("qkv", "proj", "gain2", "hid", "outw", "gconv", "bconv", "uconv"):
        local[name].start()

    def lanes256(ref):
        return jnp.concatenate([ref[...].reshape(1, CH), jnp.zeros((1, 256 - CH), F32)], axis=1)

    g1 = lanes256(gain1_v)

    def store_normed(x, starts):
        n = normalize(x, g1)
        width = x[0].shape[0] // len(starts)
        for k, start in enumerate(starts):
            for half in range(2):
                npad[half, pl.ds(start, width), :] = n[half][k * width : (k + 1) * width]

    def own_pixels():
        for h in range(0, TH, 4):
            store_normed(
                region(fpad, h + 4, 4, 8, TW), [(h + k + 4) * PITCH + 8 for k in range(4)]
            )

    own_pixels()
    for ref in (qpad, ppad, hpad, opad, gpad, bpad):
        ref[...] = jnp.zeros(ref.shape, ref.dtype)
    for a in range(3):
        upad[a, 192:256, :] = jnp.zeros((64, 256), BF16)

    r = iota((256, 256), 0)
    c = iota((256, 256), 1)
    identity = one_hot(r == c)

    def prepare_bias():
        whole = jnp.concatenate(
            [table_v[...] * LOG2E, jnp.zeros((HEADS, 1536 - TABLE), F32)], axis=1
        )
        whole = jnp.concatenate([whole, jnp.zeros((2, 1536), F32)], axis=0)
        lane8 = iota((8, 128), 1)
        sub8 = iota((8, 128), 0)
        pieces = []
        for tile in range(5):
            first = SIDE * (SIDE - 8 - 8 * tile)
            pieces.append(pltpu.roll(whole, (1536 - first) % 1536, 1)[:, 0:384])
        rows = jnp.concatenate(pieces, axis=0)
        hi = rows.astype(BF16)
        rest = rows - hi.astype(F32)
        mid = rest.astype(BF16)
        low = (rest - mid.astype(F32)).astype(BF16)
        picked = mm(hi, sel_v[...]) + mm(mid, sel_v[...]) + mm(low, sel_v[...])
        lane24 = iota((KWIN, 128), 1)
        for head in range(HEADS):
            tiles = []
            for tile in range(5):
                z = picked[8 * tile + head : 8 * tile + head + 1, :]
                blocks = []
                for part, base in ((1, 7), (0, 15), (0, 7)):
                    first = jnp.broadcast_to(z[:, 128 * part : 128 * part + 128], (8, 128))
                    second = jnp.broadcast_to(z[:, 128 * part + 128 : 128 * part + 256], (8, 128))
                    first = pltpu.roll(first, 128 - base, 1, stride=1, stride_axis=0)
                    second = pltpu.roll(second, 16 - base, 1, stride=1, stride_axis=0)
                    blocks.append(jnp.where((lane8 & 15) + base - sub8 < 16, first, second))
                tiles.append(jnp.concatenate(blocks, axis=0))
            for shift in range(8):
                amount = 16 * shift
                if shift:
                    rolled = [pltpu.roll(t, 128 - amount, 1) for t in tiles]
                    joined = [
                        jnp.where(lane24 < 128 - amount, rolled[k], rolled[k + 1]) for k in range(4)
                    ]
                else:
                    joined = tiles
                for block in range(3):
                    p = KWIN - 1 - 8 * block - shift
                    for half in range(2):
                        bias[head, KWIN * p : KWIN * (p + 1), 128 * half : 128 * half + 128] = (
                            joined[block + half]
                        )

    arrive("table", "selector")
    prepare_bias()

    def prepare_weights():
        qpad[0:CH, 0 : 3 * CH] = qkv_v[...]
        wqt[...] = mm_nt(one_hot((r == c) & (r < CH)), qpad[:, 0:256]).astype(BF16)
        wk[...] = mm(qpad[:, 128:384], one_hot((r == c + 52) & (c < CH))).astype(BF16)
        rv = iota((192, 384), 0)
        cv = iota((192, 384), 1)
        slot_source = HEAD * lax.shift_right_logical(rv, 5) + (rv & 31)
        wvt[...] = mm_nt(one_hot((cv == slot_source + 104) & ((rv & 31) < HEAD)), qpad[:, 256:640]).astype(BF16)
        ppad[0:CH, 0:CH] = proj_v[...]
        slot_source = HEAD * lax.shift_right_logical(r, 5) + (r & 31)
        pw[...] = mm(one_hot((c == slot_source) & ((r & 31) < HEAD) & (r < 192)), ppad[...]).astype(BF16)
        hpad[0:CH, 0 : 2 * CH] = hid_v[...]
        opad[0:CH, 0 : 2 * CH] = outw_v[...]
        wout[...] = mm_nt(one_hot(iota((384, 384), 0) == iota((384, 384), 1)), opad[...]).astype(BF16)
        for tap in range(9):
            gpad[tap, 0:CH, 0:CH] = gconv_v[tap // 3, tap % 3]
        order = 4 * (r & 63) + 2 * (lax.shift_right_logical(r, 6) & 1) + lax.shift_right_logical(r, 7)
        shuffle_rows = one_hot(c == order)
        for a in range(3):
            for b in range(3):
                bpad[a, 64 * b : 64 * (b + 1), 0:CH] = bconv_v[a, b]
            w2[a] = mm_nt(identity, bpad[a]).astype(BF16)
            w3[a] = mm_nt(shuffle_rows, upad[a]).astype(BF16)

    arrive("qkv", "proj", "gain2", "hid", "outw", "gconv", "bconv", "uconv")
    prepare_weights()
    def halo_pixels():
        groups = [
            (halo_t[...], has_up, [h * PITCH + 8 for h in range(4)]),
            (halo_b[...], has_down, [(20 + h) * PITCH + 8 for h in range(4)]),
            (halo_l[...], has_left, [(4 + h) * PITCH for h in range(TH)]),
            (halo_r[...], has_right, [(4 + h) * PITCH + 72 for h in range(TH)]),
            (halo_c[0], has_up & has_left, [h * PITCH for h in range(4)]),
            (halo_c[1], has_up & has_right, [h * PITCH + 72 for h in range(4)]),
            (halo_c[2], has_down & has_left, [(20 + h) * PITCH for h in range(4)]),
            (halo_c[3], has_down & has_right, [(20 + h) * PITCH + 72 for h in range(4)]),
        ]
        for packed, valid, starts in groups:
            x = unpack_pixels(packed, valid)
            width = x[0].shape[0] // len(starts)
            for k, start in enumerate(starts):
                for half in range(2):
                    fpad[half, pl.ds(start, width), :] = x[half][k * width : (k + 1) * width]
            store_normed(x, starts)

    for copy in fcopies:
        copy.wait_recv()
    halo_pixels()

    g2 = lanes256(gain2_v)
    inside = c < CH
    ones_row = (iota((192, KWIN * KWIN), 0) & 31) == HEAD
    tops = {}

    def pixels(ref, half, w, first_row, count_rows, first_col, count_cols):
        return jnp.concatenate(
            [
                ref[half, pl.ds((first_row + p) * PITCH + first_col + w * WIN, count_cols), :]
                for p in range(count_rows)
            ],
            axis=0,
        )

    def project_keys(w):
        keys_in = jnp.concatenate(
            [pixels(npad, half, w, 0, KWIN, 4, KWIN).astype(BF16) for half in range(2)], axis=1
        )
        xwin[...] = keys_in
        kwin[w] = mm(keys_in, wk[...]).astype(BF16)

    def project_values(w):
        vwin[w] = jnp.where(ones_row, 1.0, mm_nt(wvt[...], xwin[...])).astype(BF16)

    def project_queries(w):
        query_in = jnp.concatenate(
            [pixels(npad, half, w, 4, WIN, 8, WIN).astype(BF16) for half in range(2)], axis=1
        )
        qwin[w] = mm_nt(wqt[...], query_in) * QSCALE

    def score(number, w, head):
        mine = (r >= HEAD * head) & (r < HEAD * (head + 1))
        q = jnp.where(mine, qwin[w], 0.0).astype(BF16)
        top = None
        for part in (slice(0, 288), slice(288, 576)):
            scores = mm(kwin[w, part, :], q) + bias[head, part, :]
            sbuf[number % 2, part, :] = scores
            best = jnp.max(scores, axis=0, keepdims=True)
            top = best if top is None else jnp.maximum(top, best)
        tops[number] = top

    def exponent(number):
        pbuf[number % 2] = jnp.exp2(sbuf[number % 2] - tops[number]).astype(BF16)

    def combine(number, w, head):
        rows = slice(SLOT * head, SLOT * (head + 1))
        mixed_values = mm(vwin[w, rows, :], pbuf[number % 2])
        attt[w, rows, :] = (mixed_values / mixed_values[HEAD : HEAD + 1, :]).astype(BF16)

    def merge_heads(w):
        attended = mm_nt(identity, attt[w]).astype(BF16)
        base = jnp.concatenate([pixels(fpad, half, w, 4, WIN, 8, WIN) for half in range(2)], axis=1)
        first = base + mm(attended, pw[0:192, :])
        fbuf[...] = first
        center = first - jnp.sum(first, axis=-1, keepdims=True) * (1.0 / CH)
        center = jnp.where(inside, center, 0.0)
        spread = jnp.sum(center * center, axis=-1, keepdims=True) * (1.0 / CH)
        second[...] = (center * lax.rsqrt(spread + 1e-05) * g2).astype(BF16)

    def hidden(part):
        lanes = slice(128 * part, 128 * part + 128)
        value = mm(second[...], hpad[:, lanes])
        inner[:, lanes] = (0.5 * value * (1.0 + lax.erf(value * math.sqrt(0.5)))).astype(BF16)

    def finish_window(w):
        mixed = fbuf[...] + mm(inner[...], wout[...])
        for i in range(WIN):
            block = mixed[WIN * i : WIN * (i + 1), :]
            rows = pl.ds((3 + i) * PITCH + 8 + w * WIN, WIN)
            mixpad[0, rows, :] = block[:, 0:128]
            mixpad[1, rows, :] = block[:, 128:256]
            mix_own[i, w * WIN : (w + 1) * WIN, :] = block.astype(BF16)
        for copy in mcopies[w]:
            copy.start()

    def strip(w):
        cols = slice(w * WIN, (w + 1) * WIN)
        return [
            (mix_own.at[0:3, cols], mix_b.at[:, cols], (up, col)),
            (mix_own.at[13:16, cols], mix_t.at[:, cols], (down, col)),
        ]

    specs = {
        0: [
            (mix_own.at[:, 0:16], mix_r, (row, left)),
            (mix_own.at[0:3, 0:16], mix_c.at[3], (up, left)),
            (mix_own.at[13:16, 0:16], mix_c.at[1], (down, left)),
        ] + strip(0),
        3: [
            (mix_own.at[:, 48:64], mix_l, (row, right)),
            (mix_own.at[0:3, 48:64], mix_c.at[2], (up, right)),
            (mix_own.at[13:16, 48:64], mix_c.at[0], (down, right)),
        ] + strip(3),
        1: strip(1),
        2: strip(2),
    }
    windows = (0, 3, 1, 2)
    every = exchange([item for w in windows for item in specs[w]], msend, mrecv)
    mcopies = {0: every[0:5], 3: every[5:10], 1: every[10:12], 2: every[12:14]}
    steps = [(w, head) for w in windows for head in range(HEADS)]

    def attend():
        project_keys(0)
        project_values(0)
        project_queries(0)
        for number in range(len(steps) + 2):
            place, head = divmod(number, HEADS)
            if number < len(steps):
                score(number, windows[place], head)
            if 0 <= number - 1 < len(steps):
                exponent(number - 1)
            if 0 <= number - 2:
                combine(number - 2, *steps[number - 2])
            if place + 1 < len(windows) and head < 3:
                (project_keys, project_values, project_queries)[head](windows[place + 1])
            if 0 < place < len(windows):
                if head == 1:
                    merge_heads(windows[place - 1])
                elif 2 <= head <= 4:
                    hidden(head - 2)
                elif head == 5:
                    finish_window(windows[place - 1])
        merge_heads(windows[-1])
        for part in range(3):
            hidden(part)
        finish_window(windows[-1])

    attend()

    def store_mixed(start, count, values, valid):
        x = jnp.where(valid, values, 0.0)
        rows = pl.ds(start, count)
        mixpad[0, rows, :] = x[:, 0:128]
        mixpad[1, rows, :] = x[:, 128:256]

    def side_mixed():
        for h in range(TH):
            start = (3 + h) * PITCH
            store_mixed(start, 8, mix_l[h].astype(F32)[8:16], has_left)
            store_mixed(start + 72, 8, mix_r[h].astype(F32)[0:8], has_right)

    def ends_mixed():
        for h in range(3):
            for ref, first, valid, kinds in ((mix_t, 0, has_up, (0, 1)), (mix_b, 19, has_down, (2, 3))):
                start = (first + h) * PITCH
                store_mixed(start + 8, TW, ref[h].astype(F32), valid)
                store_mixed(start, 8, mix_c[kinds[0], h].astype(F32)[8:16], valid & has_left)
                store_mixed(start + 72, 8, mix_c[kinds[1], h].astype(F32)[0:8], valid & has_right)

    cols72 = iota((GP, 128), 0)
    gcols = ((cols72 >= 2) | has_left) & ((cols72 < 66) | has_right)
    lcols = ((cols72 >= 1) | has_left) & ((cols72 < 65) | has_right)

    def conv_group(h0, count):
        acc = None
        for a in range(3):
            for b in range(3):
                halves = []
                for half in range(2):
                    rows = [
                        mixpad[half, pl.ds((h0 + k + a) * PITCH + 5 + b, GP), :] for k in range(count)
                    ]
                    halves.append(jnp.concatenate(rows, axis=0).astype(BF16))
                term = mm(jnp.concatenate(halves, axis=1), gpad[3 * a + b])
                acc = term if acc is None else acc + term
        for k in range(count):
            h = h0 + k
            keep = gcols & has_up if h < 2 else gcols & has_down if h >= 18 else gcols
            for half in range(2):
                base = fpad[half, pl.ds((h + 2) * PITCH + 6, GP), :]
                value = base + acc[GP * k : GP * (k + 1), 128 * half : 128 * half + 128]
                gbuf[half, pl.ds(h * GP, GP), :] = jnp.where(keep, value, 0.0)

    low_lanes = iota((GP, 128), 1) < 64
    low64 = iota((TW, 128), 1) < 64

    def conv_before(first, count):
        start = first * GP
        acc = None
        for a in range(3):
            rows = pl.ds(start + a * GP, count * GP)
            lhs = jnp.concatenate([gbuf[half, rows, :].astype(BF16) for half in range(2)], axis=1)
            term = mm(lhs, w2[a])
            acc = term if acc is None else acc + term
        rows = pl.ds(start, count * GP)
        ybuf[0, rows, :] = acc[:, 0:128]
        ybuf[1, rows, :] = acc[:, 128:256]
        for h in range(first, first + count):
            start = h * GP
            value = (
                ybuf[0, pl.ds(start, GP), :]
                + pltpu.roll(ybuf[0, pl.ds(start + 1, GP), :], 64, 1)
                + ybuf[1, pl.ds(start + 2, GP), :]
            )
            value = jnp.where(value >= 0, value, 0.01 * value)
            keep = lcols & has_up if h < 1 else lcols & has_down if h >= 17 else lcols
            value = jnp.where(keep, value, 0.0)
            lbuf[pl.ds(start, GP), :] = jnp.where(low_lanes, value, pltpu.roll(value, 64, 1))
        for h in range(first, first + count):
            start = h * GP
            zero = lbuf[pl.ds(start, TW), :]
            one = lbuf[pl.ds(start + 1, TW), :]
            two = lbuf[pl.ds(start + 2, TW), :]
            l3[h, :, 0:128] = jnp.where(low64, zero, one).astype(BF16)
            l3[h, :, 128:256] = jnp.where(low64, two, 0.0).astype(BF16)

    target = 128 * (lax.shift_right_logical(r, 6) & 1) + 2 * (r & 63) + lax.shift_right_logical(r, 7)
    weave = one_hot(c == target)

    def conv_up(step):
        acc = None
        for a in range(3):
            rhs = jnp.concatenate([l3[4 * step + a + k] for k in range(4)], axis=0)
            term = mm_nt(w3[a], rhs)
            acc = term if acc is None else acc + term
        acc = acc.astype(BF16)
        for pair in range(2):
            lanes = slice(128 * pair, 128 * pair + 128)
            both = jnp.concatenate([acc[0:128, lanes], acc[128:256, lanes]], axis=1)
            woven = mm(both, weave)
            for k in range(2):
                for a in range(2):
                    line = (2 * (4 * step + 2 * pair + k) + a) % 16
                    obuf[step // 2, pl.ds(line, 64, stride=16), :] = woven[
                        64 * a : 64 * (a + 1), 128 * k : 128 * k + 128
                    ]

    def inner_rows():
        for h0 in range(3, 17, 2):
            conv_group(h0, 2)
        conv_before(3, 6)
        conv_before(9, 6)
        conv_up(1)
        conv_up(2)

    def end_rows():
        for h0 in (0, 17):
            conv_group(h0, 2)
            conv_group(h0 + 2, 1)
        conv_before(0, 3)
        conv_before(15, 3)
        conv_up(0)
        conv_up(3)
        for half in range(2):
            out[:, 16 * half : 16 * half + 16, :] = obuf[half].reshape(64, 16, 128).astype(BF16)

    ybuf[:, 18 * GP :, :] = jnp.zeros((2, 8, 128), F32)
    for number in (0, 5):
        every[number].wait_recv()
    side_mixed()
    inner_rows()
    for number in (1, 2, 3, 4, 6, 7, 8, 9, 10, 11, 12, 13):
        every[number].wait_recv()
    ends_mixed()
    end_rows()
    for copy in fcopies + every:
        copy.wait_send()


def on_device(
    nr, nc, features, gain_one, qkv_weight, bias_table, proj_weight, gain_two,
    hidden_weight, output_weight, group_conv, before_conv, upsample_conv,
):
    selector = jnp.asarray(table_selector(), BF16)
    operands = (
        features, gain_one, qkv_weight, bias_table.T, proj_weight, gain_two, hidden_weight,
        output_weight.T, group_conv, before_conv.transpose(0, 1, 3, 2),
        upsample_conv.reshape(3, 192, 256), selector,
    )
    any_space = pl.BlockSpec(memory_space=pltpu.HBM)
    staged = [pltpu.VMEM(x.shape, x.dtype) for x in operands]
    staged[10] = pltpu.VMEM((3, 256, 256), BF16)
    scratch = staged + [
        pltpu.VMEM((384, 128), BF16), pltpu.VMEM((384, 128), BF16),
        pltpu.VMEM((192, 128), BF16), pltpu.VMEM((192, 128), BF16), pltpu.VMEM((4, 48, 128), BF16),
        pltpu.VMEM((384, 128), BF16), pltpu.VMEM((384, 128), BF16),
        pltpu.VMEM((192, 128), BF16), pltpu.VMEM((192, 128), BF16), pltpu.VMEM((4, 48, 128), BF16),
        pltpu.VMEM((3, TW, 256), BF16), pltpu.VMEM((3, TW, 256), BF16),
        pltpu.VMEM((TH, 16, 256), BF16), pltpu.VMEM((TH, 16, 256), BF16),
        pltpu.VMEM((4, 3, 16, 256), BF16), pltpu.VMEM((TH, TW, 256), BF16),
        pltpu.VMEM((2, 24 * PITCH, 128), F32), pltpu.VMEM((2, 24 * PITCH, 128), F32),
        pltpu.VMEM((2, 22 * PITCH, 128), F32), pltpu.VMEM((2, 20 * GP, 128), F32),
        pltpu.VMEM((2, 18 * GP + 8, 128), F32), pltpu.VMEM((18 * GP + 8, 128), F32),
        pltpu.VMEM((18, TW, 256), BF16),
        pltpu.VMEM((256, 640), BF16), pltpu.VMEM((256, 256), BF16), pltpu.VMEM((256, 256), BF16),
        pltpu.VMEM((192, 256), BF16), pltpu.VMEM((256, 256), BF16), pltpu.VMEM((256, 256), BF16),
        pltpu.VMEM((256, 384), BF16), pltpu.VMEM((256, 384), BF16), pltpu.VMEM((384, 256), BF16),
        pltpu.VMEM((9, 256, 256), BF16), pltpu.VMEM((3, 256, 256), BF16),
        pltpu.VMEM((3, 256, 256), BF16), pltpu.VMEM((3, 256, 256), BF16),
        pltpu.VMEM((HEADS, KWIN * KWIN, 256), F32), pltpu.VMEM((KWIN * KWIN, 256), BF16),
        pltpu.VMEM((4, KWIN * KWIN, 256), BF16), pltpu.VMEM((4, 192, KWIN * KWIN), BF16),
        pltpu.VMEM((4, 256, 256), F32), pltpu.VMEM((2, KWIN * KWIN, 256), F32),
        pltpu.VMEM((2, KWIN * KWIN, 256), BF16), pltpu.VMEM((4, 192, 256), BF16),
        pltpu.VMEM((256, 256), F32), pltpu.VMEM((256, 256), BF16), pltpu.VMEM((256, 384), BF16),
        pltpu.VMEM((2, 64 * 16, 128), F32),
        pltpu.SemaphoreType.DMA((12,)), pltpu.SemaphoreType.DMA((8,)), pltpu.SemaphoreType.DMA((8,)),
        pltpu.SemaphoreType.DMA((14,)), pltpu.SemaphoreType.DMA((14,)),
    ]
    result = pl.pallas_call(
        functools.partial(kernel, nr, nc),
        out_shape=jax.ShapeDtypeStruct((64, 2 * TH, 2 * TW), BF16),
        in_specs=[any_space] * len(operands),
        out_specs=pl.BlockSpec(memory_space=pltpu.VMEM),
        scratch_shapes=scratch,
        compiler_params=pltpu.CompilerParams(
            collective_id=0, has_side_effects=True, vmem_limit_bytes=62 * 1024 * 1024
        ),
    )(*operands)
    return result


def solution(mesh):
    placed = (P("rows", "cols", None),) + (P(),) * 10
    body = functools.partial(on_device, mesh.shape["rows"], mesh.shape["cols"])
    return jax.shard_map(
        body, mesh=mesh, in_specs=placed, out_specs=P(None, "rows", "cols"), check_vma=False
    )
```

```python
import functools
import math

import jax
import jax.numpy as jnp
import numpy as np
from jax import lax
from jax.experimental import pallas as pl
from jax.experimental.pallas import tpu as pltpu
from jax.sharding import PartitionSpec as P

HEADS = 6
HEAD = 30
SLOT = 32
CH = 180
WIN = 16
KWIN = 24
SIDE = WIN + KWIN - 1
TABLE = SIDE * SIDE
TH = 16
TW = 64
PITCH = 80
GP = 72
QSCALE = math.log2(math.e) / math.sqrt(HEAD)
LOG2E = math.log2(math.e)
F32 = jnp.float32
BF16 = jnp.bfloat16
MESH = pl.DeviceIdType.MESH
NT = (((1,), (1,)), ((), ()))


def table_selector():
    out = np.zeros((384, 384), np.float32)
    for lane in range(128):
        for part in range(3):
            entry = 16 * part + lane % 16
            if entry < SIDE:
                out[SIDE * (7 - lane // 16) + SIDE - 1 - entry, 128 * part + lane] = 1.0
    return out


def mm(a, b):
    return jnp.dot(a, b, preferred_element_type=F32)


def mm_nt(a, b):
    return lax.dot_general(a, b, NT, preferred_element_type=F32)


def iota(shape, dim):
    return lax.broadcasted_iota(jnp.int32, shape, dim)


def one_hot(mask):
    return jnp.where(mask, 1.0, 0.0).astype(BF16)


def normalize(x, gain):
    lane = iota(x[1].shape, 1)
    mean = jnp.sum(x[0] + x[1], axis=-1, keepdims=True) * (1.0 / CH)
    low = x[0] - mean
    high = jnp.where(lane < CH - 128, x[1] - mean, 0.0)
    spread = jnp.sum(low * low + high * high, axis=-1, keepdims=True) * (1.0 / CH)
    scale = lax.rsqrt(spread + 1e-05)
    return low * scale * gain[:, 0:128], high * scale * gain[:, 128:256]


def pack_pixels(low, high):
    half = low.shape[0] // 2
    lane = iota((half, 128), 1)
    joined = jnp.where(lane < 64, high[:half], pltpu.roll(high[half:], 64, 1))
    return jnp.concatenate([low, joined], axis=0).astype(BF16)


def unpack_pixels(packed, valid):
    count = packed.shape[0] * 2 // 3
    x = jnp.where(valid, packed.astype(F32), 0.0)
    joined = x[count:]
    high = jnp.concatenate([joined, pltpu.roll(joined, 64, 1)], axis=0)
    return x[:count], jnp.where(iota(high.shape, 1) < CH - 128, high, 0.0)


def kernel(
    nr, nc,
    feat, gain1, qkv, table, proj, gain2, hid, outw, gconv, bconv, uconv, selector,
    out,
    feat_v, gain1_v, qkv_v, table_v, proj_v, gain2_v, hid_v, outw_v, gconv_v, bconv_v, upad, sel_v,
    send_t, send_b, send_l, send_r, send_c, halo_t, halo_b, halo_l, halo_r, halo_c,
    mix_t, mix_b, mix_l, mix_r, mix_c, mix_sl, mix_sr, mix_sc, mix_own,
    fpad, npad, mixpad, gbuf, ybuf, lbuf, l3,
    qpad, wqt, wk, wvt, ppad, pw, hpad, opad, wout, gpad, bpad, w2, w3, bias, xwin, kwin, vwin, qwin, sbuf, pbuf, attt, fbuf, second, inner, obuf, ostage, osem,
    local_sem, fsend, frecv, msend, mrecv,
):
    row = lax.axis_index("rows")
    col = lax.axis_index("cols")
    up = lax.rem(row + nr - 1, nr)
    down = lax.rem(row + 1, nr)
    left = lax.rem(col + nc - 1, nc)
    right = lax.rem(col + 1, nc)
    neighbours = [
        (up, col), (down, col), (row, left), (row, right),
        (up, left), (up, right), (down, left), (down, right),
    ]
    barrier = pltpu.get_barrier_semaphore()
    for target in neighbours:
        pl.semaphore_signal(barrier, inc=1, device_id=target, device_id_type=MESH)

    local = {}
    pairs = [
        ("feat", feat, feat_v), ("gain1", gain1, gain1_v), ("table", table, table_v),
        ("selector", selector, sel_v), ("qkv", qkv, qkv_v), ("proj", proj, proj_v),
        ("gain2", gain2, gain2_v), ("hid", hid, hid_v), ("outw", outw, outw_v),
        ("gconv", gconv, gconv_v), ("bconv", bconv, bconv_v), ("uconv", uconv, upad.at[:, 0:192, :]),
    ]
    for number, (name, source, target) in enumerate(pairs):
        local[name] = pltpu.make_async_copy(source, target, local_sem.at[number])
    for name in ("feat", "gain1", "table", "selector"):
        local[name].start()

    def arrive(*names):
        for name in names:
            local[name].wait()

    def exchange(specs, send_sem, recv_sem):
        copies = []
        for number, (source, target, device) in enumerate(specs):
            copies.append(
                pltpu.make_async_remote_copy(
                    src_ref=source, dst_ref=target, send_sem=send_sem.at[number],
                    recv_sem=recv_sem.at[number], device_id=device, device_id_type=MESH,
                )
            )
        return copies

    fcopies = exchange(
        [
            (send_c.at[3], halo_c.at[0], (down, right)),
            (send_c.at[1], halo_c.at[2], (up, right)),
            (send_t.at[0], halo_b.at[0], (up, col)),
            (send_b.at[0], halo_t.at[0], (down, col)),
            (send_r, halo_l, (row, right)),
            (send_c.at[0], halo_c.at[3], (up, left)),
            (send_c.at[2], halo_c.at[1], (down, left)),
            (send_l, halo_r, (row, left)),
            (send_t.at[1], halo_b.at[1], (up, col)),
            (send_b.at[1], halo_t.at[1], (down, col)),
        ],
        fsend, frecv,
    )

    has_up = row > 0
    has_down = row < nr - 1
    has_left = col > 0
    has_right = col < nc - 1

    fpad[1] = jnp.zeros(fpad.shape[1:], F32)
    arrive("feat", "gain1")
    for h in range(0, TH, 4):
        x = feat_v[h : h + 4].astype(F32).reshape(4 * TW, CH)
        for k in range(4):
            rows = pl.ds((h + k + 4) * PITCH + 8, TW)
            fpad[0, rows, :] = x[k * TW : (k + 1) * TW, 0:128]
            fpad[1, rows, 0 : CH - 128] = x[k * TW : (k + 1) * TW, 128:CH]

    def region(ref, first_row, count_rows, first_col, count_cols):
        return [
            jnp.concatenate(
                [
                    ref[half, pl.ds((first_row + k) * PITCH + first_col, count_cols), :]
                    for k in range(count_rows)
                ],
                axis=0,
            )
            for half in range(2)
        ]

    for part in range(2):
        send_t[part] = pack_pixels(*region(fpad, 4, 4, 8 + 32 * part, 32))
        send_b[part] = pack_pixels(*region(fpad, 16, 4, 8 + 32 * part, 32))
    send_l[...] = pack_pixels(*region(fpad, 4, TH, 8, 8))
    send_r[...] = pack_pixels(*region(fpad, 4, TH, 64, 8))
    for corner, (first_row, first_col) in enumerate(((4, 8), (4, 64), (16, 8), (16, 64))):
        send_c[corner] = pack_pixels(*region(fpad, first_row, 4, first_col, 8))
    pl.semaphore_wait(barrier, 8)
    for copy in fcopies:
        copy.start()
    for name in ("qkv", "proj", "gain2", "hid", "outw", "gconv", "bconv", "uconv"):
        local[name].start()

    def lanes256(ref):
        return jnp.concatenate([ref[...].reshape(1, CH), jnp.zeros((1, 256 - CH), F32)], axis=1)

    g1 = lanes256(gain1_v)

    def store_normed(x, starts):
        n = normalize(x, g1)
        width = x[0].shape[0] // len(starts)
        for k, start in enumerate(starts):
            for half in range(2):
                npad[half, pl.ds(start, width), :] = n[half][k * width : (k + 1) * width]

    def own_pixels():
        for h in range(0, TH, 4):
            store_normed(
                region(fpad, h + 4, 4, 8, TW), [(h + k + 4) * PITCH + 8 for k in range(4)]
            )

    own_pixels()
    for ref in (qpad, ppad, hpad, opad, gpad, bpad):
        ref[...] = jnp.zeros(ref.shape, ref.dtype)
    for a in range(3):
        upad[a, 192:256, :] = jnp.zeros((64, 256), BF16)

    r = iota((256, 256), 0)
    c = iota((256, 256), 1)
    identity = one_hot(r == c)

    def prepare_bias():
        whole = jnp.concatenate(
            [table_v[...] * LOG2E, jnp.zeros((HEADS, 1536 - TABLE), F32)], axis=1
        )
        whole = jnp.concatenate([whole, jnp.zeros((2, 1536), F32)], axis=0)
        lane8 = iota((8, 128), 1)
        sub8 = iota((8, 128), 0)
        pieces = []
        for tile in range(5):
            first = SIDE * (SIDE - 8 - 8 * tile)
            pieces.append(pltpu.roll(whole, (1536 - first) % 1536, 1)[:, 0:384])
        rows = jnp.concatenate(pieces, axis=0)
        hi = rows.astype(BF16)
        rest = rows - hi.astype(F32)
        mid = rest.astype(BF16)
        low = (rest - mid.astype(F32)).astype(BF16)
        picked = mm(hi, sel_v[...]) + mm(mid, sel_v[...]) + mm(low, sel_v[...])
        lane24 = iota((KWIN, 128), 1)
        for head in range(HEADS):
            tiles = []
            for tile in range(5):
                z = picked[8 * tile + head : 8 * tile + head + 1, :]
                blocks = []
                for part, base in ((1, 7), (0, 15), (0, 7)):
                    first = jnp.broadcast_to(z[:, 128 * part : 128 * part + 128], (8, 128))
                    second = jnp.broadcast_to(z[:, 128 * part + 128 : 128 * part + 256], (8, 128))
                    first = pltpu.roll(first, 128 - base, 1, stride=1, stride_axis=0)
                    second = pltpu.roll(second, 16 - base, 1, stride=1, stride_axis=0)
                    blocks.append(jnp.where((lane8 & 15) + base - sub8 < 16, first, second))
                tiles.append(jnp.concatenate(blocks, axis=0))
            for shift in range(8):
                amount = 16 * shift
                if shift:
                    rolled = [pltpu.roll(t, 128 - amount, 1) for t in tiles]
                    joined = [
                        jnp.where(lane24 < 128 - amount, rolled[k], rolled[k + 1]) for k in range(4)
                    ]
                else:
                    joined = tiles
                for block in range(3):
                    p = KWIN - 1 - 8 * block - shift
                    for half in range(2):
                        bias[head, KWIN * p : KWIN * (p + 1), 128 * half : 128 * half + 128] = (
                            joined[block + half]
                        )

    arrive("table", "selector")
    prepare_bias()

    def prepare_weights():
        qpad[0:CH, 0 : 3 * CH] = qkv_v[...]
        wqt[...] = mm_nt(one_hot((r == c) & (r < CH)), qpad[:, 0:256]).astype(BF16)
        wk[...] = mm(qpad[:, 128:384], one_hot((r == c + 52) & (c < CH))).astype(BF16)
        rv = iota((192, 384), 0)
        cv = iota((192, 384), 1)
        slot_source = HEAD * lax.shift_right_logical(rv, 5) + (rv & 31)
        wvt[...] = mm_nt(one_hot((cv == slot_source + 104) & ((rv & 31) < HEAD)), qpad[:, 256:640]).astype(BF16)
        ppad[0:CH, 0:CH] = proj_v[...]
        slot_source = HEAD * lax.shift_right_logical(r, 5) + (r & 31)
        pw[...] = mm(one_hot((c == slot_source) & ((r & 31) < HEAD) & (r < 192)), ppad[...]).astype(BF16)
        hpad[0:CH, 0 : 2 * CH] = hid_v[...]
        opad[0:CH, 0 : 2 * CH] = outw_v[...]
        wout[...] = mm_nt(one_hot(iota((384, 384), 0) == iota((384, 384), 1)), opad[...]).astype(BF16)
        for tap in range(9):
            gpad[tap, 0:CH, 0:CH] = gconv_v[tap // 3, tap % 3]
        order = 4 * (r & 63) + 2 * (lax.shift_right_logical(r, 6) & 1) + lax.shift_right_logical(r, 7)
        shuffle_rows = one_hot(c == order)
        for a in range(3):
            for b in range(3):
                bpad[a, 64 * b : 64 * (b + 1), 0:CH] = bconv_v[a, b]
            w2[a] = mm_nt(identity, bpad[a]).astype(BF16)
            w3[a] = mm_nt(shuffle_rows, upad[a]).astype(BF16)

    arrive("qkv", "proj", "gain2", "hid", "outw", "gconv", "bconv", "uconv")
    prepare_weights()
    def halo_pixels(part):
        side, rim, has_side = ((halo_l, 0, has_left), (halo_r, 72, has_right))[part]
        groups = [
            (halo_t[part], has_up, [h * PITCH + 8 + 32 * part for h in range(4)]),
            (halo_b[part], has_down, [(20 + h) * PITCH + 8 + 32 * part for h in range(4)]),
            (side[...], has_side, [(4 + h) * PITCH + rim for h in range(TH)]),
            (halo_c[part], has_up & has_side, [h * PITCH + rim for h in range(4)]),
            (halo_c[2 + part], has_down & has_side, [(20 + h) * PITCH + rim for h in range(4)]),
        ]
        for packed, valid, starts in groups:
            x = unpack_pixels(packed, valid)
            width = x[0].shape[0] // len(starts)
            for k, start in enumerate(starts):
                for half in range(2):
                    fpad[half, pl.ds(start, width), :] = x[half][k * width : (k + 1) * width]
            store_normed(x, starts)

    g2 = lanes256(gain2_v)
    inside = c < CH
    ones_row = (iota((192, KWIN * KWIN), 0) & 31) == HEAD
    tops = {}

    def pixels(ref, half, w, first_row, count_rows, first_col, count_cols):
        return jnp.concatenate(
            [
                ref[half, pl.ds((first_row + p) * PITCH + first_col + w * WIN, count_cols), :]
                for p in range(count_rows)
            ],
            axis=0,
        )

    def project_keys(w):
        keys_in = jnp.concatenate(
            [pixels(npad, half, w, 0, KWIN, 4, KWIN).astype(BF16) for half in range(2)], axis=1
        )
        xwin[...] = keys_in
        kwin[w] = mm(keys_in, wk[...]).astype(BF16)

    def project_values(w):
        vwin[w] = jnp.where(ones_row, 1.0, mm_nt(wvt[...], xwin[...])).astype(BF16)

    def project_queries(w):
        query_in = jnp.concatenate(
            [pixels(npad, half, w, 4, WIN, 8, WIN).astype(BF16) for half in range(2)], axis=1
        )
        qwin[w] = mm_nt(wqt[...], query_in) * QSCALE

    def score(number, w, head):
        mine = (r >= HEAD * head) & (r < HEAD * (head + 1))
        q = jnp.where(mine, qwin[w], 0.0).astype(BF16)
        top = None
        for part in (slice(0, 288), slice(288, 576)):
            scores = mm(kwin[w, part, :], q) + bias[head, part, :]
            sbuf[number % 2, part, :] = scores
            best = jnp.max(scores, axis=0, keepdims=True)
            top = best if top is None else jnp.maximum(top, best)
        tops[number] = top

    def exponent(number):
        pbuf[number % 2] = jnp.exp2(sbuf[number % 2] - tops[number]).astype(BF16)

    def combine(number, w, head):
        rows = slice(SLOT * head, SLOT * (head + 1))
        mixed_values = mm(vwin[w, rows, :], pbuf[number % 2])
        attt[w, rows, :] = (mixed_values / mixed_values[HEAD : HEAD + 1, :]).astype(BF16)

    def merge_heads(w):
        attended = mm_nt(identity, attt[w]).astype(BF16)
        base = jnp.concatenate([pixels(fpad, half, w, 4, WIN, 8, WIN) for half in range(2)], axis=1)
        first = base + mm(attended, pw[0:192, :])
        fbuf[...] = first
        center = first - jnp.sum(first, axis=-1, keepdims=True) * (1.0 / CH)
        center = jnp.where(inside, center, 0.0)
        spread = jnp.sum(center * center, axis=-1, keepdims=True) * (1.0 / CH)
        second[...] = (center * lax.rsqrt(spread + 1e-05) * g2).astype(BF16)

    def hidden(part):
        lanes = slice(128 * part, 128 * part + 128)
        value = mm(second[...], hpad[:, lanes])
        inner[:, lanes] = (0.5 * value * (1.0 + lax.erf(value * math.sqrt(0.5)))).astype(BF16)

    def finish_window(w):
        mixed = fbuf[...] + mm(inner[...], wout[...])
        for i in range(WIN):
            block = mixed[WIN * i : WIN * (i + 1), :]
            rows = pl.ds((3 + i) * PITCH + 8 + w * WIN, WIN)
            mixpad[0, rows, :] = block[:, 0:128]
            mixpad[1, rows, :] = block[:, 128:256]
            mix_own[i, w * WIN : (w + 1) * WIN, :] = block.astype(BF16)
        if w == 0:
            mix_sl[...] = pack_pixels(*region(mixpad, 3, TH, 8, 8))
            mix_sc[0] = pack_pixels(*region(mixpad, 3, 4, 8, 8))
            mix_sc[2] = pack_pixels(*region(mixpad, 15, 4, 8, 8))
        if w == 3:
            mix_sr[...] = pack_pixels(*region(mixpad, 3, TH, 64, 8))
            mix_sc[1] = pack_pixels(*region(mixpad, 3, 4, 64, 8))
            mix_sc[3] = pack_pixels(*region(mixpad, 15, 4, 64, 8))
        for copy in mcopies[w]:
            copy.start()

    def strip(w):
        cols = slice(w * WIN, (w + 1) * WIN)
        return [
            (mix_own.at[0:3, cols], mix_b.at[:, cols], (up, col)),
            (mix_own.at[13:16, cols], mix_t.at[:, cols], (down, col)),
        ]

    specs = {
        0: [
            (mix_sl, mix_r, (row, left)),
            (mix_sc.at[0], mix_c.at[3], (up, left)),
            (mix_sc.at[2], mix_c.at[1], (down, left)),
        ] + strip(0),
        3: [
            (mix_sr, mix_l, (row, right)),
            (mix_sc.at[1], mix_c.at[2], (up, right)),
            (mix_sc.at[3], mix_c.at[0], (down, right)),
        ] + strip(3),
        1: strip(1),
        2: strip(2),
    }
    windows = (0, 3, 1, 2)
    every = exchange([item for w in windows for item in specs[w]], msend, mrecv)
    mcopies = {0: every[0:5], 3: every[5:10], 1: every[10:12], 2: every[12:14]}
    steps = [(w, head) for w in windows for head in range(HEADS)]

    def first_half():
        halo_pixels(0)
        project_keys(0)
        project_values(0)
        attend(0, 3)

    def second_half():
        halo_pixels(1)
        attend(3, len(steps) + 2)
        merge_heads(windows[-1])
        for part in range(3):
            hidden(part)
        finish_window(windows[-1])

    def attend(begin, end):
        for number in range(begin, end):
            place, head = divmod(number, HEADS)
            if number < len(steps):
                score(number, windows[place], head)
            if 0 <= number - 1 < len(steps):
                exponent(number - 1)
            if 0 <= number - 2:
                combine(number - 2, *steps[number - 2])
            if place + 1 < len(windows) and 3 <= head <= 4:
                (project_keys, project_values)[head - 3](windows[place + 1])
            if 0 < place < len(windows):
                if head == 1:
                    merge_heads(windows[place - 1])
                elif 2 <= head <= 4:
                    hidden(head - 2)
                elif head == 5:
                    finish_window(windows[place - 1])

    def all_queries():
        for w in windows:
            project_queries(w)

    all_queries()
    for number in (0, 1, 2, 3, 4):
        fcopies[number].wait_recv()
    first_half()
    for number in (5, 6, 7, 8, 9):
        fcopies[number].wait_recv()
    second_half()

    def store_mixed(start, count, values, valid):
        x = jnp.where(valid, values, 0.0)
        rows = pl.ds(start, count)
        mixpad[0, rows, :] = x[:, 0:128]
        mixpad[1, rows, :] = x[:, 128:256]

    def store_packed(packed, valid, starts, skip=0):
        x = unpack_pixels(packed, valid)
        for k, start in enumerate(starts):
            part = slice((k + skip) * 8, (k + skip + 1) * 8)
            for half in range(2):
                mixpad[half, pl.ds(start, 8), :] = x[half][part]

    def side_mixed():
        store_packed(mix_l[...], has_left, [(3 + h) * PITCH for h in range(TH)])
        store_packed(mix_r[...], has_right, [(3 + h) * PITCH + 72 for h in range(TH)])

    def top_mixed():
        for h in range(3):
            store_mixed(h * PITCH + 8, TW, mix_t[h].astype(F32), has_up)
        store_packed(mix_c[0], has_up & has_left, [h * PITCH for h in range(3)], 1)
        store_packed(mix_c[1], has_up & has_right, [h * PITCH + 72 for h in range(3)], 1)

    def bottom_mixed():
        for h in range(3):
            store_mixed((19 + h) * PITCH + 8, TW, mix_b[h].astype(F32), has_down)
        store_packed(mix_c[2], has_down & has_left, [(19 + h) * PITCH for h in range(3)])
        store_packed(mix_c[3], has_down & has_right, [(19 + h) * PITCH + 72 for h in range(3)])

    cols72 = iota((GP, 128), 0)
    gcols = ((cols72 >= 2) | has_left) & ((cols72 < 66) | has_right)
    lcols = ((cols72 >= 1) | has_left) & ((cols72 < 65) | has_right)

    def conv_group(h0, count):
        acc = None
        for a in range(3):
            for b in range(3):
                halves = []
                for half in range(2):
                    rows = [
                        mixpad[half, pl.ds((h0 + k + a) * PITCH + 5 + b, GP), :] for k in range(count)
                    ]
                    halves.append(jnp.concatenate(rows, axis=0).astype(BF16))
                term = mm(jnp.concatenate(halves, axis=1), gpad[3 * a + b])
                acc = term if acc is None else acc + term
        for k in range(count):
            h = h0 + k
            keep = gcols & has_up if h < 2 else gcols & has_down if h >= 18 else gcols
            for half in range(2):
                base = fpad[half, pl.ds((h + 2) * PITCH + 6, GP), :]
                value = base + acc[GP * k : GP * (k + 1), 128 * half : 128 * half + 128]
                gbuf[half, pl.ds(h * GP, GP), :] = jnp.where(keep, value, 0.0)

    low_lanes = iota((GP, 128), 1) < 64
    low64 = iota((TW, 128), 1) < 64

    def conv_before(first, count):
        start = first * GP
        acc = None
        for a in range(3):
            rows = pl.ds(start + a * GP, count * GP)
            lhs = jnp.concatenate([gbuf[half, rows, :].astype(BF16) for half in range(2)], axis=1)
            term = mm(lhs, w2[a])
            acc = term if acc is None else acc + term
        rows = pl.ds(start, count * GP)
        ybuf[0, rows, :] = acc[:, 0:128]
        ybuf[1, rows, :] = acc[:, 128:256]
        for h in range(first, first + count):
            start = h * GP
            value = (
                ybuf[0, pl.ds(start, GP), :]
                + pltpu.roll(ybuf[0, pl.ds(start + 1, GP), :], 64, 1)
                + ybuf[1, pl.ds(start + 2, GP), :]
            )
            value = jnp.where(value >= 0, value, 0.01 * value)
            keep = lcols & has_up if h < 1 else lcols & has_down if h >= 17 else lcols
            value = jnp.where(keep, value, 0.0)
            lbuf[pl.ds(start, GP), :] = jnp.where(low_lanes, value, pltpu.roll(value, 64, 1))
        for h in range(first, first + count):
            start = h * GP
            zero = lbuf[pl.ds(start, TW), :]
            one = lbuf[pl.ds(start + 1, TW), :]
            two = lbuf[pl.ds(start + 2, TW), :]
            l3[h, :, 0:128] = jnp.where(low64, zero, one).astype(BF16)
            l3[h, :, 128:256] = jnp.where(low64, two, 0.0).astype(BF16)

    target = 128 * (lax.shift_right_logical(r, 6) & 1) + 2 * (r & 63) + lax.shift_right_logical(r, 7)
    weave = one_hot(c == target)

    def conv_up(step):
        acc = None
        for a in range(3):
            rhs = jnp.concatenate([l3[4 * step + a + k] for k in range(4)], axis=0)
            term = mm_nt(w3[a], rhs)
            acc = term if acc is None else acc + term
        acc = acc.astype(BF16)
        for pair in range(2):
            lanes = slice(128 * pair, 128 * pair + 128)
            both = jnp.concatenate([acc[0:128, lanes], acc[128:256, lanes]], axis=1)
            woven = mm(both, weave)
            for k in range(2):
                for a in range(2):
                    line = (2 * (4 * step + 2 * pair + k) + a) % 16
                    obuf[step // 2, pl.ds(line, 64, stride=16), :] = woven[
                        64 * a : 64 * (a + 1), 128 * k : 128 * k + 128
                    ]

    def inner_rows():
        for h0 in range(3, 17, 2):
            conv_group(h0, 2)
        conv_before(3, 6)
        conv_before(9, 6)
        conv_up(1)
        conv_up(2)

    def out_half(half):
        ostage[half] = obuf[half].reshape(64, 16, 128).astype(BF16)

    def top_rows():
        conv_group(0, 2)
        conv_group(2, 1)
        conv_before(0, 3)
        conv_up(0)
        out_half(0)

    def bottom_rows():
        conv_group(17, 2)
        conv_group(19, 1)
        conv_before(15, 3)
        conv_up(3)
        out_half(1)

    ybuf[:, 18 * GP :, :] = jnp.zeros((2, 8, 128), F32)
    for number in (0, 5):
        every[number].wait_recv()
    side_mixed()
    inner_rows()
    stores = [
        pltpu.make_async_copy(ostage.at[half], out.at[:, 16 * half : 16 * half + 16], osem.at[half])
        for half in range(2)
    ]
    for number in (2, 4, 7, 9, 11, 13):
        every[number].wait_recv()
    top_mixed()
    top_rows()
    stores[0].start()
    for number in (1, 3, 6, 8, 10, 12):
        every[number].wait_recv()
    bottom_mixed()
    bottom_rows()
    stores[1].start()
    for store in stores:
        store.wait()
    for copy in fcopies + every:
        copy.wait_send()


def on_device(
    nr, nc, features, gain_one, qkv_weight, bias_table, proj_weight, gain_two,
    hidden_weight, output_weight, group_conv, before_conv, upsample_conv,
):
    selector = jnp.asarray(table_selector(), BF16)
    operands = (
        features, gain_one, qkv_weight, bias_table.T, proj_weight, gain_two, hidden_weight,
        output_weight.T, group_conv, before_conv.transpose(0, 1, 3, 2),
        upsample_conv.reshape(3, 192, 256), selector,
    )
    any_space = pl.BlockSpec(memory_space=pl.ANY)
    staged = [pltpu.VMEM(x.shape, x.dtype) for x in operands]
    staged[10] = pltpu.VMEM((3, 256, 256), BF16)
    scratch = staged + [
        pltpu.VMEM((2, 192, 128), BF16), pltpu.VMEM((2, 192, 128), BF16),
        pltpu.VMEM((192, 128), BF16), pltpu.VMEM((192, 128), BF16), pltpu.VMEM((4, 48, 128), BF16),
        pltpu.VMEM((2, 192, 128), BF16), pltpu.VMEM((2, 192, 128), BF16),
        pltpu.VMEM((192, 128), BF16), pltpu.VMEM((192, 128), BF16), pltpu.VMEM((4, 48, 128), BF16),
        pltpu.VMEM((3, TW, 256), BF16), pltpu.VMEM((3, TW, 256), BF16),
        pltpu.VMEM((192, 128), BF16), pltpu.VMEM((192, 128), BF16), pltpu.VMEM((4, 48, 128), BF16),
        pltpu.VMEM((192, 128), BF16), pltpu.VMEM((192, 128), BF16), pltpu.VMEM((4, 48, 128), BF16),
        pltpu.VMEM((TH, TW, 256), BF16),
        pltpu.VMEM((2, 24 * PITCH, 128), F32), pltpu.VMEM((2, 24 * PITCH, 128), F32),
        pltpu.VMEM((2, 22 * PITCH, 128), F32), pltpu.VMEM((2, 20 * GP, 128), F32),
        pltpu.VMEM((2, 18 * GP + 8, 128), F32), pltpu.VMEM((18 * GP + 8, 128), F32),
        pltpu.VMEM((18, TW, 256), BF16),
        pltpu.VMEM((256, 640), BF16), pltpu.VMEM((256, 256), BF16), pltpu.VMEM((256, 256), BF16),
        pltpu.VMEM((192, 256), BF16), pltpu.VMEM((256, 256), BF16), pltpu.VMEM((256, 256), BF16),
        pltpu.VMEM((256, 384), BF16), pltpu.VMEM((256, 384), BF16), pltpu.VMEM((384, 256), BF16),
        pltpu.VMEM((9, 256, 256), BF16), pltpu.VMEM((3, 256, 256), BF16),
        pltpu.VMEM((3, 256, 256), BF16), pltpu.VMEM((3, 256, 256), BF16),
        pltpu.VMEM((HEADS, KWIN * KWIN, 256), F32), pltpu.VMEM((KWIN * KWIN, 256), BF16),
        pltpu.VMEM((4, KWIN * KWIN, 256), BF16), pltpu.VMEM((4, 192, KWIN * KWIN), BF16),
        pltpu.VMEM((4, 256, 256), F32), pltpu.VMEM((2, KWIN * KWIN, 256), F32),
        pltpu.VMEM((2, KWIN * KWIN, 256), BF16), pltpu.VMEM((4, 192, 256), BF16),
        pltpu.VMEM((256, 256), F32), pltpu.VMEM((256, 256), BF16), pltpu.VMEM((256, 384), BF16),
        pltpu.VMEM((2, 64 * 16, 128), F32), pltpu.VMEM((2, 64, 16, 128), BF16),
        pltpu.SemaphoreType.DMA((2,)),
        pltpu.SemaphoreType.DMA((12,)), pltpu.SemaphoreType.DMA((10,)), pltpu.SemaphoreType.DMA((10,)),
        pltpu.SemaphoreType.DMA((14,)), pltpu.SemaphoreType.DMA((14,)),
    ]
    result = pl.pallas_call(
        functools.partial(kernel, nr, nc),
        out_shape=jax.ShapeDtypeStruct((64, 2 * TH, 2 * TW), BF16),
        in_specs=[any_space] * len(operands),
        out_specs=pl.BlockSpec(memory_space=pl.ANY),
        scratch_shapes=scratch,
        compiler_params=pltpu.CompilerParams(
            collective_id=0, has_side_effects=True, vmem_limit_bytes=62 * 1024 * 1024
        ),
    )(*operands)
    return result


def solution(mesh):
    placed = (P("rows", "cols", None),) + (P(),) * 10
    body = functools.partial(on_device, mesh.shape["rows"], mesh.shape["cols"])
    return jax.shard_map(
        body, mesh=mesh, in_specs=placed, out_specs=P(None, "rows", "cols"), check_vma=False
    )
```

```python
import functools
import math

import jax
import jax.numpy as jnp
import numpy as np
from jax import lax
from jax.experimental import pallas as pl
from jax.experimental.pallas import tpu as pltpu
from jax.sharding import PartitionSpec as P

HEADS = 6
HEAD = 30
SLOT = 32
CH = 180
WIN = 16
KWIN = 24
SIDE = WIN + KWIN - 1
TABLE = SIDE * SIDE
TH = 16
TW = 64
PITCH = 80
GP = 72
QSCALE = math.log2(math.e) / math.sqrt(HEAD)
LOG2E = math.log2(math.e)
F32 = jnp.float32
BF16 = jnp.bfloat16
MESH = pl.DeviceIdType.MESH
NT = (((1,), (1,)), ((), ()))


def table_selector():
    out = np.zeros((384, 384), np.float32)
    for lane in range(128):
        for part in range(3):
            entry = 16 * part + lane % 16
            if entry < SIDE:
                out[SIDE * (7 - lane // 16) + SIDE - 1 - entry, 128 * part + lane] = 1.0
    return out


def mm(a, b):
    return jnp.dot(a, b, preferred_element_type=F32)


def mm_nt(a, b):
    return lax.dot_general(a, b, NT, preferred_element_type=F32)


def iota(shape, dim):
    return lax.broadcasted_iota(jnp.int32, shape, dim)


def one_hot(mask):
    return jnp.where(mask, 1.0, 0.0).astype(BF16)


def normalize(x, gain):
    lane = iota(x[1].shape, 1)
    mean = jnp.sum(x[0] + x[1], axis=-1, keepdims=True) * (1.0 / CH)
    low = x[0] - mean
    high = jnp.where(lane < CH - 128, x[1] - mean, 0.0)
    spread = jnp.sum(low * low + high * high, axis=-1, keepdims=True) * (1.0 / CH)
    scale = lax.rsqrt(spread + 1e-05)
    return low * scale * gain[:, 0:128], high * scale * gain[:, 128:256]


def pack_pixels(low, high):
    half = low.shape[0] // 2
    lane = iota((half, 128), 1)
    joined = jnp.where(lane < 64, high[:half], pltpu.roll(high[half:], 64, 1))
    return jnp.concatenate([low, joined], axis=0).astype(BF16)


def unpack_pixels(packed, valid):
    count = packed.shape[0] * 2 // 3
    x = jnp.where(valid, packed.astype(F32), 0.0)
    joined = x[count:]
    high = jnp.concatenate([joined, pltpu.roll(joined, 64, 1)], axis=0)
    return x[:count], jnp.where(iota(high.shape, 1) < CH - 128, high, 0.0)


def kernel(
    nr, nc,
    feat, gain1, qkv, table, proj, gain2, hid, outw, gconv, bconv, uconv, selector,
    out,
    feat_v, gain1_v, qkv_v, table_v, proj_v, gain2_v, hid_v, outw_v, gconv_v, bconv_v, upad, sel_v,
    send_t, send_b, send_l, send_r, send_c, halo_t, halo_b, halo_l, halo_r, halo_c,
    mix_t, mix_b, mix_l, mix_r, mix_c, mix_sl, mix_sr, mix_sc, mix_own,
    fpad, npad, mixpad, gbuf, ybuf, lbuf, l3,
    qpad, wqt, wk, wvt, ppad, pw, hpad, opad, wout, gpad, bpad, w2, w3, bias, xwin, kwin, vwin, qwin, sbuf, pbuf, attt, fbuf, second, inner, obuf, ostage, osem,
    local_sem, fsend, frecv, msend, mrecv,
):
    row = lax.axis_index("rows")
    col = lax.axis_index("cols")
    up = lax.rem(row + nr - 1, nr)
    down = lax.rem(row + 1, nr)
    left = lax.rem(col + nc - 1, nc)
    right = lax.rem(col + 1, nc)
    has_up = row > 0
    has_down = row < nr - 1
    has_left = col > 0
    has_right = col < nc - 1
    place = {
        "u": ((up, col), has_up), "d": ((down, col), has_down),
        "l": ((row, left), has_left), "r": ((row, right), has_right),
        "ul": ((up, left), has_up & has_left), "ur": ((up, right), has_up & has_right),
        "dl": ((down, left), has_down & has_left), "dr": ((down, right), has_down & has_right),
    }
    opposite = {"u": "d", "d": "u", "l": "r", "r": "l", "ul": "dr", "dr": "ul", "ur": "dl", "dl": "ur"}
    barrier = pltpu.get_barrier_semaphore()
    expected = 0
    for device, exists in place.values():
        expected = expected + jnp.where(exists, 1, 0)

        @pl.when(exists)
        def _(device=device):
            pl.semaphore_signal(barrier, inc=1, device_id=device, device_id_type=MESH)

    local = {}
    pairs = [
        ("feat", feat, feat_v), ("gain1", gain1, gain1_v), ("table", table, table_v),
        ("selector", selector, sel_v), ("qkv", qkv, qkv_v), ("proj", proj, proj_v),
        ("gain2", gain2, gain2_v), ("hid", hid, hid_v), ("outw", outw, outw_v),
        ("gconv", gconv, gconv_v), ("bconv", bconv, bconv_v), ("uconv", uconv, upad.at[:, 0:192, :]),
    ]
    for number, (name, source, target) in enumerate(pairs):
        local[name] = pltpu.make_async_copy(source, target, local_sem.at[number])
    for name in ("feat", "gain1", "table", "selector"):
        local[name].start()

    def arrive(*names):
        for name in names:
            local[name].wait()

    def exchange(specs, send_sem, recv_sem):
        copies = []
        for number, (source, target, way) in enumerate(specs):
            copy = pltpu.make_async_remote_copy(
                src_ref=source, dst_ref=target, send_sem=send_sem.at[number],
                recv_sem=recv_sem.at[number], device_id=place[way][0], device_id_type=MESH,
            )
            copies.append((copy, place[way][1], place[opposite[way]][1]))
        return copies

    def start(copies):
        for copy, sends, _ in copies:
            pl.when(sends)(copy.start)

    def wait_recv(copies):
        for copy, _, receives in copies:
            pl.when(receives)(copy.wait_recv)

    def wait_send(copies):
        for copy, sends, _ in copies:
            pl.when(sends)(copy.wait_send)

    fcopies = exchange(
        [
            (send_c.at[3], halo_c.at[0], "dr"),
            (send_c.at[1], halo_c.at[2], "ur"),
            (send_t.at[0], halo_b.at[0], "u"),
            (send_b.at[0], halo_t.at[0], "d"),
            (send_r, halo_l, "r"),
            (send_c.at[0], halo_c.at[3], "ul"),
            (send_c.at[2], halo_c.at[1], "dl"),
            (send_l, halo_r, "l"),
            (send_t.at[1], halo_b.at[1], "u"),
            (send_b.at[1], halo_t.at[1], "d"),
        ],
        fsend, frecv,
    )

    fpad[1] = jnp.zeros(fpad.shape[1:], F32)
    arrive("feat", "gain1")
    for h in range(0, TH, 4):
        x = feat_v[h : h + 4].astype(F32).reshape(4 * TW, CH)
        for k in range(4):
            rows = pl.ds((h + k + 4) * PITCH + 8, TW)
            fpad[0, rows, :] = x[k * TW : (k + 1) * TW, 0:128]
            fpad[1, rows, 0 : CH - 128] = x[k * TW : (k + 1) * TW, 128:CH]

    def region(ref, first_row, count_rows, first_col, count_cols):
        return [
            jnp.concatenate(
                [
                    ref[half, pl.ds((first_row + k) * PITCH + first_col, count_cols), :]
                    for k in range(count_rows)
                ],
                axis=0,
            )
            for half in range(2)
        ]

    for part in range(2):
        send_t[part] = pack_pixels(*region(fpad, 4, 4, 8 + 32 * part, 32))
        send_b[part] = pack_pixels(*region(fpad, 16, 4, 8 + 32 * part, 32))
    send_l[...] = pack_pixels(*region(fpad, 4, TH, 8, 8))
    send_r[...] = pack_pixels(*region(fpad, 4, TH, 64, 8))
    for corner, (first_row, first_col) in enumerate(((4, 8), (4, 64), (16, 8), (16, 64))):
        send_c[corner] = pack_pixels(*region(fpad, first_row, 4, first_col, 8))
    pl.semaphore_wait(barrier, expected)
    start(fcopies)
    for name in ("qkv", "proj", "gain2", "hid", "outw", "gconv", "bconv", "uconv"):
        local[name].start()

    def lanes256(ref):
        return jnp.concatenate([ref[...].reshape(1, CH), jnp.zeros((1, 256 - CH), F32)], axis=1)

    g1 = lanes256(gain1_v)

    def store_normed(x, starts):
        n = normalize(x, g1)
        width = x[0].shape[0] // len(starts)
        for k, start in enumerate(starts):
            for half in range(2):
                npad[half, pl.ds(start, width), :] = n[half][k * width : (k + 1) * width]

    def own_pixels():
        for h in range(0, TH, 4):
            store_normed(
                region(fpad, h + 4, 4, 8, TW), [(h + k + 4) * PITCH + 8 for k in range(4)]
            )

    own_pixels()
    for ref in (qpad, ppad, hpad, opad, gpad, bpad):
        ref[...] = jnp.zeros(ref.shape, ref.dtype)
    for a in range(3):
        upad[a, 192:256, :] = jnp.zeros((64, 256), BF16)

    r = iota((256, 256), 0)
    c = iota((256, 256), 1)
    identity = one_hot(r == c)

    def prepare_bias():
        whole = jnp.concatenate(
            [table_v[...] * LOG2E, jnp.zeros((HEADS, 1536 - TABLE), F32)], axis=1
        )
        whole = jnp.concatenate([whole, jnp.zeros((2, 1536), F32)], axis=0)
        lane8 = iota((8, 128), 1)
        sub8 = iota((8, 128), 0)
        pieces = []
        for tile in range(5):
            first = SIDE * (SIDE - 8 - 8 * tile)
            pieces.append(pltpu.roll(whole, (1536 - first) % 1536, 1)[:, 0:384])
        rows = jnp.concatenate(pieces, axis=0)
        hi = rows.astype(BF16)
        rest = rows - hi.astype(F32)
        mid = rest.astype(BF16)
        low = (rest - mid.astype(F32)).astype(BF16)
        picked = mm(hi, sel_v[...]) + mm(mid, sel_v[...]) + mm(low, sel_v[...])
        lane24 = iota((KWIN, 128), 1)
        for head in range(HEADS):
            tiles = []
            for tile in range(5):
                z = picked[8 * tile + head : 8 * tile + head + 1, :]
                blocks = []
                for part, base in ((1, 7), (0, 15), (0, 7)):
                    first = jnp.broadcast_to(z[:, 128 * part : 128 * part + 128], (8, 128))
                    second = jnp.broadcast_to(z[:, 128 * part + 128 : 128 * part + 256], (8, 128))
                    first = pltpu.roll(first, 128 - base, 1, stride=1, stride_axis=0)
                    second = pltpu.roll(second, 16 - base, 1, stride=1, stride_axis=0)
                    blocks.append(jnp.where((lane8 & 15) + base - sub8 < 16, first, second))
                tiles.append(jnp.concatenate(blocks, axis=0))
            for shift in range(8):
                amount = 16 * shift
                if shift:
                    rolled = [pltpu.roll(t, 128 - amount, 1) for t in tiles]
                    joined = [
                        jnp.where(lane24 < 128 - amount, rolled[k], rolled[k + 1]) for k in range(4)
                    ]
                else:
                    joined = tiles
                for block in range(3):
                    p = KWIN - 1 - 8 * block - shift
                    for half in range(2):
                        bias[head, KWIN * p : KWIN * (p + 1), 128 * half : 128 * half + 128] = (
                            joined[block + half]
                        )

    arrive("table", "selector")
    prepare_bias()

    def prepare_weights():
        qpad[0:CH, 0 : 3 * CH] = qkv_v[...]
        wqt[...] = mm_nt(one_hot((r == c) & (r < CH)), qpad[:, 0:256]).astype(BF16)
        wk[...] = mm(qpad[:, 128:384], one_hot((r == c + 52) & (c < CH))).astype(BF16)
        rv = iota((192, 384), 0)
        cv = iota((192, 384), 1)
        slot_source = HEAD * lax.shift_right_logical(rv, 5) + (rv & 31)
        wvt[...] = mm_nt(one_hot((cv == slot_source + 104) & ((rv & 31) < HEAD)), qpad[:, 256:640]).astype(BF16)
        ppad[0:CH, 0:CH] = proj_v[...]
        slot_source = HEAD * lax.shift_right_logical(r, 5) + (r & 31)
        pw[...] = mm(one_hot((c == slot_source) & ((r & 31) < HEAD) & (r < 192)), ppad[...]).astype(BF16)
        hpad[0:CH, 0 : 2 * CH] = hid_v[...]
        opad[0:CH, 0 : 2 * CH] = outw_v[...]
        wout[...] = mm_nt(one_hot(iota((384, 384), 0) == iota((384, 384), 1)), opad[...]).astype(BF16)
        for tap in range(9):
            gpad[tap, 0:CH, 0:CH] = gconv_v[tap // 3, tap % 3]
        order = 4 * (r & 63) + 2 * (lax.shift_right_logical(r, 6) & 1) + lax.shift_right_logical(r, 7)
        shuffle_rows = one_hot(c == order)
        for a in range(3):
            for b in range(3):
                bpad[a, 64 * b : 64 * (b + 1), 0:CH] = bconv_v[a, b]
            w2[a] = mm_nt(identity, bpad[a]).astype(BF16)
            w3[a] = mm_nt(shuffle_rows, upad[a]).astype(BF16)

    arrive("qkv", "proj", "gain2", "hid", "outw", "gconv", "bconv", "uconv")
    prepare_weights()
    def halo_pixels(part):
        side, rim, has_side = ((halo_l, 0, has_left), (halo_r, 72, has_right))[part]
        groups = [
            (halo_t[part], has_up, [h * PITCH + 8 + 32 * part for h in range(4)]),
            (halo_b[part], has_down, [(20 + h) * PITCH + 8 + 32 * part for h in range(4)]),
            (side[...], has_side, [(4 + h) * PITCH + rim for h in range(TH)]),
            (halo_c[part], has_up & has_side, [h * PITCH + rim for h in range(4)]),
            (halo_c[2 + part], has_down & has_side, [(20 + h) * PITCH + rim for h in range(4)]),
        ]
        for packed, valid, starts in groups:
            x = unpack_pixels(packed, valid)
            width = x[0].shape[0] // len(starts)
            for k, start in enumerate(starts):
                for half in range(2):
                    fpad[half, pl.ds(start, width), :] = x[half][k * width : (k + 1) * width]
            store_normed(x, starts)

    g2 = lanes256(gain2_v)
    inside = c < CH
    ones_row = (iota((192, KWIN * KWIN), 0) & 31) == HEAD
    tops = {}

    def pixels(ref, half, w, first_row, count_rows, first_col, count_cols):
        return jnp.concatenate(
            [
                ref[half, pl.ds((first_row + p) * PITCH + first_col + w * WIN, count_cols), :]
                for p in range(count_rows)
            ],
            axis=0,
        )

    def project_keys(w):
        keys_in = jnp.concatenate(
            [pixels(npad, half, w, 0, KWIN, 4, KWIN).astype(BF16) for half in range(2)], axis=1
        )
        xwin[...] = keys_in
        kwin[w] = mm(keys_in, wk[...]).astype(BF16)

    def project_values(w):
        vwin[w] = jnp.where(ones_row, 1.0, mm_nt(wvt[...], xwin[...])).astype(BF16)

    def project_queries(w):
        query_in = jnp.concatenate(
            [pixels(npad, half, w, 4, WIN, 8, WIN).astype(BF16) for half in range(2)], axis=1
        )
        qwin[w] = mm_nt(wqt[...], query_in) * QSCALE

    def score(number, w, head):
        mine = (r >= HEAD * head) & (r < HEAD * (head + 1))
        q = jnp.where(mine, qwin[w], 0.0).astype(BF16)
        top = None
        for part in (slice(0, 288), slice(288, 576)):
            scores = mm(kwin[w, part, :], q) + bias[head, part, :]
            sbuf[number % 2, part, :] = scores
            best = jnp.max(scores, axis=0, keepdims=True)
            top = best if top is None else jnp.maximum(top, best)
        tops[number] = top

    def exponent(number):
        pbuf[number % 2] = jnp.exp2(sbuf[number % 2] - tops[number]).astype(BF16)

    def combine(number, w, head):
        rows = slice(SLOT * head, SLOT * (head + 1))
        mixed_values = mm(vwin[w, rows, :], pbuf[number % 2])
        attt[w, rows, :] = (mixed_values / mixed_values[HEAD : HEAD + 1, :]).astype(BF16)

    def merge_heads(w):
        attended = mm_nt(identity, attt[w]).astype(BF16)
        base = jnp.concatenate([pixels(fpad, half, w, 4, WIN, 8, WIN) for half in range(2)], axis=1)
        first = base + mm(attended, pw[0:192, :])
        fbuf[...] = first
        center = first - jnp.sum(first, axis=-1, keepdims=True) * (1.0 / CH)
        center = jnp.where(inside, center, 0.0)
        spread = jnp.sum(center * center, axis=-1, keepdims=True) * (1.0 / CH)
        second[...] = (center * lax.rsqrt(spread + 1e-05) * g2).astype(BF16)

    def hidden(part):
        lanes = slice(128 * part, 128 * part + 128)
        value = mm(second[...], hpad[:, lanes])
        inner[:, lanes] = (0.5 * value * (1.0 + lax.erf(value * math.sqrt(0.5)))).astype(BF16)

    def finish_window(w):
        mixed = fbuf[...] + mm(inner[...], wout[...])
        for i in range(WIN):
            block = mixed[WIN * i : WIN * (i + 1), :]
            rows = pl.ds((3 + i) * PITCH + 8 + w * WIN, WIN)
            mixpad[0, rows, :] = block[:, 0:128]
            mixpad[1, rows, :] = block[:, 128:256]
            mix_own[i, w * WIN : (w + 1) * WIN, :] = block.astype(BF16)
        if w == 0:
            mix_sl[...] = pack_pixels(*region(mixpad, 3, TH, 8, 8))
            mix_sc[0] = pack_pixels(*region(mixpad, 3, 4, 8, 8))
            mix_sc[2] = pack_pixels(*region(mixpad, 15, 4, 8, 8))
        if w == 3:
            mix_sr[...] = pack_pixels(*region(mixpad, 3, TH, 64, 8))
            mix_sc[1] = pack_pixels(*region(mixpad, 3, 4, 64, 8))
            mix_sc[3] = pack_pixels(*region(mixpad, 15, 4, 64, 8))
        start(mcopies[w])

    def strip(w):
        cols = slice(w * WIN, (w + 1) * WIN)
        return [
            (mix_own.at[0:3, cols], mix_b.at[:, cols], "u"),
            (mix_own.at[13:16, cols], mix_t.at[:, cols], "d"),
        ]

    specs = {
        0: [
            (mix_sl, mix_r, "l"),
            (mix_sc.at[0], mix_c.at[3], "ul"),
            (mix_sc.at[2], mix_c.at[1], "dl"),
        ] + strip(0),
        3: [
            (mix_sr, mix_l, "r"),
            (mix_sc.at[1], mix_c.at[2], "ur"),
            (mix_sc.at[3], mix_c.at[0], "dr"),
        ] + strip(3),
        1: strip(1),
        2: strip(2),
    }
    windows = (0, 3, 1, 2)
    every = exchange([item for w in windows for item in specs[w]], msend, mrecv)
    mcopies = {0: every[0:5], 3: every[5:10], 1: every[10:12], 2: every[12:14]}
    steps = [(w, head) for w in windows for head in range(HEADS)]

    def first_half():
        halo_pixels(0)
        project_keys(0)
        project_values(0)
        attend(0, 3)

    def second_half():
        halo_pixels(1)
        attend(3, len(steps) + 2)
        merge_heads(windows[-1])
        for part in range(3):
            hidden(part)
        finish_window(windows[-1])

    def attend(begin, end):
        for number in range(begin, end):
            turn, head = divmod(number, HEADS)
            if number < len(steps):
                score(number, windows[turn], head)
            if 0 <= number - 1 < len(steps):
                exponent(number - 1)
            if 0 <= number - 2:
                combine(number - 2, *steps[number - 2])
            if turn + 1 < len(windows) and 3 <= head <= 4:
                (project_keys, project_values)[head - 3](windows[turn + 1])
            if 0 < turn < len(windows):
                if head == 1:
                    merge_heads(windows[turn - 1])
                elif 2 <= head <= 4:
                    hidden(head - 2)
                elif head == 5:
                    finish_window(windows[turn - 1])

    def all_queries():
        for w in windows:
            project_queries(w)

    all_queries()
    wait_recv(fcopies[k] for k in (0, 1, 2, 3, 4))
    first_half()
    wait_recv(fcopies[k] for k in (5, 6, 7, 8, 9))
    second_half()

    def store_mixed(start, count, values, valid):
        x = jnp.where(valid, values, 0.0)
        rows = pl.ds(start, count)
        mixpad[0, rows, :] = x[:, 0:128]
        mixpad[1, rows, :] = x[:, 128:256]

    def store_packed(packed, valid, starts, skip=0):
        x = unpack_pixels(packed, valid)
        for k, start in enumerate(starts):
            part = slice((k + skip) * 8, (k + skip + 1) * 8)
            for half in range(2):
                mixpad[half, pl.ds(start, 8), :] = x[half][part]

    def side_mixed():
        store_packed(mix_l[...], has_left, [(3 + h) * PITCH for h in range(TH)])
        store_packed(mix_r[...], has_right, [(3 + h) * PITCH + 72 for h in range(TH)])

    def top_mixed():
        for h in range(3):
            store_mixed(h * PITCH + 8, TW, mix_t[h].astype(F32), has_up)
        store_packed(mix_c[0], has_up & has_left, [h * PITCH for h in range(3)], 1)
        store_packed(mix_c[1], has_up & has_right, [h * PITCH + 72 for h in range(3)], 1)

    def bottom_mixed():
        for h in range(3):
            store_mixed((19 + h) * PITCH + 8, TW, mix_b[h].astype(F32), has_down)
        store_packed(mix_c[2], has_down & has_left, [(19 + h) * PITCH for h in range(3)])
        store_packed(mix_c[3], has_down & has_right, [(19 + h) * PITCH + 72 for h in range(3)])

    cols72 = iota((GP, 128), 0)
    gcols = ((cols72 >= 2) | has_left) & ((cols72 < 66) | has_right)
    lcols = ((cols72 >= 1) | has_left) & ((cols72 < 65) | has_right)

    def conv_group(h0, count):
        acc = None
        for a in range(3):
            for b in range(3):
                halves = []
                for half in range(2):
                    rows = [
                        mixpad[half, pl.ds((h0 + k + a) * PITCH + 5 + b, GP), :] for k in range(count)
                    ]
                    halves.append(jnp.concatenate(rows, axis=0).astype(BF16))
                term = mm(jnp.concatenate(halves, axis=1), gpad[3 * a + b])
                acc = term if acc is None else acc + term
        for k in range(count):
            h = h0 + k
            keep = gcols & has_up if h < 2 else gcols & has_down if h >= 18 else gcols
            for half in range(2):
                base = fpad[half, pl.ds((h + 2) * PITCH + 6, GP), :]
                value = base + acc[GP * k : GP * (k + 1), 128 * half : 128 * half + 128]
                gbuf[half, pl.ds(h * GP, GP), :] = jnp.where(keep, value, 0.0)

    low_lanes = iota((GP, 128), 1) < 64
    low64 = iota((TW, 128), 1) < 64

    def conv_before(first, count):
        start = first * GP
        acc = None
        for a in range(3):
            rows = pl.ds(start + a * GP, count * GP)
            lhs = jnp.concatenate([gbuf[half, rows, :].astype(BF16) for half in range(2)], axis=1)
            term = mm(lhs, w2[a])
            acc = term if acc is None else acc + term
        rows = pl.ds(start, count * GP)
        ybuf[0, rows, :] = acc[:, 0:128]
        ybuf[1, rows, :] = acc[:, 128:256]
        for h in range(first, first + count):
            start = h * GP
            value = (
                ybuf[0, pl.ds(start, GP), :]
                + pltpu.roll(ybuf[0, pl.ds(start + 1, GP), :], 64, 1)
                + ybuf[1, pl.ds(start + 2, GP), :]
            )
            value = jnp.where(value >= 0, value, 0.01 * value)
            keep = lcols & has_up if h < 1 else lcols & has_down if h >= 17 else lcols
            value = jnp.where(keep, value, 0.0)
            lbuf[pl.ds(start, GP), :] = jnp.where(low_lanes, value, pltpu.roll(value, 64, 1))
        for h in range(first, first + count):
            start = h * GP
            zero = lbuf[pl.ds(start, TW), :]
            one = lbuf[pl.ds(start + 1, TW), :]
            two = lbuf[pl.ds(start + 2, TW), :]
            l3[h, :, 0:128] = jnp.where(low64, zero, one).astype(BF16)
            l3[h, :, 128:256] = jnp.where(low64, two, 0.0).astype(BF16)

    target = 128 * (lax.shift_right_logical(r, 6) & 1) + 2 * (r & 63) + lax.shift_right_logical(r, 7)
    weave = one_hot(c == target)

    def conv_up(step):
        acc = None
        for a in range(3):
            rhs = jnp.concatenate([l3[4 * step + a + k] for k in range(4)], axis=0)
            term = mm_nt(w3[a], rhs)
            acc = term if acc is None else acc + term
        acc = acc.astype(BF16)
        for pair in range(2):
            lanes = slice(128 * pair, 128 * pair + 128)
            both = jnp.concatenate([acc[0:128, lanes], acc[128:256, lanes]], axis=1)
            woven = mm(both, weave)
            for k in range(2):
                for a in range(2):
                    line = (2 * (4 * step + 2 * pair + k) + a) % 16
                    obuf[step // 2, pl.ds(line, 64, stride=16), :] = woven[
                        64 * a : 64 * (a + 1), 128 * k : 128 * k + 128
                    ]

    def inner_rows():
        for h0 in range(3, 17, 2):
            conv_group(h0, 2)
        conv_before(3, 6)
        conv_before(9, 6)
        conv_up(1)
        conv_up(2)

    def out_half(half):
        ostage[half] = obuf[half].reshape(64, 16, 128).astype(BF16)

    def top_rows():
        conv_group(0, 2)
        conv_group(2, 1)
        conv_before(0, 3)
        conv_up(0)
        out_half(0)

    def bottom_rows():
        conv_group(17, 2)
        conv_group(19, 1)
        conv_before(15, 3)
        conv_up(3)
        out_half(1)

    ybuf[:, 18 * GP :, :] = jnp.zeros((2, 8, 128), F32)
    wait_recv(every[k] for k in (0, 5))
    side_mixed()
    inner_rows()
    stores = [
        pltpu.make_async_copy(ostage.at[half], out.at[:, 16 * half : 16 * half + 16], osem.at[half])
        for half in range(2)
    ]
    wait_recv(every[k] for k in (2, 4, 7, 9, 11, 13))
    top_mixed()
    top_rows()
    stores[0].start()
    wait_recv(every[k] for k in (1, 3, 6, 8, 10, 12))
    bottom_mixed()
    bottom_rows()
    stores[1].start()
    for store in stores:
        store.wait()
    wait_send(fcopies + every)


def on_device(
    nr, nc, features, gain_one, qkv_weight, bias_table, proj_weight, gain_two,
    hidden_weight, output_weight, group_conv, before_conv, upsample_conv,
):
    selector = jnp.asarray(table_selector(), BF16)
    operands = (
        features, gain_one, qkv_weight, bias_table.T, proj_weight, gain_two, hidden_weight,
        output_weight.T, group_conv, before_conv.transpose(0, 1, 3, 2),
        upsample_conv.reshape(3, 192, 256), selector,
    )
    any_space = pl.BlockSpec(memory_space=pl.ANY)
    staged = [pltpu.VMEM(x.shape, x.dtype) for x in operands]
    staged[10] = pltpu.VMEM((3, 256, 256), BF16)
    scratch = staged + [
        pltpu.VMEM((2, 192, 128), BF16), pltpu.VMEM((2, 192, 128), BF16),
        pltpu.VMEM((192, 128), BF16), pltpu.VMEM((192, 128), BF16), pltpu.VMEM((4, 48, 128), BF16),
        pltpu.VMEM((2, 192, 128), BF16), pltpu.VMEM((2, 192, 128), BF16),
        pltpu.VMEM((192, 128), BF16), pltpu.VMEM((192, 128), BF16), pltpu.VMEM((4, 48, 128), BF16),
        pltpu.VMEM((3, TW, 256), BF16), pltpu.VMEM((3, TW, 256), BF16),
        pltpu.VMEM((192, 128), BF16), pltpu.VMEM((192, 128), BF16), pltpu.VMEM((4, 48, 128), BF16),
        pltpu.VMEM((192, 128), BF16), pltpu.VMEM((192, 128), BF16), pltpu.VMEM((4, 48, 128), BF16),
        pltpu.VMEM((TH, TW, 256), BF16),
        pltpu.VMEM((2, 24 * PITCH, 128), F32), pltpu.VMEM((2, 24 * PITCH, 128), F32),
        pltpu.VMEM((2, 22 * PITCH, 128), F32), pltpu.VMEM((2, 20 * GP, 128), F32),
        pltpu.VMEM((2, 18 * GP + 8, 128), F32), pltpu.VMEM((18 * GP + 8, 128), F32),
        pltpu.VMEM((18, TW, 256), BF16),
        pltpu.VMEM((256, 640), BF16), pltpu.VMEM((256, 256), BF16), pltpu.VMEM((256, 256), BF16),
        pltpu.VMEM((192, 256), BF16), pltpu.VMEM((256, 256), BF16), pltpu.VMEM((256, 256), BF16),
        pltpu.VMEM((256, 384), BF16), pltpu.VMEM((256, 384), BF16), pltpu.VMEM((384, 256), BF16),
        pltpu.VMEM((9, 256, 256), BF16), pltpu.VMEM((3, 256, 256), BF16),
        pltpu.VMEM((3, 256, 256), BF16), pltpu.VMEM((3, 256, 256), BF16),
        pltpu.VMEM((HEADS, KWIN * KWIN, 256), F32), pltpu.VMEM((KWIN * KWIN, 256), BF16),
        pltpu.VMEM((4, KWIN * KWIN, 256), BF16), pltpu.VMEM((4, 192, KWIN * KWIN), BF16),
        pltpu.VMEM((4, 256, 256), F32), pltpu.VMEM((2, KWIN * KWIN, 256), F32),
        pltpu.VMEM((2, KWIN * KWIN, 256), BF16), pltpu.VMEM((4, 192, 256), BF16),
        pltpu.VMEM((256, 256), F32), pltpu.VMEM((256, 256), BF16), pltpu.VMEM((256, 384), BF16),
        pltpu.VMEM((2, 64 * 16, 128), F32), pltpu.VMEM((2, 64, 16, 128), BF16),
        pltpu.SemaphoreType.DMA((2,)),
        pltpu.SemaphoreType.DMA((12,)), pltpu.SemaphoreType.DMA((10,)), pltpu.SemaphoreType.DMA((10,)),
        pltpu.SemaphoreType.DMA((14,)), pltpu.SemaphoreType.DMA((14,)),
    ]
    result = pl.pallas_call(
        functools.partial(kernel, nr, nc),
        out_shape=jax.ShapeDtypeStruct((64, 2 * TH, 2 * TW), BF16),
        in_specs=[any_space] * len(operands),
        out_specs=pl.BlockSpec(memory_space=pl.ANY),
        scratch_shapes=scratch,
        compiler_params=pltpu.CompilerParams(
            collective_id=0, has_side_effects=True, vmem_limit_bytes=62 * 1024 * 1024
        ),
    )(*operands)
    return result


def solution(mesh):
    placed = (P("rows", "cols", None),) + (P(),) * 10
    body = functools.partial(on_device, mesh.shape["rows"], mesh.shape["cols"])
    return jax.shard_map(
        body, mesh=mesh, in_specs=placed, out_specs=P(None, "rows", "cols"), check_vma=False
    )
```

```python
import functools
import math

import jax
import jax.numpy as jnp
import numpy as np
from jax import lax
from jax.experimental import pallas as pl
from jax.experimental.pallas import tpu as pltpu
from jax.sharding import PartitionSpec as P

HEADS = 6
HEAD = 30
SLOT = 32
CH = 180
WIN = 16
KWIN = 24
SIDE = WIN + KWIN - 1
TABLE = SIDE * SIDE
TH = 16
TW = 64
PITCH = 80
GP = 72
QSCALE = math.log2(math.e) / math.sqrt(HEAD)
LOG2E = math.log2(math.e)
F32 = jnp.float32
BF16 = jnp.bfloat16
MESH = pl.DeviceIdType.MESH
NT = (((1,), (1,)), ((), ()))


def table_selector():
    out = np.zeros((384, 384), np.float32)
    for lane in range(128):
        for part in range(3):
            entry = 16 * part + lane % 16
            if entry < SIDE:
                out[SIDE * (7 - lane // 16) + SIDE - 1 - entry, 128 * part + lane] = 1.0
    return out


def mm(a, b):
    return jnp.dot(a, b, preferred_element_type=F32)


def mm_nt(a, b):
    return lax.dot_general(a, b, NT, preferred_element_type=F32)


def iota(shape, dim):
    return lax.broadcasted_iota(jnp.int32, shape, dim)


def one_hot(mask):
    return jnp.where(mask, 1.0, 0.0).astype(BF16)


def normalize(x, gain):
    lane = iota(x[1].shape, 1)
    mean = jnp.sum(x[0] + x[1], axis=-1, keepdims=True) * (1.0 / CH)
    low = x[0] - mean
    high = jnp.where(lane < CH - 128, x[1] - mean, 0.0)
    spread = jnp.sum(low * low + high * high, axis=-1, keepdims=True) * (1.0 / CH)
    scale = lax.rsqrt(spread + 1e-05)
    return low * scale * gain[:, 0:128], high * scale * gain[:, 128:256]


def pack_pixels(low, high):
    half = low.shape[0] // 2
    lane = iota((half, 128), 1)
    joined = jnp.where(lane < 64, high[:half], pltpu.roll(high[half:], 64, 1))
    return jnp.concatenate([low, joined], axis=0).astype(BF16)


def unpack_pixels(packed, valid):
    count = packed.shape[0] * 2 // 3
    x = jnp.where(valid, packed.astype(F32), 0.0)
    joined = x[count:]
    high = jnp.concatenate([joined, pltpu.roll(joined, 64, 1)], axis=0)
    return x[:count], jnp.where(iota(high.shape, 1) < CH - 128, high, 0.0)


def kernel(
    nr, nc,
    feat, gain1, qkv, table, proj, gain2, hid, outw, gconv, bconv, uconv, selector,
    out,
    feat_v, gain1_v, qkv_v, table_v, proj_v, gain2_v, hid_v, outw_v, gconv_v, bconv_v, upad, sel_v,
    send_t, send_b, send_l, send_r, send_c, halo_t, halo_b, halo_l, halo_r, halo_c,
    mix_t, mix_b, mix_l, mix_r, mix_c, mix_sl, mix_sr, mix_sc, mix_own,
    fpad, npad, mixpad, gbuf, ybuf, lbuf, l3,
    qpad, wqt, wk, wvt, ppad, pw, hpad, opad, wout, gpad, bpad, w2, w3, bias, xwin, kwin, vwin, qwin, sbuf, pbuf, attt, fbuf, second, inner, obuf, ostage, osem,
    local_sem, fsend, frecv, msend, mrecv,
):
    row = lax.axis_index("rows")
    col = lax.axis_index("cols")
    up = lax.rem(row + nr - 1, nr)
    down = lax.rem(row + 1, nr)
    left = lax.rem(col + nc - 1, nc)
    right = lax.rem(col + 1, nc)
    has_up = row > 0
    has_down = row < nr - 1
    has_left = col > 0
    has_right = col < nc - 1
    place = {
        "u": ((up, col), has_up), "d": ((down, col), has_down),
        "l": ((row, left), has_left), "r": ((row, right), has_right),
        "ul": ((up, left), has_up & has_left), "ur": ((up, right), has_up & has_right),
        "dl": ((down, left), has_down & has_left), "dr": ((down, right), has_down & has_right),
    }
    opposite = {"u": "d", "d": "u", "l": "r", "r": "l", "ul": "dr", "dr": "ul", "ur": "dl", "dl": "ur"}
    barrier = pltpu.get_barrier_semaphore()
    expected = 0
    for device, exists in place.values():
        expected = expected + jnp.where(exists, 1, 0)

        @pl.when(exists)
        def _(device=device):
            pl.semaphore_signal(barrier, inc=1, device_id=device, device_id_type=MESH)

    local = {}
    pairs = [
        ("feat", feat, feat_v), ("gain1", gain1, gain1_v), ("table", table, table_v),
        ("selector", selector, sel_v), ("qkv", qkv, qkv_v), ("proj", proj, proj_v),
        ("gain2", gain2, gain2_v), ("hid", hid, hid_v), ("outw", outw, outw_v),
        ("gconv", gconv, gconv_v), ("bconv", bconv, bconv_v), ("uconv", uconv, upad.at[:, 0:192, :]),
    ]
    for number, (name, source, target) in enumerate(pairs):
        local[name] = pltpu.make_async_copy(source, target, local_sem.at[number])
    for name in ("feat", "gain1", "table", "selector"):
        local[name].start()

    def arrive(*names):
        for name in names:
            local[name].wait()

    def exchange(specs, send_sem, recv_sem):
        copies = []
        for number, (source, target, way) in enumerate(specs):
            copy = pltpu.make_async_remote_copy(
                src_ref=source, dst_ref=target, send_sem=send_sem.at[number],
                recv_sem=recv_sem.at[number], device_id=place[way][0], device_id_type=MESH,
            )
            copies.append((copy, place[way][1], place[opposite[way]][1]))
        return copies

    def start(copies):
        for copy, sends, _ in copies:
            pl.when(sends)(copy.start)

    def wait_recv(copies):
        for copy, _, receives in copies:
            pl.when(receives)(copy.wait_recv)

    def wait_send(copies):
        for copy, sends, _ in copies:
            pl.when(sends)(copy.wait_send)

    fcopies = exchange(
        [
            (send_c.at[3], halo_c.at[0], "dr"),
            (send_c.at[1], halo_c.at[2], "ur"),
            (send_t.at[0], halo_b.at[0], "u"),
            (send_b.at[0], halo_t.at[0], "d"),
            (send_r, halo_l, "r"),
            (send_c.at[0], halo_c.at[3], "ul"),
            (send_c.at[2], halo_c.at[1], "dl"),
            (send_l, halo_r, "l"),
            (send_t.at[1], halo_b.at[1], "u"),
            (send_b.at[1], halo_t.at[1], "d"),
        ],
        fsend, frecv,
    )

    fpad[1] = jnp.zeros(fpad.shape[1:], F32)
    arrive("feat", "gain1")
    for h in range(0, TH, 4):
        x = feat_v[h : h + 4].astype(F32).reshape(4 * TW, CH)
        for k in range(4):
            rows = pl.ds((h + k + 4) * PITCH + 8, TW)
            fpad[0, rows, :] = x[k * TW : (k + 1) * TW, 0:128]
            fpad[1, rows, 0 : CH - 128] = x[k * TW : (k + 1) * TW, 128:CH]

    def region(ref, first_row, count_rows, first_col, count_cols):
        return [
            jnp.concatenate(
                [
                    ref[half, pl.ds((first_row + k) * PITCH + first_col, count_cols), :]
                    for k in range(count_rows)
                ],
                axis=0,
            )
            for half in range(2)
        ]

    corner_place = ((4, 8), (4, 64), (16, 8), (16, 64))
    pl.semaphore_wait(barrier, expected)
    for part, corners in ((0, (3, 1)), (1, (0, 2))):
        for corner in corners:
            first_row, first_col = corner_place[corner]
            send_c[corner] = pack_pixels(*region(fpad, first_row, 4, first_col, 8))
        send_t[part] = pack_pixels(*region(fpad, 4, 4, 8 + 32 * part, 32))
        send_b[part] = pack_pixels(*region(fpad, 16, 4, 8 + 32 * part, 32))
        if part == 0:
            send_r[...] = pack_pixels(*region(fpad, 4, TH, 64, 8))
        else:
            send_l[...] = pack_pixels(*region(fpad, 4, TH, 8, 8))
        start(fcopies[5 * part : 5 * part + 5])
    for name in ("qkv", "proj", "gain2", "hid", "outw", "gconv", "bconv", "uconv"):
        local[name].start()

    def lanes256(ref):
        return jnp.concatenate([ref[...].reshape(1, CH), jnp.zeros((1, 256 - CH), F32)], axis=1)

    g1 = lanes256(gain1_v)

    def store_normed(x, starts):
        n = normalize(x, g1)
        width = x[0].shape[0] // len(starts)
        for k, start in enumerate(starts):
            for half in range(2):
                npad[half, pl.ds(start, width), :] = n[half][k * width : (k + 1) * width]

    def own_pixels():
        for h in range(0, TH, 4):
            store_normed(
                region(fpad, h + 4, 4, 8, TW), [(h + k + 4) * PITCH + 8 for k in range(4)]
            )

    own_pixels()
    for ref in (qpad, ppad, hpad, opad, gpad, bpad):
        ref[...] = jnp.zeros(ref.shape, ref.dtype)
    for a in range(3):
        upad[a, 192:256, :] = jnp.zeros((64, 256), BF16)

    r = iota((256, 256), 0)
    c = iota((256, 256), 1)
    identity = one_hot(r == c)

    def prepare_bias():
        whole = jnp.concatenate(
            [table_v[...] * LOG2E, jnp.zeros((HEADS, 1536 - TABLE), F32)], axis=1
        )
        whole = jnp.concatenate([whole, jnp.zeros((2, 1536), F32)], axis=0)
        lane8 = iota((8, 128), 1)
        sub8 = iota((8, 128), 0)
        pieces = []
        for tile in range(5):
            first = SIDE * (SIDE - 8 - 8 * tile)
            pieces.append(pltpu.roll(whole, (1536 - first) % 1536, 1)[:, 0:384])
        rows = jnp.concatenate(pieces, axis=0)
        hi = rows.astype(BF16)
        rest = rows - hi.astype(F32)
        mid = rest.astype(BF16)
        low = (rest - mid.astype(F32)).astype(BF16)
        picked = mm(hi, sel_v[...]) + mm(mid, sel_v[...]) + mm(low, sel_v[...])
        lane24 = iota((KWIN, 128), 1)
        for head in range(HEADS):
            tiles = []
            for tile in range(5):
                z = picked[8 * tile + head : 8 * tile + head + 1, :]
                blocks = []
                for part, base in ((1, 7), (0, 15), (0, 7)):
                    first = jnp.broadcast_to(z[:, 128 * part : 128 * part + 128], (8, 128))
                    second = jnp.broadcast_to(z[:, 128 * part + 128 : 128 * part + 256], (8, 128))
                    first = pltpu.roll(first, 128 - base, 1, stride=1, stride_axis=0)
                    second = pltpu.roll(second, 16 - base, 1, stride=1, stride_axis=0)
                    blocks.append(jnp.where((lane8 & 15) + base - sub8 < 16, first, second))
                tiles.append(jnp.concatenate(blocks, axis=0))
            for shift in range(8):
                amount = 16 * shift
                if shift:
                    rolled = [pltpu.roll(t, 128 - amount, 1) for t in tiles]
                    joined = [
                        jnp.where(lane24 < 128 - amount, rolled[k], rolled[k + 1]) for k in range(4)
                    ]
                else:
                    joined = tiles
                for block in range(3):
                    p = KWIN - 1 - 8 * block - shift
                    for half in range(2):
                        bias[head, KWIN * p : KWIN * (p + 1), 128 * half : 128 * half + 128] = (
                            joined[block + half]
                        )

    arrive("table", "selector")
    prepare_bias()

    def prepare_weights():
        qpad[0:CH, 0 : 3 * CH] = qkv_v[...]
        wqt[...] = mm_nt(one_hot((r == c) & (r < CH)), qpad[:, 0:256]).astype(BF16)
        wk[...] = mm(qpad[:, 128:384], one_hot((r == c + 52) & (c < CH))).astype(BF16)
        rv = iota((192, 384), 0)
        cv = iota((192, 384), 1)
        slot_source = HEAD * lax.shift_right_logical(rv, 5) + (rv & 31)
        wvt[...] = mm_nt(one_hot((cv == slot_source + 104) & ((rv & 31) < HEAD)), qpad[:, 256:640]).astype(BF16)
        ppad[0:CH, 0:CH] = proj_v[...]
        slot_source = HEAD * lax.shift_right_logical(r, 5) + (r & 31)
        pw[...] = mm(one_hot((c == slot_source) & ((r & 31) < HEAD) & (r < 192)), ppad[...]).astype(BF16)
        hpad[0:CH, 0 : 2 * CH] = hid_v[...]
        opad[0:CH, 0 : 2 * CH] = outw_v[...]
        wout[...] = mm_nt(one_hot(iota((384, 384), 0) == iota((384, 384), 1)), opad[...]).astype(BF16)
        for tap in range(9):
            gpad[tap, 0:CH, 0:CH] = gconv_v[tap // 3, tap % 3]
        order = 4 * (r & 63) + 2 * (lax.shift_right_logical(r, 6) & 1) + lax.shift_right_logical(r, 7)
        shuffle_rows = one_hot(c == order)
        for a in range(3):
            for b in range(3):
                bpad[a, 64 * b : 64 * (b + 1), 0:CH] = bconv_v[a, b]
            w2[a] = mm_nt(identity, bpad[a]).astype(BF16)
            w3[a] = mm_nt(shuffle_rows, upad[a]).astype(BF16)

    arrive("qkv", "proj", "gain2", "hid", "outw", "gconv", "bconv", "uconv")
    prepare_weights()
    def halo_pixels(part):
        side, rim, has_side = ((halo_l, 0, has_left), (halo_r, 72, has_right))[part]
        groups = [
            (halo_t[part], has_up, [h * PITCH + 8 + 32 * part for h in range(4)]),
            (halo_b[part], has_down, [(20 + h) * PITCH + 8 + 32 * part for h in range(4)]),
            (side[...], has_side, [(4 + h) * PITCH + rim for h in range(TH)]),
            (halo_c[part], has_up & has_side, [h * PITCH + rim for h in range(4)]),
            (halo_c[2 + part], has_down & has_side, [(20 + h) * PITCH + rim for h in range(4)]),
        ]
        for packed, valid, starts in groups:
            x = unpack_pixels(packed, valid)
            width = x[0].shape[0] // len(starts)
            for k, start in enumerate(starts):
                for half in range(2):
                    fpad[half, pl.ds(start, width), :] = x[half][k * width : (k + 1) * width]
            store_normed(x, starts)

    g2 = lanes256(gain2_v)
    inside = c < CH
    ones_row = (iota((192, KWIN * KWIN), 0) & 31) == HEAD
    tops = {}

    def pixels(ref, half, w, first_row, count_rows, first_col, count_cols):
        return jnp.concatenate(
            [
                ref[half, pl.ds((first_row + p) * PITCH + first_col + w * WIN, count_cols), :]
                for p in range(count_rows)
            ],
            axis=0,
        )

    def project_keys(w, spans):
        for first, count in spans:
            keys_in = jnp.concatenate(
                [pixels(npad, half, w, first, count, 4, KWIN).astype(BF16) for half in range(2)],
                axis=1,
            )
            rows = slice(KWIN * first, KWIN * (first + count))
            xwin[w, rows, :] = keys_in
            kwin[w, rows, :] = mm(keys_in, wk[...]).astype(BF16)

    def project_values(w):
        vwin[w] = jnp.where(ones_row, 1.0, mm_nt(wvt[...], xwin[w])).astype(BF16)

    def project_queries(w):
        query_in = jnp.concatenate(
            [pixels(npad, half, w, 4, WIN, 8, WIN).astype(BF16) for half in range(2)], axis=1
        )
        qwin[w] = mm_nt(wqt[...], query_in) * QSCALE

    whole_keys = ((0, 288), (288, 576))
    own_keys = ((96, 288), (288, 480))
    halo_keys = ((0, 96), (480, 576))
    inner_from = 2 * HEADS

    def slot(number):
        return number % 2 if number < inner_from else 2 + number - inner_from

    def score(number, w, head, spans):
        mine = (r >= HEAD * head) & (r < HEAD * (head + 1))
        q = jnp.where(mine, qwin[w], 0.0).astype(BF16)
        top = tops.get(number)
        for first, last in spans:
            scores = mm(kwin[w, first:last, :], q) + bias[head, first:last, :]
            sbuf[slot(number), first:last, :] = scores
            best = jnp.max(scores, axis=0, keepdims=True)
            top = best if top is None else jnp.maximum(top, best)
        tops[number] = top

    def exponent(number):
        pbuf[number % 2] = jnp.exp2(sbuf[slot(number)] - tops[number]).astype(BF16)

    def combine(number, w, head):
        rows = slice(SLOT * head, SLOT * (head + 1))
        mixed_values = mm(vwin[w, rows, :], pbuf[number % 2])
        attt[w, rows, :] = (mixed_values / mixed_values[HEAD : HEAD + 1, :]).astype(BF16)

    def merge_heads(w):
        attended = mm_nt(identity, attt[w]).astype(BF16)
        base = jnp.concatenate([pixels(fpad, half, w, 4, WIN, 8, WIN) for half in range(2)], axis=1)
        first = base + mm(attended, pw[0:192, :])
        fbuf[...] = first
        center = first - jnp.sum(first, axis=-1, keepdims=True) * (1.0 / CH)
        center = jnp.where(inside, center, 0.0)
        spread = jnp.sum(center * center, axis=-1, keepdims=True) * (1.0 / CH)
        second[...] = (center * lax.rsqrt(spread + 1e-05) * g2).astype(BF16)

    def hidden(part):
        lanes = slice(128 * part, 128 * part + 128)
        value = mm(second[...], hpad[:, lanes])
        inner[:, lanes] = (0.5 * value * (1.0 + lax.erf(value * math.sqrt(0.5)))).astype(BF16)

    def finish_window(w):
        mixed = fbuf[...] + mm(inner[...], wout[...])
        for i in range(WIN):
            block = mixed[WIN * i : WIN * (i + 1), :]
            rows = pl.ds((3 + i) * PITCH + 8 + w * WIN, WIN)
            mixpad[0, rows, :] = block[:, 0:128]
            mixpad[1, rows, :] = block[:, 128:256]
            mix_own[i, w * WIN : (w + 1) * WIN, :] = block.astype(BF16)
        if w == 0:
            mix_sl[...] = pack_pixels(*region(mixpad, 3, TH, 8, 8))
            mix_sc[0] = pack_pixels(*region(mixpad, 3, 4, 8, 8))
            mix_sc[2] = pack_pixels(*region(mixpad, 15, 4, 8, 8))
        if w == 3:
            mix_sr[...] = pack_pixels(*region(mixpad, 3, TH, 64, 8))
            mix_sc[1] = pack_pixels(*region(mixpad, 3, 4, 64, 8))
            mix_sc[3] = pack_pixels(*region(mixpad, 15, 4, 64, 8))
        start(mcopies[w])

    def strip(w):
        cols = slice(w * WIN, (w + 1) * WIN)
        return [
            (mix_own.at[0:3, cols], mix_b.at[:, cols], "u"),
            (mix_own.at[13:16, cols], mix_t.at[:, cols], "d"),
        ]

    specs = {
        0: [
            (mix_sl, mix_r, "l"),
            (mix_sc.at[0], mix_c.at[3], "ul"),
            (mix_sc.at[2], mix_c.at[1], "dl"),
        ] + strip(0),
        3: [
            (mix_sr, mix_l, "r"),
            (mix_sc.at[1], mix_c.at[2], "ur"),
            (mix_sc.at[3], mix_c.at[0], "dr"),
        ] + strip(3),
        1: strip(1),
        2: strip(2),
    }
    windows = (0, 3, 1, 2)
    every = exchange([item for w in windows for item in specs[w]], msend, mrecv)
    mcopies = {0: every[0:5], 3: every[5:10], 1: every[10:12], 2: every[12:14]}
    steps = [(w, head) for w in windows for head in range(HEADS)]

    def first_half():
        halo_pixels(0)
        project_keys(0, ((0, KWIN),))
        project_values(0)
        attend(0, 3)

    def second_half():
        halo_pixels(1)
        attend(3, len(steps) + 2)
        merge_heads(windows[-1])
        for part in range(3):
            hidden(part)
        finish_window(windows[-1])

    def attend(begin, end):
        for number in range(begin, end):
            turn, head = divmod(number, HEADS)
            if number < len(steps):
                inner_window = number >= inner_from
                score(number, windows[turn], head, halo_keys if inner_window else whole_keys)
            if 0 <= number - 1 < len(steps):
                exponent(number - 1)
            if 0 <= number - 2:
                combine(number - 2, *steps[number - 2])
            if turn + 1 < len(windows) and head == 3:
                project_keys(windows[turn + 1], ((0, 4), (20, 4)) if turn else ((0, KWIN),))
            if turn + 1 < len(windows) and head == 4:
                project_values(windows[turn + 1])
            if 0 < turn < len(windows):
                if head == 1:
                    merge_heads(windows[turn - 1])
                elif 2 <= head <= 4:
                    hidden(head - 2)
                elif head == 5:
                    finish_window(windows[turn - 1])

    def all_queries():
        for w in windows:
            project_queries(w)

    def own_scores():
        for w in windows[2:]:
            project_keys(w, ((4, TH),))
        for number in range(inner_from, len(steps)):
            score(number, *steps[number], own_keys)

    all_queries()
    own_scores()
    wait_recv(fcopies[k] for k in (0, 1, 2, 3, 4))
    first_half()
    wait_recv(fcopies[k] for k in (5, 6, 7, 8, 9))
    second_half()

    def store_mixed(start, count, values, valid):
        x = jnp.where(valid, values, 0.0)
        rows = pl.ds(start, count)
        mixpad[0, rows, :] = x[:, 0:128]
        mixpad[1, rows, :] = x[:, 128:256]

    def store_packed(packed, valid, starts, skip=0):
        x = unpack_pixels(packed, valid)
        for k, start in enumerate(starts):
            part = slice((k + skip) * 8, (k + skip + 1) * 8)
            for half in range(2):
                mixpad[half, pl.ds(start, 8), :] = x[half][part]

    def side_mixed():
        store_packed(mix_l[...], has_left, [(3 + h) * PITCH for h in range(TH)])
        store_packed(mix_r[...], has_right, [(3 + h) * PITCH + 72 for h in range(TH)])

    def top_mixed():
        for h in range(3):
            store_mixed(h * PITCH + 8, TW, mix_t[h].astype(F32), has_up)
        store_packed(mix_c[0], has_up & has_left, [h * PITCH for h in range(3)], 1)
        store_packed(mix_c[1], has_up & has_right, [h * PITCH + 72 for h in range(3)], 1)

    def bottom_mixed():
        for h in range(3):
            store_mixed((19 + h) * PITCH + 8, TW, mix_b[h].astype(F32), has_down)
        store_packed(mix_c[2], has_down & has_left, [(19 + h) * PITCH for h in range(3)])
        store_packed(mix_c[3], has_down & has_right, [(19 + h) * PITCH + 72 for h in range(3)])

    cols72 = iota((GP, 128), 0)
    gcols = ((cols72 >= 2) | has_left) & ((cols72 < 66) | has_right)
    lcols = ((cols72 >= 1) | has_left) & ((cols72 < 65) | has_right)

    def conv_group(h0, count):
        acc = None
        for a in range(3):
            for b in range(3):
                halves = []
                for half in range(2):
                    rows = [
                        mixpad[half, pl.ds((h0 + k + a) * PITCH + 5 + b, GP), :] for k in range(count)
                    ]
                    halves.append(jnp.concatenate(rows, axis=0).astype(BF16))
                term = mm(jnp.concatenate(halves, axis=1), gpad[3 * a + b])
                acc = term if acc is None else acc + term
        for k in range(count):
            h = h0 + k
            keep = gcols & has_up if h < 2 else gcols & has_down if h >= 18 else gcols
            for half in range(2):
                base = fpad[half, pl.ds((h + 2) * PITCH + 6, GP), :]
                value = base + acc[GP * k : GP * (k + 1), 128 * half : 128 * half + 128]
                gbuf[half, pl.ds(h * GP, GP), :] = jnp.where(keep, value, 0.0)

    low_lanes = iota((GP, 128), 1) < 64
    low64 = iota((TW, 128), 1) < 64

    def conv_before(first, count):
        start = first * GP
        acc = None
        for a in range(3):
            rows = pl.ds(start + a * GP, count * GP)
            lhs = jnp.concatenate([gbuf[half, rows, :].astype(BF16) for half in range(2)], axis=1)
            term = mm(lhs, w2[a])
            acc = term if acc is None else acc + term
        rows = pl.ds(start, count * GP)
        ybuf[0, rows, :] = acc[:, 0:128]
        ybuf[1, rows, :] = acc[:, 128:256]
        for h in range(first, first + count):
            start = h * GP
            value = (
                ybuf[0, pl.ds(start, GP), :]
                + pltpu.roll(ybuf[0, pl.ds(start + 1, GP), :], 64, 1)
                + ybuf[1, pl.ds(start + 2, GP), :]
            )
            value = jnp.where(value >= 0, value, 0.01 * value)
            keep = lcols & has_up if h < 1 else lcols & has_down if h >= 17 else lcols
            value = jnp.where(keep, value, 0.0)
            lbuf[pl.ds(start, GP), :] = jnp.where(low_lanes, value, pltpu.roll(value, 64, 1))
        for h in range(first, first + count):
            start = h * GP
            zero = lbuf[pl.ds(start, TW), :]
            one = lbuf[pl.ds(start + 1, TW), :]
            two = lbuf[pl.ds(start + 2, TW), :]
            l3[h, :, 0:128] = jnp.where(low64, zero, one).astype(BF16)
            l3[h, :, 128:256] = jnp.where(low64, two, 0.0).astype(BF16)

    target = 128 * (lax.shift_right_logical(r, 6) & 1) + 2 * (r & 63) + lax.shift_right_logical(r, 7)
    weave = one_hot(c == target)

    def conv_up(step):
        acc = None
        for a in range(3):
            rhs = jnp.concatenate([l3[4 * step + a + k] for k in range(4)], axis=0)
            term = mm_nt(w3[a], rhs)
            acc = term if acc is None else acc + term
        acc = acc.astype(BF16)
        for pair in range(2):
            lanes = slice(128 * pair, 128 * pair + 128)
            both = jnp.concatenate([acc[0:128, lanes], acc[128:256, lanes]], axis=1)
            woven = mm(both, weave)
            for k in range(2):
                for a in range(2):
                    line = (2 * (4 * step + 2 * pair + k) + a) % 16
                    obuf[step // 2, pl.ds(line, 64, stride=16), :] = woven[
                        64 * a : 64 * (a + 1), 128 * k : 128 * k + 128
                    ]

    def inner_rows():
        for h0 in range(3, 17, 2):
            conv_group(h0, 2)
        conv_before(3, 6)
        conv_before(9, 6)
        conv_up(1)
        conv_up(2)

    def out_half(half):
        ostage[half] = obuf[half].reshape(64, 16, 128).astype(BF16)

    def end_rows():
        conv_group(0, 2)
        conv_group(17, 2)
        conv_group(2, 1)
        conv_group(19, 1)
        conv_before(0, 3)
        conv_before(15, 3)
        conv_up(0)
        conv_up(3)
        out_half(0)

    ybuf[:, 18 * GP :, :] = jnp.zeros((2, 8, 128), F32)
    wait_recv(every[k] for k in (0, 5))
    side_mixed()
    inner_rows()
    stores = [
        pltpu.make_async_copy(ostage.at[half], out.at[:, 16 * half : 16 * half + 16], osem.at[half])
        for half in range(2)
    ]
    wait_recv(every[k] for k in (1, 2, 3, 4, 6, 7, 8, 9, 10, 11, 12, 13))
    top_mixed()
    bottom_mixed()
    end_rows()
    stores[0].start()
    out_half(1)
    stores[1].start()
    for store in stores:
        store.wait()
    wait_send(fcopies + every)


def on_device(
    nr, nc, features, gain_one, qkv_weight, bias_table, proj_weight, gain_two,
    hidden_weight, output_weight, group_conv, before_conv, upsample_conv,
):
    selector = jnp.asarray(table_selector(), BF16)
    operands = (
        features, gain_one, qkv_weight, bias_table.T, proj_weight, gain_two, hidden_weight,
        output_weight.T, group_conv, before_conv.transpose(0, 1, 3, 2),
        upsample_conv.reshape(3, 192, 256), selector,
    )
    any_space = pl.BlockSpec(memory_space=pl.ANY)
    staged = [pltpu.VMEM(x.shape, x.dtype) for x in operands]
    staged[10] = pltpu.VMEM((3, 256, 256), BF16)
    scratch = staged + [
        pltpu.VMEM((2, 192, 128), BF16), pltpu.VMEM((2, 192, 128), BF16),
        pltpu.VMEM((192, 128), BF16), pltpu.VMEM((192, 128), BF16), pltpu.VMEM((4, 48, 128), BF16),
        pltpu.VMEM((2, 192, 128), BF16), pltpu.VMEM((2, 192, 128), BF16),
        pltpu.VMEM((192, 128), BF16), pltpu.VMEM((192, 128), BF16), pltpu.VMEM((4, 48, 128), BF16),
        pltpu.VMEM((3, TW, 256), BF16), pltpu.VMEM((3, TW, 256), BF16),
        pltpu.VMEM((192, 128), BF16), pltpu.VMEM((192, 128), BF16), pltpu.VMEM((4, 48, 128), BF16),
        pltpu.VMEM((192, 128), BF16), pltpu.VMEM((192, 128), BF16), pltpu.VMEM((4, 48, 128), BF16),
        pltpu.VMEM((TH, TW, 256), BF16),
        pltpu.VMEM((2, 24 * PITCH, 128), F32), pltpu.VMEM((2, 24 * PITCH, 128), F32),
        pltpu.VMEM((2, 22 * PITCH, 128), F32), pltpu.VMEM((2, 20 * GP, 128), F32),
        pltpu.VMEM((2, 18 * GP + 8, 128), F32), pltpu.VMEM((18 * GP + 8, 128), F32),
        pltpu.VMEM((18, TW, 256), BF16),
        pltpu.VMEM((256, 640), BF16), pltpu.VMEM((256, 256), BF16), pltpu.VMEM((256, 256), BF16),
        pltpu.VMEM((192, 256), BF16), pltpu.VMEM((256, 256), BF16), pltpu.VMEM((256, 256), BF16),
        pltpu.VMEM((256, 384), BF16), pltpu.VMEM((256, 384), BF16), pltpu.VMEM((384, 256), BF16),
        pltpu.VMEM((9, 256, 256), BF16), pltpu.VMEM((3, 256, 256), BF16),
        pltpu.VMEM((3, 256, 256), BF16), pltpu.VMEM((3, 256, 256), BF16),
        pltpu.VMEM((HEADS, KWIN * KWIN, 256), F32), pltpu.VMEM((4, KWIN * KWIN, 256), BF16),
        pltpu.VMEM((4, KWIN * KWIN, 256), BF16), pltpu.VMEM((4, 192, KWIN * KWIN), BF16),
        pltpu.VMEM((4, 256, 256), F32), pltpu.VMEM((14, KWIN * KWIN, 256), F32),
        pltpu.VMEM((2, KWIN * KWIN, 256), BF16), pltpu.VMEM((4, 192, 256), BF16),
        pltpu.VMEM((256, 256), F32), pltpu.VMEM((256, 256), BF16), pltpu.VMEM((256, 384), BF16),
        pltpu.VMEM((2, 64 * 16, 128), F32), pltpu.VMEM((2, 64, 16, 128), BF16),
        pltpu.SemaphoreType.DMA((2,)),
        pltpu.SemaphoreType.DMA((12,)), pltpu.SemaphoreType.DMA((10,)), pltpu.SemaphoreType.DMA((10,)),
        pltpu.SemaphoreType.DMA((14,)), pltpu.SemaphoreType.DMA((14,)),
    ]
    result = pl.pallas_call(
        functools.partial(kernel, nr, nc),
        out_shape=jax.ShapeDtypeStruct((64, 2 * TH, 2 * TW), BF16),
        in_specs=[any_space] * len(operands),
        out_specs=pl.BlockSpec(memory_space=pl.ANY),
        scratch_shapes=scratch,
        compiler_params=pltpu.CompilerParams(
            collective_id=0, has_side_effects=True, vmem_limit_bytes=62 * 1024 * 1024
        ),
    )(*operands)
    return result


def solution(mesh):
    placed = (P("rows", "cols", None),) + (P(),) * 10
    body = functools.partial(on_device, mesh.shape["rows"], mesh.shape["cols"])
    return jax.shard_map(
        body, mesh=mesh, in_specs=placed, out_specs=P(None, "rows", "cols"), check_vma=False
    )
```

```python
import functools
import math

import jax
import jax.numpy as jnp
import numpy as np
from jax import lax
from jax.experimental import pallas as pl
from jax.experimental.pallas import tpu as pltpu
from jax.sharding import PartitionSpec as P

HEADS = 6
HEAD = 30
SLOT = 32
CH = 180
WIN = 16
KWIN = 24
SIDE = WIN + KWIN - 1
TABLE = SIDE * SIDE
TH = 16
TW = 64
PITCH = 80
GP = 72
QSCALE = math.log2(math.e) / math.sqrt(HEAD)
LOG2E = math.log2(math.e)
F32 = jnp.float32
BF16 = jnp.bfloat16
MESH = pl.DeviceIdType.MESH
NT = (((1,), (1,)), ((), ()))


def table_selector():
    out = np.zeros((384, 384), np.float32)
    for lane in range(128):
        for part in range(3):
            entry = 16 * part + lane % 16
            if entry < SIDE:
                out[SIDE * (7 - lane // 16) + SIDE - 1 - entry, 128 * part + lane] = 1.0
    return out


def mm(a, b):
    return jnp.dot(a, b, preferred_element_type=F32)


def mm_nt(a, b):
    return lax.dot_general(a, b, NT, preferred_element_type=F32)


def iota(shape, dim):
    return lax.broadcasted_iota(jnp.int32, shape, dim)


def one_hot(mask):
    return jnp.where(mask, 1.0, 0.0).astype(BF16)


def normalize(x, gain):
    lane = iota(x[1].shape, 1)
    mean = jnp.sum(x[0] + x[1], axis=-1, keepdims=True) * (1.0 / CH)
    low = x[0] - mean
    high = jnp.where(lane < CH - 128, x[1] - mean, 0.0)
    spread = jnp.sum(low * low + high * high, axis=-1, keepdims=True) * (1.0 / CH)
    scale = lax.rsqrt(spread + 1e-05)
    return low * scale * gain[:, 0:128], high * scale * gain[:, 128:256]


def pack_pixels(low, high):
    half = low.shape[0] // 2
    lane = iota((half, 128), 1)
    joined = jnp.where(lane < 64, high[:half], pltpu.roll(high[half:], 64, 1))
    return jnp.concatenate([low, joined], axis=0).astype(BF16)


def unpack_pixels(packed, valid):
    count = packed.shape[0] * 2 // 3
    x = jnp.where(valid, packed.astype(F32), 0.0)
    joined = x[count:]
    high = jnp.concatenate([joined, pltpu.roll(joined, 64, 1)], axis=0)
    return x[:count], jnp.where(iota(high.shape, 1) < CH - 128, high, 0.0)


def kernel(
    nr, nc,
    feat, gain1, qkv, table, proj, gain2, hid, outw, gconv, bconv, uconv, selector,
    out,
    feat_v, gain1_v, qkv_v, table_v, proj_v, gain2_v, hid_v, outw_v, gconv_v, bconv_v, upad, sel_v,
    send_t, send_b, send_l, send_r, send_c, halo_t, halo_b, halo_l, halo_r, halo_c,
    mix_t, mix_b, mix_l, mix_r, mix_c, mix_sl, mix_sr, mix_sc, mix_own,
    fpad, npad, mixpad, gbuf, ybuf, lbuf, l3,
    qpad, wqt, wk, wvt, ppad, pw, hpad, opad, wout, gpad, bpad, w2, w3, bias, xwin, kwin, vwin, qwin, sbuf, pbuf, attt, fbuf, second, inner, obuf, ostage, osem,
    local_sem, fsend, frecv, msend, mrecv,
):
    row = lax.axis_index("rows")
    col = lax.axis_index("cols")
    up = lax.rem(row + nr - 1, nr)
    down = lax.rem(row + 1, nr)
    left = lax.rem(col + nc - 1, nc)
    right = lax.rem(col + 1, nc)
    has_up = row > 0
    has_down = row < nr - 1
    has_left = col > 0
    has_right = col < nc - 1
    place = {
        "u": ((up, col), has_up), "d": ((down, col), has_down),
        "l": ((row, left), has_left), "r": ((row, right), has_right),
        "ul": ((up, left), has_up & has_left), "ur": ((up, right), has_up & has_right),
        "dl": ((down, left), has_down & has_left), "dr": ((down, right), has_down & has_right),
    }
    opposite = {"u": "d", "d": "u", "l": "r", "r": "l", "ul": "dr", "dr": "ul", "ur": "dl", "dl": "ur"}
    barrier = pltpu.get_barrier_semaphore()
    expected = 0
    for device, exists in place.values():
        expected = expected + jnp.where(exists, 1, 0)

        @pl.when(exists)
        def _(device=device):
            pl.semaphore_signal(barrier, inc=1, device_id=device, device_id_type=MESH)

    local = {}
    pairs = [
        ("feat", feat, feat_v), ("gain1", gain1, gain1_v), ("table", table, table_v),
        ("selector", selector, sel_v), ("qkv", qkv, qkv_v), ("proj", proj, proj_v),
        ("gain2", gain2, gain2_v), ("hid", hid, hid_v), ("outw", outw, outw_v),
        ("gconv", gconv, gconv_v), ("bconv", bconv, bconv_v), ("uconv", uconv, upad.at[:, 0:192, :]),
    ]
    for number, (name, source, target) in enumerate(pairs):
        local[name] = pltpu.make_async_copy(source, target, local_sem.at[number])
    for name in ("feat", "gain1", "table", "selector"):
        local[name].start()

    def arrive(*names):
        for name in names:
            local[name].wait()

    def exchange(specs, send_sem, recv_sem):
        copies = []
        for number, (source, target, way) in enumerate(specs):
            copy = pltpu.make_async_remote_copy(
                src_ref=source, dst_ref=target, send_sem=send_sem.at[number],
                recv_sem=recv_sem.at[number], device_id=place[way][0], device_id_type=MESH,
            )
            copies.append((copy, place[way][1], place[opposite[way]][1]))
        return copies

    def start(copies):
        for copy, sends, _ in copies:
            pl.when(sends)(copy.start)

    def wait_recv(copies):
        for copy, _, receives in copies:
            pl.when(receives)(copy.wait_recv)

    def wait_send(copies):
        for copy, sends, _ in copies:
            pl.when(sends)(copy.wait_send)

    fcopies = exchange(
        [
            (send_c.at[3], halo_c.at[0], "dr"),
            (send_c.at[1], halo_c.at[2], "ur"),
            (send_t.at[0], halo_b.at[0], "u"),
            (send_b.at[0], halo_t.at[0], "d"),
            (send_r, halo_l, "r"),
            (send_c.at[0], halo_c.at[3], "ul"),
            (send_c.at[2], halo_c.at[1], "dl"),
            (send_l, halo_r, "l"),
            (send_t.at[1], halo_b.at[1], "u"),
            (send_b.at[1], halo_t.at[1], "d"),
        ],
        fsend, frecv,
    )

    fpad[1] = jnp.zeros(fpad.shape[1:], F32)
    arrive("feat", "gain1")
    for h in range(0, TH, 4):
        x = feat_v[h : h + 4].astype(F32).reshape(4 * TW, CH)
        for k in range(4):
            rows = pl.ds((h + k + 4) * PITCH + 8, TW)
            fpad[0, rows, :] = x[k * TW : (k + 1) * TW, 0:128]
            fpad[1, rows, 0 : CH - 128] = x[k * TW : (k + 1) * TW, 128:CH]

    def region(ref, first_row, count_rows, first_col, count_cols):
        return [
            jnp.concatenate(
                [
                    ref[half, pl.ds((first_row + k) * PITCH + first_col, count_cols), :]
                    for k in range(count_rows)
                ],
                axis=0,
            )
            for half in range(2)
        ]

    corner_place = ((4, 8), (4, 64), (16, 8), (16, 64))
    pl.semaphore_wait(barrier, expected)
    for part, corners in ((0, (3, 1)), (1, (0, 2))):
        for corner in corners:
            first_row, first_col = corner_place[corner]
            send_c[corner] = pack_pixels(*region(fpad, first_row, 4, first_col, 8))
        send_t[part] = pack_pixels(*region(fpad, 4, 4, 8 + 32 * part, 32))
        send_b[part] = pack_pixels(*region(fpad, 16, 4, 8 + 32 * part, 32))
        if part == 0:
            send_r[...] = pack_pixels(*region(fpad, 4, TH, 64, 8))
        else:
            send_l[...] = pack_pixels(*region(fpad, 4, TH, 8, 8))
        start(fcopies[5 * part : 5 * part + 5])
    for name in ("qkv", "proj", "gain2", "hid", "outw", "gconv", "bconv", "uconv"):
        local[name].start()

    def lanes256(ref):
        return jnp.concatenate([ref[...].reshape(1, CH), jnp.zeros((1, 256 - CH), F32)], axis=1)

    g1 = lanes256(gain1_v)

    def store_normed(x, starts):
        n = normalize(x, g1)
        width = x[0].shape[0] // len(starts)
        for k, start in enumerate(starts):
            for half in range(2):
                npad[half, pl.ds(start, width), :] = n[half][k * width : (k + 1) * width]

    def own_pixels():
        for h in range(0, TH, 4):
            store_normed(
                region(fpad, h + 4, 4, 8, TW), [(h + k + 4) * PITCH + 8 for k in range(4)]
            )

    own_pixels()
    for ref in (qpad, ppad, hpad, opad):
        ref[...] = jnp.zeros(ref.shape, ref.dtype)

    r = iota((256, 256), 0)
    c = iota((256, 256), 1)
    identity = one_hot(r == c)

    def select_bias():
        whole = jnp.concatenate(
            [table_v[...] * LOG2E, jnp.zeros((HEADS, 1536 - TABLE), F32)], axis=1
        )
        whole = jnp.concatenate([whole, jnp.zeros((2, 1536), F32)], axis=0)
        pieces = []
        for tile in range(5):
            first = SIDE * (SIDE - 8 - 8 * tile)
            pieces.append(pltpu.roll(whole, (1536 - first) % 1536, 1)[:, 0:384])
        rows = jnp.concatenate(pieces, axis=0)
        hi = rows.astype(BF16)
        rest = rows - hi.astype(F32)
        mid = rest.astype(BF16)
        low = (rest - mid.astype(F32)).astype(BF16)
        picked = mm(hi, sel_v[...]) + mm(mid, sel_v[...]) + mm(low, sel_v[...])
        return picked

    lane8 = iota((8, 128), 1)
    sub8 = iota((8, 128), 0)
    lane24 = iota((KWIN, 128), 1)

    def head_bias(picked, head):
        tiles = []
        for tile in range(5):
            z = picked[8 * tile + head : 8 * tile + head + 1, :]
            blocks = []
            for part, base in ((1, 7), (0, 15), (0, 7)):
                first = jnp.broadcast_to(z[:, 128 * part : 128 * part + 128], (8, 128))
                second = jnp.broadcast_to(z[:, 128 * part + 128 : 128 * part + 256], (8, 128))
                first = pltpu.roll(first, 128 - base, 1, stride=1, stride_axis=0)
                second = pltpu.roll(second, 16 - base, 1, stride=1, stride_axis=0)
                blocks.append(jnp.where((lane8 & 15) + base - sub8 < 16, first, second))
            tiles.append(jnp.concatenate(blocks, axis=0))
        for shift in range(8):
            amount = 16 * shift
            if shift:
                rolled = [pltpu.roll(t, 128 - amount, 1) for t in tiles]
                joined = [
                    jnp.where(lane24 < 128 - amount, rolled[k], rolled[k + 1]) for k in range(4)
                ]
            else:
                joined = tiles
            for block in range(3):
                p = KWIN - 1 - 8 * block - shift
                for half in range(2):
                    bias[head, KWIN * p : KWIN * (p + 1), 128 * half : 128 * half + 128] = (
                        joined[block + half]
                    )

    def prepare_weights():
        qpad[0:CH, 0 : 3 * CH] = qkv_v[...]
        wqt[...] = mm_nt(one_hot((r == c) & (r < CH)), qpad[:, 0:256]).astype(BF16)
        wk[...] = mm(qpad[:, 128:384], one_hot((r == c + 52) & (c < CH))).astype(BF16)
        rv = iota((192, 384), 0)
        cv = iota((192, 384), 1)
        source = HEAD * lax.shift_right_logical(rv, 5) + (rv & 31)
        wvt[...] = mm_nt(one_hot((cv == source + 104) & ((rv & 31) < HEAD)), qpad[:, 256:640]).astype(BF16)

    def proj_weights():
        ppad[0:CH, 0:CH] = proj_v[...]
        source = HEAD * lax.shift_right_logical(r, 5) + (r & 31)
        pw[...] = mm(one_hot((c == source) & ((r & 31) < HEAD) & (r < 192)), ppad[...]).astype(BF16)
        hpad[0:CH, 0 : 2 * CH] = hid_v[...]

    def out_weights():
        opad[0:CH, 0 : 2 * CH] = outw_v[...]
        wout[...] = mm_nt(one_hot(iota((384, 384), 0) == iota((384, 384), 1)), opad[...]).astype(BF16)

    def conv_weights(a):
        for b in range(3):
            tap = 3 * a + b
            gpad[tap] = jnp.zeros((256, 256), BF16)
            gpad[tap, 0:CH, 0:CH] = gconv_v[a, b]
        bpad[a] = jnp.zeros((256, 256), BF16)
        upad[a, 192:256, :] = jnp.zeros((64, 256), BF16)
        order = 4 * (r & 63) + 2 * (lax.shift_right_logical(r, 6) & 1) + lax.shift_right_logical(r, 7)
        for b in range(3):
            bpad[a, 64 * b : 64 * (b + 1), 0:CH] = bconv_v[a, b]
        w2[a] = mm_nt(identity, bpad[a]).astype(BF16)
        w3[a] = mm_nt(one_hot(c == order), upad[a]).astype(BF16)

    late_weights = [
        proj_weights, out_weights, functools.partial(conv_weights, 0),
        functools.partial(conv_weights, 1), functools.partial(conv_weights, 2),
    ]
    arrive("qkv")
    prepare_weights()

    def halo_pixels(part):
        side, rim, has_side = ((halo_l, 0, has_left), (halo_r, 72, has_right))[part]
        groups = [
            (halo_t[part], has_up, [h * PITCH + 8 + 32 * part for h in range(4)]),
            (halo_b[part], has_down, [(20 + h) * PITCH + 8 + 32 * part for h in range(4)]),
            (side[...], has_side, [(4 + h) * PITCH + rim for h in range(TH)]),
            (halo_c[part], has_up & has_side, [h * PITCH + rim for h in range(4)]),
            (halo_c[2 + part], has_down & has_side, [(20 + h) * PITCH + rim for h in range(4)]),
        ]
        for packed, valid, starts in groups:
            x = unpack_pixels(packed, valid)
            width = x[0].shape[0] // len(starts)
            for k, start in enumerate(starts):
                for half in range(2):
                    fpad[half, pl.ds(start, width), :] = x[half][k * width : (k + 1) * width]
            store_normed(x, starts)

    inside = c < CH
    ones_row = (iota((192, KWIN * KWIN), 0) & 31) == HEAD
    tops = {}

    def pixels(ref, half, w, first_row, count_rows, first_col, count_cols):
        return jnp.concatenate(
            [
                ref[half, pl.ds((first_row + p) * PITCH + first_col + w * WIN, count_cols), :]
                for p in range(count_rows)
            ],
            axis=0,
        )

    def project_keys(w, spans):
        for first, count in spans:
            keys_in = jnp.concatenate(
                [pixels(npad, half, w, first, count, 4, KWIN).astype(BF16) for half in range(2)],
                axis=1,
            )
            rows = slice(KWIN * first, KWIN * (first + count))
            xwin[w, rows, :] = keys_in
            kwin[w, rows, :] = mm(keys_in, wk[...]).astype(BF16)

    def project_values(w):
        vwin[w] = jnp.where(ones_row, 1.0, mm_nt(wvt[...], xwin[w])).astype(BF16)

    def project_queries(w):
        query_in = jnp.concatenate(
            [pixels(npad, half, w, 4, WIN, 8, WIN).astype(BF16) for half in range(2)], axis=1
        )
        qwin[w] = mm_nt(wqt[...], query_in) * QSCALE

    whole_keys = ((0, 288), (288, 576))
    own_keys = ((96, 288), (288, 480))
    halo_keys = ((0, 96), (480, 576))
    inner_from = 2 * HEADS

    def slot(number):
        return number % 2 if number < inner_from else 2 + number - inner_from

    def score(number, w, head, spans):
        mine = (r >= HEAD * head) & (r < HEAD * (head + 1))
        q = jnp.where(mine, qwin[w], 0.0).astype(BF16)
        top = tops.get(number)
        for first, last in spans:
            scores = mm(kwin[w, first:last, :], q) + bias[head, first:last, :]
            sbuf[slot(number), first:last, :] = scores
            best = jnp.max(scores, axis=0, keepdims=True)
            top = best if top is None else jnp.maximum(top, best)
        tops[number] = top

    def exponent(number):
        pbuf[number % 2] = jnp.exp2(sbuf[slot(number)] - tops[number]).astype(BF16)

    def combine(number, w, head):
        rows = slice(SLOT * head, SLOT * (head + 1))
        mixed_values = mm(vwin[w, rows, :], pbuf[number % 2])
        attt[w, rows, :] = (mixed_values / mixed_values[HEAD : HEAD + 1, :]).astype(BF16)

    def merge_heads(w):
        attended = mm_nt(identity, attt[w]).astype(BF16)
        base = jnp.concatenate([pixels(fpad, half, w, 4, WIN, 8, WIN) for half in range(2)], axis=1)
        first = base + mm(attended, pw[0:192, :])
        fbuf[...] = first
        center = first - jnp.sum(first, axis=-1, keepdims=True) * (1.0 / CH)
        center = jnp.where(inside, center, 0.0)
        spread = jnp.sum(center * center, axis=-1, keepdims=True) * (1.0 / CH)
        second[...] = (center * lax.rsqrt(spread + 1e-05) * g2).astype(BF16)

    def hidden(part):
        lanes = slice(128 * part, 128 * part + 128)
        value = mm(second[...], hpad[:, lanes])
        inner[:, lanes] = (0.5 * value * (1.0 + lax.erf(value * math.sqrt(0.5)))).astype(BF16)

    def finish_window(w):
        mixed = fbuf[...] + mm(inner[...], wout[...])
        for i in range(WIN):
            block = mixed[WIN * i : WIN * (i + 1), :]
            rows = pl.ds((3 + i) * PITCH + 8 + w * WIN, WIN)
            mixpad[0, rows, :] = block[:, 0:128]
            mixpad[1, rows, :] = block[:, 128:256]
            mix_own[i, w * WIN : (w + 1) * WIN, :] = block.astype(BF16)
        if w == 0:
            mix_sl[...] = pack_pixels(*region(mixpad, 3, TH, 8, 8))
            mix_sc[0] = pack_pixels(*region(mixpad, 3, 4, 8, 8))
            mix_sc[2] = pack_pixels(*region(mixpad, 15, 4, 8, 8))
        if w == 3:
            mix_sr[...] = pack_pixels(*region(mixpad, 3, TH, 64, 8))
            mix_sc[1] = pack_pixels(*region(mixpad, 3, 4, 64, 8))
            mix_sc[3] = pack_pixels(*region(mixpad, 15, 4, 64, 8))
        start(mcopies[w])

    def strip(w):
        cols = slice(w * WIN, (w + 1) * WIN)
        return [
            (mix_own.at[0:3, cols], mix_b.at[:, cols], "u"),
            (mix_own.at[13:16, cols], mix_t.at[:, cols], "d"),
        ]

    specs = {
        0: [
            (mix_sl, mix_r, "l"),
            (mix_sc.at[0], mix_c.at[3], "ul"),
            (mix_sc.at[2], mix_c.at[1], "dl"),
        ] + strip(0),
        3: [
            (mix_sr, mix_l, "r"),
            (mix_sc.at[1], mix_c.at[2], "ur"),
            (mix_sc.at[3], mix_c.at[0], "dr"),
        ] + strip(3),
        1: strip(1),
        2: strip(2),
    }
    windows = (0, 3, 1, 2)
    every = exchange([item for w in windows for item in specs[w]], msend, mrecv)
    mcopies = {0: every[0:5], 3: every[5:10], 1: every[10:12], 2: every[12:14]}
    steps = [(w, head) for w in windows for head in range(HEADS)]

    def first_half():
        halo_pixels(0)
        project_keys(0, ((0, KWIN),))
        project_values(0)
        attend(0, 3)

    def second_half():
        halo_pixels(1)
        attend(3, len(steps) + 2)
        merge_heads(windows[-1])
        for part in range(3):
            hidden(part)
        finish_window(windows[-1])

    def attend(begin, end):
        for number in range(begin, end):
            turn, head = divmod(number, HEADS)
            if number < len(steps):
                inner_window = number >= inner_from
                score(number, windows[turn], head, halo_keys if inner_window else whole_keys)
            if 0 <= number - 1 < len(steps):
                exponent(number - 1)
            if 0 <= number - 2:
                combine(number - 2, *steps[number - 2])
            if number < len(late_weights):
                late_weights[number]()
            if turn + 1 < len(windows) and head == 3:
                project_keys(windows[turn + 1], ((0, 4), (20, 4)) if turn else ((0, KWIN),))
            if turn + 1 < len(windows) and head == 4:
                project_values(windows[turn + 1])
            if 0 < turn < len(windows):
                if head == 1:
                    merge_heads(windows[turn - 1])
                elif 2 <= head <= 4:
                    hidden(head - 2)
                elif head == 5:
                    finish_window(windows[turn - 1])

    def all_queries():
        for w in windows:
            project_queries(w)

    def own_scores():
        for w in windows[2:]:
            project_keys(w, ((4, TH),))
        picked = select_bias()
        head_bias(picked, 0)
        for head in range(HEADS):
            score(inner_from + head, windows[2], head, own_keys)
            if head + 1 < HEADS:
                head_bias(picked, head + 1)
            score(inner_from + HEADS + head, windows[3], head, own_keys)

    all_queries()
    arrive("table", "selector")
    own_scores()
    arrive("proj", "gain2", "hid", "outw", "gconv", "bconv", "uconv")
    g2 = lanes256(gain2_v)
    wait_recv(fcopies[k] for k in (0, 1, 2, 3, 4))
    first_half()
    wait_recv(fcopies[k] for k in (5, 6, 7, 8, 9))
    second_half()

    def store_mixed(start, count, values, valid):
        x = jnp.where(valid, values, 0.0)
        rows = pl.ds(start, count)
        mixpad[0, rows, :] = x[:, 0:128]
        mixpad[1, rows, :] = x[:, 128:256]

    def store_packed(packed, valid, starts, skip=0):
        x = unpack_pixels(packed, valid)
        for k, start in enumerate(starts):
            part = slice((k + skip) * 8, (k + skip + 1) * 8)
            for half in range(2):
                mixpad[half, pl.ds(start, 8), :] = x[half][part]

    def side_mixed():
        store_packed(mix_l[...], has_left, [(3 + h) * PITCH for h in range(TH)])
        store_packed(mix_r[...], has_right, [(3 + h) * PITCH + 72 for h in range(TH)])

    def top_mixed():
        for h in range(3):
            store_mixed(h * PITCH + 8, TW, mix_t[h].astype(F32), has_up)
        store_packed(mix_c[0], has_up & has_left, [h * PITCH for h in range(3)], 1)
        store_packed(mix_c[1], has_up & has_right, [h * PITCH + 72 for h in range(3)], 1)

    def bottom_mixed():
        for h in range(3):
            store_mixed((19 + h) * PITCH + 8, TW, mix_b[h].astype(F32), has_down)
        store_packed(mix_c[2], has_down & has_left, [(19 + h) * PITCH for h in range(3)])
        store_packed(mix_c[3], has_down & has_right, [(19 + h) * PITCH + 72 for h in range(3)])

    cols72 = iota((GP, 128), 0)
    gcols = ((cols72 >= 2) | has_left) & ((cols72 < 66) | has_right)
    lcols = ((cols72 >= 1) | has_left) & ((cols72 < 65) | has_right)

    def conv_group(h0, count):
        acc = None
        for a in range(3):
            for b in range(3):
                halves = []
                for half in range(2):
                    rows = [
                        mixpad[half, pl.ds((h0 + k + a) * PITCH + 5 + b, GP), :] for k in range(count)
                    ]
                    halves.append(jnp.concatenate(rows, axis=0).astype(BF16))
                term = mm(jnp.concatenate(halves, axis=1), gpad[3 * a + b])
                acc = term if acc is None else acc + term
        for k in range(count):
            h = h0 + k
            keep = gcols & has_up if h < 2 else gcols & has_down if h >= 18 else gcols
            for half in range(2):
                base = fpad[half, pl.ds((h + 2) * PITCH + 6, GP), :]
                value = base + acc[GP * k : GP * (k + 1), 128 * half : 128 * half + 128]
                gbuf[half, pl.ds(h * GP, GP), :] = jnp.where(keep, value, 0.0)

    low_lanes = iota((GP, 128), 1) < 64
    low64 = iota((TW, 128), 1) < 64

    def conv_before(first, count):
        start = first * GP
        acc = None
        for a in range(3):
            rows = pl.ds(start + a * GP, count * GP)
            lhs = jnp.concatenate([gbuf[half, rows, :].astype(BF16) for half in range(2)], axis=1)
            term = mm(lhs, w2[a])
            acc = term if acc is None else acc + term
        rows = pl.ds(start, count * GP)
        ybuf[0, rows, :] = acc[:, 0:128]
        ybuf[1, rows, :] = acc[:, 128:256]
        for h in range(first, first + count):
            start = h * GP
            value = (
                ybuf[0, pl.ds(start, GP), :]
                + pltpu.roll(ybuf[0, pl.ds(start + 1, GP), :], 64, 1)
                + ybuf[1, pl.ds(start + 2, GP), :]
            )
            value = jnp.where(value >= 0, value, 0.01 * value)
            keep = lcols & has_up if h < 1 else lcols & has_down if h >= 17 else lcols
            value = jnp.where(keep, value, 0.0)
            lbuf[pl.ds(start, GP), :] = jnp.where(low_lanes, value, pltpu.roll(value, 64, 1))
        for h in range(first, first + count):
            start = h * GP
            zero = lbuf[pl.ds(start, TW), :]
            one = lbuf[pl.ds(start + 1, TW), :]
            two = lbuf[pl.ds(start + 2, TW), :]
            l3[h, :, 0:128] = jnp.where(low64, zero, one).astype(BF16)
            l3[h, :, 128:256] = jnp.where(low64, two, 0.0).astype(BF16)

    target = 128 * (lax.shift_right_logical(r, 6) & 1) + 2 * (r & 63) + lax.shift_right_logical(r, 7)
    weave = one_hot(c == target)

    def conv_up(step):
        acc = None
        for a in range(3):
            rhs = jnp.concatenate([l3[4 * step + a + k] for k in range(4)], axis=0)
            term = mm_nt(w3[a], rhs)
            acc = term if acc is None else acc + term
        acc = acc.astype(BF16)
        for pair in range(2):
            lanes = slice(128 * pair, 128 * pair + 128)
            both = jnp.concatenate([acc[0:128, lanes], acc[128:256, lanes]], axis=1)
            woven = mm(both, weave)
            for k in range(2):
                for a in range(2):
                    line = (2 * (4 * step + 2 * pair + k) + a) % 16
                    obuf[step // 2, pl.ds(line, 64, stride=16), :] = woven[
                        64 * a : 64 * (a + 1), 128 * k : 128 * k + 128
                    ]

    def inner_rows():
        for h0 in range(3, 17, 2):
            conv_group(h0, 2)
        conv_before(3, 6)
        conv_before(9, 6)
        conv_up(1)
        conv_up(2)

    def out_half(half):
        ostage[half] = obuf[half].reshape(64, 16, 128).astype(BF16)

    def end_rows():
        conv_group(0, 2)
        conv_group(17, 2)
        conv_group(2, 1)
        conv_group(19, 1)
        conv_before(0, 3)
        conv_before(15, 3)
        conv_up(0)
        conv_up(3)
        out_half(0)

    ybuf[:, 18 * GP :, :] = jnp.zeros((2, 8, 128), F32)
    wait_recv(every[k] for k in (0, 5))
    side_mixed()
    inner_rows()
    stores = [
        pltpu.make_async_copy(ostage.at[half], out.at[:, 16 * half : 16 * half + 16], osem.at[half])
        for half in range(2)
    ]
    wait_recv(every[k] for k in (1, 2, 3, 4, 6, 7, 8, 9, 10, 11, 12, 13))
    top_mixed()
    bottom_mixed()
    end_rows()
    stores[0].start()
    out_half(1)
    stores[1].start()
    for store in stores:
        store.wait()
    wait_send(fcopies + every)


def on_device(
    nr, nc, features, gain_one, qkv_weight, bias_table, proj_weight, gain_two,
    hidden_weight, output_weight, group_conv, before_conv, upsample_conv,
):
    selector = jnp.asarray(table_selector(), BF16)
    operands = (
        features, gain_one, qkv_weight, bias_table.T, proj_weight, gain_two, hidden_weight,
        output_weight.T, group_conv, before_conv.transpose(0, 1, 3, 2),
        upsample_conv.reshape(3, 192, 256), selector,
    )
    any_space = pl.BlockSpec(memory_space=pl.ANY)
    staged = [pltpu.VMEM(x.shape, x.dtype) for x in operands]
    staged[10] = pltpu.VMEM((3, 256, 256), BF16)
    scratch = staged + [
        pltpu.VMEM((2, 192, 128), BF16), pltpu.VMEM((2, 192, 128), BF16),
        pltpu.VMEM((192, 128), BF16), pltpu.VMEM((192, 128), BF16), pltpu.VMEM((4, 48, 128), BF16),
        pltpu.VMEM((2, 192, 128), BF16), pltpu.VMEM((2, 192, 128), BF16),
        pltpu.VMEM((192, 128), BF16), pltpu.VMEM((192, 128), BF16), pltpu.VMEM((4, 48, 128), BF16),
        pltpu.VMEM((3, TW, 256), BF16), pltpu.VMEM((3, TW, 256), BF16),
        pltpu.VMEM((192, 128), BF16), pltpu.VMEM((192, 128), BF16), pltpu.VMEM((4, 48, 128), BF16),
        pltpu.VMEM((192, 128), BF16), pltpu.VMEM((192, 128), BF16), pltpu.VMEM((4, 48, 128), BF16),
        pltpu.VMEM((TH, TW, 256), BF16),
        pltpu.VMEM((2, 24 * PITCH, 128), F32), pltpu.VMEM((2, 24 * PITCH, 128), F32),
        pltpu.VMEM((2, 22 * PITCH, 128), F32), pltpu.VMEM((2, 20 * GP, 128), F32),
        pltpu.VMEM((2, 18 * GP + 8, 128), F32), pltpu.VMEM((18 * GP + 8, 128), F32),
        pltpu.VMEM((18, TW, 256), BF16),
        pltpu.VMEM((256, 640), BF16), pltpu.VMEM((256, 256), BF16), pltpu.VMEM((256, 256), BF16),
        pltpu.VMEM((192, 256), BF16), pltpu.VMEM((256, 256), BF16), pltpu.VMEM((256, 256), BF16),
        pltpu.VMEM((256, 384), BF16), pltpu.VMEM((256, 384), BF16), pltpu.VMEM((384, 256), BF16),
        pltpu.VMEM((9, 256, 256), BF16), pltpu.VMEM((3, 256, 256), BF16),
        pltpu.VMEM((3, 256, 256), BF16), pltpu.VMEM((3, 256, 256), BF16),
        pltpu.VMEM((HEADS, KWIN * KWIN, 256), F32), pltpu.VMEM((4, KWIN * KWIN, 256), BF16),
        pltpu.VMEM((4, KWIN * KWIN, 256), BF16), pltpu.VMEM((4, 192, KWIN * KWIN), BF16),
        pltpu.VMEM((4, 256, 256), F32), pltpu.VMEM((14, KWIN * KWIN, 256), F32),
        pltpu.VMEM((2, KWIN * KWIN, 256), BF16), pltpu.VMEM((4, 192, 256), BF16),
        pltpu.VMEM((256, 256), F32), pltpu.VMEM((256, 256), BF16), pltpu.VMEM((256, 384), BF16),
        pltpu.VMEM((2, 64 * 16, 128), F32), pltpu.VMEM((2, 64, 16, 128), BF16),
        pltpu.SemaphoreType.DMA((2,)),
        pltpu.SemaphoreType.DMA((12,)), pltpu.SemaphoreType.DMA((10,)), pltpu.SemaphoreType.DMA((10,)),
        pltpu.SemaphoreType.DMA((14,)), pltpu.SemaphoreType.DMA((14,)),
    ]
    result = pl.pallas_call(
        functools.partial(kernel, nr, nc),
        out_shape=pltpu.VMEM((64, 2 * TH, 2 * TW), BF16),
        in_specs=[any_space] * len(operands),
        out_specs=pl.BlockSpec(memory_space=pl.ANY),
        scratch_shapes=scratch,
        compiler_params=pltpu.CompilerParams(
            collective_id=0, has_side_effects=True, vmem_limit_bytes=62 * 1024 * 1024
        ),
    )(*operands)
    return result


def solution(mesh):
    placed = (P("rows", "cols", None),) + (P(),) * 10
    body = functools.partial(on_device, mesh.shape["rows"], mesh.shape["cols"])
    return jax.shard_map(
        body, mesh=mesh, in_specs=placed, out_specs=P(None, "rows", "cols"), check_vma=False
    )
```

```python
import functools
import math

import jax
import jax.numpy as jnp
import numpy as np
from jax import lax
from jax.experimental import pallas as pl
from jax.experimental.pallas import tpu as pltpu
from jax.sharding import PartitionSpec as P

HEADS = 6
HEAD = 30
SLOT = 32
CH = 180
WIN = 16
KWIN = 24
SIDE = WIN + KWIN - 1
TABLE = SIDE * SIDE
TH = 16
TW = 64
PITCH = 80
GP = 72
QSCALE = math.log2(math.e) / math.sqrt(HEAD)
LOG2E = math.log2(math.e)
F32 = jnp.float32
BF16 = jnp.bfloat16
MESH = pl.DeviceIdType.MESH
NT = (((1,), (1,)), ((), ()))


def table_selector():
    out = np.zeros((384, 384), np.float32)
    for lane in range(128):
        for part in range(3):
            entry = 16 * part + lane % 16
            if entry < SIDE:
                out[SIDE * (7 - lane // 16) + SIDE - 1 - entry, 128 * part + lane] = 1.0
    return out


def mm(a, b):
    return jnp.dot(a, b, preferred_element_type=F32)


def mm_nt(a, b):
    return lax.dot_general(a, b, NT, preferred_element_type=F32)


def iota(shape, dim):
    return lax.broadcasted_iota(jnp.int32, shape, dim)


def one_hot(mask):
    return jnp.where(mask, 1.0, 0.0).astype(BF16)


def normalize(x, gain):
    lane = iota(x[1].shape, 1)
    mean = jnp.sum(x[0] + x[1], axis=-1, keepdims=True) * (1.0 / CH)
    low = x[0] - mean
    high = jnp.where(lane < CH - 128, x[1] - mean, 0.0)
    spread = jnp.sum(low * low + high * high, axis=-1, keepdims=True) * (1.0 / CH)
    scale = lax.rsqrt(spread + 1e-05)
    return low * scale * gain[:, 0:128], high * scale * gain[:, 128:256]


def pack_pixels(low, high):
    half = low.shape[0] // 2
    lane = iota((half, 128), 1)
    joined = jnp.where(lane < 64, high[:half], pltpu.roll(high[half:], 64, 1))
    return jnp.concatenate([low, joined], axis=0).astype(BF16)


def unpack_pixels(packed, valid):
    count = packed.shape[0] * 2 // 3
    x = jnp.where(valid, packed.astype(F32), 0.0)
    joined = x[count:]
    high = jnp.concatenate([joined, pltpu.roll(joined, 64, 1)], axis=0)
    return x[:count], jnp.where(iota(high.shape, 1) < CH - 128, high, 0.0)


def kernel(
    nr, nc,
    feat, gain1, qkv, table, proj, gain2, hid, outw, gconv, bconv, uconv, selector,
    out,
    feat_v, gain1_v, qkv_v, table_v, proj_v, gain2_v, hid_v, outw_v, gconv_v, bconv_v, upad, sel_v,
    send_t, send_b, send_l, send_r, send_c, halo_t, halo_b, halo_l, halo_r, halo_c,
    mix_t, mix_b, mix_l, mix_r, mix_c, mix_sl, mix_sr, mix_sc, mix_own,
    fpad, npad, mixpad, gbuf, ybuf, lbuf, l3,
    qpad, wqt, wk, wvt, ppad, pw, hpad, opad, wout, gpad, bpad, w2, w3, bias, xwin, kwin, vwin, qwin, sbuf, pbuf, attt, fbuf, second, inner, obuf, ostage, osem,
    local_sem, fsend, frecv, msend, mrecv,
):
    row = lax.axis_index("rows")
    col = lax.axis_index("cols")
    up = lax.rem(row + nr - 1, nr)
    down = lax.rem(row + 1, nr)
    left = lax.rem(col + nc - 1, nc)
    right = lax.rem(col + 1, nc)
    has_up = row > 0
    has_down = row < nr - 1
    has_left = col > 0
    has_right = col < nc - 1
    place = {
        "u": ((up, col), has_up), "d": ((down, col), has_down),
        "l": ((row, left), has_left), "r": ((row, right), has_right),
        "ul": ((up, left), has_up & has_left), "ur": ((up, right), has_up & has_right),
        "dl": ((down, left), has_down & has_left), "dr": ((down, right), has_down & has_right),
    }
    opposite = {"u": "d", "d": "u", "l": "r", "r": "l", "ul": "dr", "dr": "ul", "ur": "dl", "dl": "ur"}
    barrier = pltpu.get_barrier_semaphore()
    expected = 0
    for device, exists in place.values():
        expected = expected + jnp.where(exists, 1, 0)

        @pl.when(exists)
        def _(device=device):
            pl.semaphore_signal(barrier, inc=1, device_id=device, device_id_type=MESH)

    local = {}
    pairs = [
        ("feat", feat, feat_v), ("gain1", gain1, gain1_v), ("table", table, table_v),
        ("selector", selector, sel_v), ("qkv", qkv, qkv_v), ("proj", proj, proj_v),
        ("gain2", gain2, gain2_v), ("hid", hid, hid_v), ("outw", outw, outw_v),
        ("gconv", gconv, gconv_v), ("bconv", bconv, bconv_v), ("uconv", uconv, upad.at[:, 0:192, :]),
    ]
    for number, (name, source, target) in enumerate(pairs):
        local[name] = pltpu.make_async_copy(source, target, local_sem.at[number])
    for name in ("feat", "gain1", "table", "selector"):
        local[name].start()

    def arrive(*names):
        for name in names:
            local[name].wait()

    def exchange(specs, send_sem, recv_sem):
        copies = []
        for number, (source, target, way) in enumerate(specs):
            copy = pltpu.make_async_remote_copy(
                src_ref=source, dst_ref=target, send_sem=send_sem.at[number],
                recv_sem=recv_sem.at[number], device_id=place[way][0], device_id_type=MESH,
            )
            copies.append((copy, place[way][1], place[opposite[way]][1]))
        return copies

    def start(copies):
        for copy, sends, _ in copies:
            pl.when(sends)(copy.start)

    def wait_recv(copies):
        for copy, _, receives in copies:
            pl.when(receives)(copy.wait_recv)

    def wait_send(copies):
        for copy, sends, _ in copies:
            pl.when(sends)(copy.wait_send)

    fcopies = exchange(
        [
            (send_r, halo_l, "r"),
            (send_t.at[0], halo_b.at[0], "u"),
            (send_b.at[0], halo_t.at[0], "d"),
            (send_c.at[3], halo_c.at[0], "dr"),
            (send_c.at[1], halo_c.at[2], "ur"),
            (send_l, halo_r, "l"),
            (send_t.at[1], halo_b.at[1], "u"),
            (send_b.at[1], halo_t.at[1], "d"),
            (send_c.at[0], halo_c.at[3], "ul"),
            (send_c.at[2], halo_c.at[1], "dl"),
        ],
        fsend, frecv,
    )

    fpad[1] = jnp.zeros(fpad.shape[1:], F32)
    arrive("feat", "gain1")
    for h in range(0, TH, 4):
        x = feat_v[h : h + 4].astype(F32).reshape(4 * TW, CH)
        for k in range(4):
            rows = pl.ds((h + k + 4) * PITCH + 8, TW)
            fpad[0, rows, :] = x[k * TW : (k + 1) * TW, 0:128]
            fpad[1, rows, 0 : CH - 128] = x[k * TW : (k + 1) * TW, 128:CH]

    def region(ref, first_row, count_rows, first_col, count_cols):
        return [
            jnp.concatenate(
                [
                    ref[half, pl.ds((first_row + k) * PITCH + first_col, count_cols), :]
                    for k in range(count_rows)
                ],
                axis=0,
            )
            for half in range(2)
        ]

    corner_place = ((4, 8), (4, 64), (16, 8), (16, 64))
    pl.semaphore_wait(barrier, expected)
    for part, corners in ((0, (3, 1)), (1, (0, 2))):
        if part == 0:
            send_r[...] = pack_pixels(*region(fpad, 4, TH, 64, 8))
        else:
            send_l[...] = pack_pixels(*region(fpad, 4, TH, 8, 8))
        send_t[part] = pack_pixels(*region(fpad, 4, 4, 8 + 32 * part, 32))
        send_b[part] = pack_pixels(*region(fpad, 16, 4, 8 + 32 * part, 32))
        start(fcopies[5 * part : 5 * part + 3])
        for corner in corners:
            first_row, first_col = corner_place[corner]
            send_c[corner] = pack_pixels(*region(fpad, first_row, 4, first_col, 8))
        start(fcopies[5 * part + 3 : 5 * part + 5])
    for name in ("qkv", "proj", "gain2", "hid", "outw", "gconv", "bconv", "uconv"):
        local[name].start()

    def lanes256(ref):
        return jnp.concatenate([ref[...].reshape(1, CH), jnp.zeros((1, 256 - CH), F32)], axis=1)

    g1 = lanes256(gain1_v)

    def store_normed(x, starts):
        n = normalize(x, g1)
        width = x[0].shape[0] // len(starts)
        for k, start in enumerate(starts):
            for half in range(2):
                npad[half, pl.ds(start, width), :] = n[half][k * width : (k + 1) * width]

    def own_pixels():
        for h in range(0, TH, 4):
            store_normed(
                region(fpad, h + 4, 4, 8, TW), [(h + k + 4) * PITCH + 8 for k in range(4)]
            )

    own_pixels()
    for ref in (qpad, ppad, hpad, opad):
        ref[...] = jnp.zeros(ref.shape, ref.dtype)

    r = iota((256, 256), 0)
    c = iota((256, 256), 1)
    identity = one_hot(r == c)

    def select_bias():
        whole = jnp.concatenate(
            [table_v[...] * LOG2E, jnp.zeros((HEADS, 1536 - TABLE), F32)], axis=1
        )
        whole = jnp.concatenate([whole, jnp.zeros((2, 1536), F32)], axis=0)
        pieces = []
        for tile in range(5):
            first = SIDE * (SIDE - 8 - 8 * tile)
            pieces.append(pltpu.roll(whole, (1536 - first) % 1536, 1)[:, 0:384])
        rows = jnp.concatenate(pieces, axis=0)
        hi = rows.astype(BF16)
        rest = rows - hi.astype(F32)
        mid = rest.astype(BF16)
        low = (rest - mid.astype(F32)).astype(BF16)
        picked = mm(hi, sel_v[...]) + mm(mid, sel_v[...]) + mm(low, sel_v[...])
        return picked

    lane8 = iota((8, 128), 1)
    sub8 = iota((8, 128), 0)
    lane24 = iota((KWIN, 128), 1)

    def head_bias(picked, head):
        tiles = []
        for tile in range(5):
            z = picked[8 * tile + head : 8 * tile + head + 1, :]
            blocks = []
            for part, base in ((1, 7), (0, 15), (0, 7)):
                first = jnp.broadcast_to(z[:, 128 * part : 128 * part + 128], (8, 128))
                second = jnp.broadcast_to(z[:, 128 * part + 128 : 128 * part + 256], (8, 128))
                first = pltpu.roll(first, 128 - base, 1, stride=1, stride_axis=0)
                second = pltpu.roll(second, 16 - base, 1, stride=1, stride_axis=0)
                blocks.append(jnp.where((lane8 & 15) + base - sub8 < 16, first, second))
            tiles.append(jnp.concatenate(blocks, axis=0))
        for shift in range(8):
            amount = 16 * shift
            if shift:
                rolled = [pltpu.roll(t, 128 - amount, 1) for t in tiles]
                joined = [
                    jnp.where(lane24 < 128 - amount, rolled[k], rolled[k + 1]) for k in range(4)
                ]
            else:
                joined = tiles
            for block in range(3):
                p = KWIN - 1 - 8 * block - shift
                for half in range(2):
                    bias[head, KWIN * p : KWIN * (p + 1), 128 * half : 128 * half + 128] = (
                        joined[block + half]
                    )

    def prepare_weights():
        qpad[0:CH, 0 : 3 * CH] = qkv_v[...]
        wqt[...] = mm_nt(one_hot((r == c) & (r < CH)), qpad[:, 0:256]).astype(BF16)
        wk[...] = mm(qpad[:, 128:384], one_hot((r == c + 52) & (c < CH))).astype(BF16)
        rv = iota((192, 384), 0)
        cv = iota((192, 384), 1)
        source = HEAD * lax.shift_right_logical(rv, 5) + (rv & 31)
        wvt[...] = mm_nt(one_hot((cv == source + 104) & ((rv & 31) < HEAD)), qpad[:, 256:640]).astype(BF16)

    def proj_weights():
        ppad[0:CH, 0:CH] = proj_v[...]
        source = HEAD * lax.shift_right_logical(r, 5) + (r & 31)
        pw[...] = mm(one_hot((c == source) & ((r & 31) < HEAD) & (r < 192)), ppad[...]).astype(BF16)
        hpad[0:CH, 0 : 2 * CH] = hid_v[...]

    def out_weights():
        opad[0:CH, 0 : 2 * CH] = outw_v[...]
        wout[...] = mm_nt(one_hot(iota((384, 384), 0) == iota((384, 384), 1)), opad[...]).astype(BF16)

    def conv_weights(a):
        for b in range(3):
            tap = 3 * a + b
            gpad[tap] = jnp.zeros((256, 256), BF16)
            gpad[tap, 0:CH, 0:CH] = gconv_v[a, b]
        bpad[a] = jnp.zeros((256, 256), BF16)
        upad[a, 192:256, :] = jnp.zeros((64, 256), BF16)
        order = 4 * (r & 63) + 2 * (lax.shift_right_logical(r, 6) & 1) + lax.shift_right_logical(r, 7)
        for b in range(3):
            bpad[a, 64 * b : 64 * (b + 1), 0:CH] = bconv_v[a, b]
        w2[a] = mm_nt(identity, bpad[a]).astype(BF16)
        w3[a] = mm_nt(one_hot(c == order), upad[a]).astype(BF16)

    late_weights = [
        proj_weights, out_weights, functools.partial(conv_weights, 0),
        functools.partial(conv_weights, 1), functools.partial(conv_weights, 2),
    ]
    arrive("qkv")
    prepare_weights()

    def halo_pixels(part):
        side, rim, has_side = ((halo_l, 0, has_left), (halo_r, 72, has_right))[part]
        groups = [
            (halo_t[part], has_up, [h * PITCH + 8 + 32 * part for h in range(4)]),
            (halo_b[part], has_down, [(20 + h) * PITCH + 8 + 32 * part for h in range(4)]),
            (side[...], has_side, [(4 + h) * PITCH + rim for h in range(TH)]),
            (halo_c[part], has_up & has_side, [h * PITCH + rim for h in range(4)]),
            (halo_c[2 + part], has_down & has_side, [(20 + h) * PITCH + rim for h in range(4)]),
        ]
        for packed, valid, starts in groups:
            x = unpack_pixels(packed, valid)
            width = x[0].shape[0] // len(starts)
            for k, start in enumerate(starts):
                for half in range(2):
                    fpad[half, pl.ds(start, width), :] = x[half][k * width : (k + 1) * width]
            store_normed(x, starts)

    inside = c < CH
    ones_row = (iota((192, KWIN * KWIN), 0) & 31) == HEAD
    tops = {}

    def pixels(ref, half, w, first_row, count_rows, first_col, count_cols):
        return jnp.concatenate(
            [
                ref[half, pl.ds((first_row + p) * PITCH + first_col + w * WIN, count_cols), :]
                for p in range(count_rows)
            ],
            axis=0,
        )

    def project_keys(w, spans):
        for first, count in spans:
            keys_in = jnp.concatenate(
                [pixels(npad, half, w, first, count, 4, KWIN).astype(BF16) for half in range(2)],
                axis=1,
            )
            rows = slice(KWIN * first, KWIN * (first + count))
            xwin[w, rows, :] = keys_in
            kwin[w, rows, :] = mm(keys_in, wk[...]).astype(BF16)

    def project_values(w):
        vwin[w] = jnp.where(ones_row, 1.0, mm_nt(wvt[...], xwin[w])).astype(BF16)

    def project_queries(w):
        query_in = jnp.concatenate(
            [pixels(npad, half, w, 4, WIN, 8, WIN).astype(BF16) for half in range(2)], axis=1
        )
        qwin[w] = mm_nt(wqt[...], query_in) * QSCALE

    whole_keys = ((0, 288), (288, 576))
    own_keys = ((96, 288), (288, 480))
    halo_keys = ((0, 96), (480, 576))
    inner_from = 2 * HEADS

    def slot(number):
        return number % 2 if number < inner_from else 2 + number - inner_from

    def score(number, w, head, spans):
        mine = (r >= HEAD * head) & (r < HEAD * (head + 1))
        q = jnp.where(mine, qwin[w], 0.0).astype(BF16)
        top = tops.get(number)
        for first, last in spans:
            scores = mm(kwin[w, first:last, :], q) + bias[head, first:last, :]
            sbuf[slot(number), first:last, :] = scores
            best = jnp.max(scores, axis=0, keepdims=True)
            top = best if top is None else jnp.maximum(top, best)
        tops[number] = top

    def exponent(number):
        pbuf[number % 2] = jnp.exp2(sbuf[slot(number)] - tops[number]).astype(BF16)

    def combine(number, w, head):
        rows = slice(SLOT * head, SLOT * (head + 1))
        mixed_values = mm(vwin[w, rows, :], pbuf[number % 2])
        attt[w, rows, :] = (mixed_values / mixed_values[HEAD : HEAD + 1, :]).astype(BF16)

    def merge_heads(w):
        attended = mm_nt(identity, attt[w]).astype(BF16)
        base = jnp.concatenate([pixels(fpad, half, w, 4, WIN, 8, WIN) for half in range(2)], axis=1)
        first = base + mm(attended, pw[0:192, :])
        fbuf[...] = first
        center = first - jnp.sum(first, axis=-1, keepdims=True) * (1.0 / CH)
        center = jnp.where(inside, center, 0.0)
        spread = jnp.sum(center * center, axis=-1, keepdims=True) * (1.0 / CH)
        second[...] = (center * lax.rsqrt(spread + 1e-05) * g2).astype(BF16)

    def hidden(part):
        lanes = slice(128 * part, 128 * part + 128)
        value = mm(second[...], hpad[:, lanes])
        inner[:, lanes] = (0.5 * value * (1.0 + lax.erf(value * math.sqrt(0.5)))).astype(BF16)

    def finish_window(w):
        mixed = fbuf[...] + mm(inner[...], wout[...])
        for i in range(WIN):
            block = mixed[WIN * i : WIN * (i + 1), :]
            rows = pl.ds((3 + i) * PITCH + 8 + w * WIN, WIN)
            mixpad[0, rows, :] = block[:, 0:128]
            mixpad[1, rows, :] = block[:, 128:256]
            mix_own[i, w * WIN : (w + 1) * WIN, :] = block.astype(BF16)
        if w == 0:
            mix_sl[...] = pack_pixels(*region(mixpad, 3, TH, 8, 8))
            mix_sc[0] = pack_pixels(*region(mixpad, 3, 4, 8, 8))
            mix_sc[2] = pack_pixels(*region(mixpad, 15, 4, 8, 8))
        if w == 3:
            mix_sr[...] = pack_pixels(*region(mixpad, 3, TH, 64, 8))
            mix_sc[1] = pack_pixels(*region(mixpad, 3, 4, 64, 8))
            mix_sc[3] = pack_pixels(*region(mixpad, 15, 4, 64, 8))
        start(mcopies[w])

    def strip(w):
        cols = slice(w * WIN, (w + 1) * WIN)
        return [
            (mix_own.at[0:3, cols], mix_b.at[:, cols], "u"),
            (mix_own.at[13:16, cols], mix_t.at[:, cols], "d"),
        ]

    specs = {
        0: [
            (mix_sl, mix_r, "l"),
            (mix_sc.at[0], mix_c.at[3], "ul"),
            (mix_sc.at[2], mix_c.at[1], "dl"),
        ] + strip(0),
        3: [
            (mix_sr, mix_l, "r"),
            (mix_sc.at[1], mix_c.at[2], "ur"),
            (mix_sc.at[3], mix_c.at[0], "dr"),
        ] + strip(3),
        1: strip(1),
        2: strip(2),
    }
    windows = (0, 3, 1, 2)
    every = exchange([item for w in windows for item in specs[w]], msend, mrecv)
    mcopies = {0: every[0:5], 3: every[5:10], 1: every[10:12], 2: every[12:14]}
    steps = [(w, head) for w in windows for head in range(HEADS)]

    def first_half():
        halo_pixels(0)
        project_keys(0, ((0, KWIN),))
        project_values(0)
        attend(0, 3)

    def second_half():
        halo_pixels(1)
        attend(3, len(steps) + 2)
        merge_heads(windows[-1])
        for part in range(3):
            hidden(part)
        finish_window(windows[-1])

    def attend(begin, end):
        for number in range(begin, end):
            turn, head = divmod(number, HEADS)
            if number < len(steps):
                inner_window = number >= inner_from
                score(number, windows[turn], head, halo_keys if inner_window else whole_keys)
            if 0 <= number - 1 < len(steps):
                exponent(number - 1)
            if 0 <= number - 2:
                combine(number - 2, *steps[number - 2])
            if number < len(late_weights):
                late_weights[number]()
            if turn + 1 < len(windows) and head == 3:
                project_keys(windows[turn + 1], ((0, 4), (20, 4)) if turn else ((0, KWIN),))
            if turn + 1 < len(windows) and head == 4:
                project_values(windows[turn + 1])
            if 0 < turn < len(windows):
                if head == 1:
                    merge_heads(windows[turn - 1])
                elif 2 <= head <= 4:
                    hidden(head - 2)
                elif head == 5:
                    finish_window(windows[turn - 1])

    def all_queries():
        for w in windows:
            project_queries(w)

    def own_scores():
        for w in windows[2:]:
            project_keys(w, ((4, TH),))
        picked = select_bias()
        head_bias(picked, 0)
        for head in range(HEADS):
            score(inner_from + head, windows[2], head, own_keys)
            if head + 1 < HEADS:
                head_bias(picked, head + 1)
            score(inner_from + HEADS + head, windows[3], head, own_keys)

    all_queries()
    arrive("table", "selector")
    own_scores()
    arrive("proj", "gain2", "hid", "outw", "gconv", "bconv", "uconv")
    g2 = lanes256(gain2_v)
    wait_recv(fcopies[k] for k in (0, 1, 2, 3, 4))
    first_half()
    wait_recv(fcopies[k] for k in (5, 6, 7, 8, 9))
    second_half()

    def store_mixed(start, count, values, valid):
        x = jnp.where(valid, values, 0.0)
        rows = pl.ds(start, count)
        mixpad[0, rows, :] = x[:, 0:128]
        mixpad[1, rows, :] = x[:, 128:256]

    def store_packed(packed, valid, starts, skip=0):
        x = unpack_pixels(packed, valid)
        for k, start in enumerate(starts):
            part = slice((k + skip) * 8, (k + skip + 1) * 8)
            for half in range(2):
                mixpad[half, pl.ds(start, 8), :] = x[half][part]

    def side_mixed():
        store_packed(mix_l[...], has_left, [(3 + h) * PITCH for h in range(TH)])
        store_packed(mix_r[...], has_right, [(3 + h) * PITCH + 72 for h in range(TH)])

    def top_mixed():
        for h in range(3):
            store_mixed(h * PITCH + 8, TW, mix_t[h].astype(F32), has_up)
        store_packed(mix_c[0], has_up & has_left, [h * PITCH for h in range(3)], 1)
        store_packed(mix_c[1], has_up & has_right, [h * PITCH + 72 for h in range(3)], 1)

    def bottom_mixed():
        for h in range(3):
            store_mixed((19 + h) * PITCH + 8, TW, mix_b[h].astype(F32), has_down)
        store_packed(mix_c[2], has_down & has_left, [(19 + h) * PITCH for h in range(3)])
        store_packed(mix_c[3], has_down & has_right, [(19 + h) * PITCH + 72 for h in range(3)])

    cols72 = iota((GP, 128), 0)
    gcols = ((cols72 >= 2) | has_left) & ((cols72 < 66) | has_right)
    lcols = ((cols72 >= 1) | has_left) & ((cols72 < 65) | has_right)

    def conv_group(h0, count):
        acc = None
        for a in range(3):
            for b in range(3):
                halves = []
                for half in range(2):
                    rows = [
                        mixpad[half, pl.ds((h0 + k + a) * PITCH + 5 + b, GP), :] for k in range(count)
                    ]
                    halves.append(jnp.concatenate(rows, axis=0).astype(BF16))
                term = mm(jnp.concatenate(halves, axis=1), gpad[3 * a + b])
                acc = term if acc is None else acc + term
        for k in range(count):
            h = h0 + k
            keep = gcols & has_up if h < 2 else gcols & has_down if h >= 18 else gcols
            for half in range(2):
                base = fpad[half, pl.ds((h + 2) * PITCH + 6, GP), :]
                value = base + acc[GP * k : GP * (k + 1), 128 * half : 128 * half + 128]
                gbuf[half, pl.ds(h * GP, GP), :] = jnp.where(keep, value, 0.0)

    low_lanes = iota((GP, 128), 1) < 64
    low64 = iota((TW, 128), 1) < 64

    def conv_before(first, count):
        start = first * GP
        acc = None
        for a in range(3):
            rows = pl.ds(start + a * GP, count * GP)
            lhs = jnp.concatenate([gbuf[half, rows, :].astype(BF16) for half in range(2)], axis=1)
            term = mm(lhs, w2[a])
            acc = term if acc is None else acc + term
        rows = pl.ds(start, count * GP)
        ybuf[0, rows, :] = acc[:, 0:128]
        ybuf[1, rows, :] = acc[:, 128:256]
        for h in range(first, first + count):
            start = h * GP
            value = (
                ybuf[0, pl.ds(start, GP), :]
                + pltpu.roll(ybuf[0, pl.ds(start + 1, GP), :], 64, 1)
                + ybuf[1, pl.ds(start + 2, GP), :]
            )
            value = jnp.where(value >= 0, value, 0.01 * value)
            keep = lcols & has_up if h < 1 else lcols & has_down if h >= 17 else lcols
            value = jnp.where(keep, value, 0.0)
            lbuf[pl.ds(start, GP), :] = jnp.where(low_lanes, value, pltpu.roll(value, 64, 1))
        for h in range(first, first + count):
            start = h * GP
            zero = lbuf[pl.ds(start, TW), :]
            one = lbuf[pl.ds(start + 1, TW), :]
            two = lbuf[pl.ds(start + 2, TW), :]
            l3[h, :, 0:128] = jnp.where(low64, zero, one).astype(BF16)
            l3[h, :, 128:256] = jnp.where(low64, two, 0.0).astype(BF16)

    target = 128 * (lax.shift_right_logical(r, 6) & 1) + 2 * (r & 63) + lax.shift_right_logical(r, 7)
    weave = one_hot(c == target)

    def conv_up(step):
        acc = None
        for a in range(3):
            rhs = jnp.concatenate([l3[4 * step + a + k] for k in range(4)], axis=0)
            term = mm_nt(w3[a], rhs)
            acc = term if acc is None else acc + term
        acc = acc.astype(BF16)
        for pair in range(2):
            lanes = slice(128 * pair, 128 * pair + 128)
            both = jnp.concatenate([acc[0:128, lanes], acc[128:256, lanes]], axis=1)
            woven = mm(both, weave)
            for k in range(2):
                for a in range(2):
                    line = (2 * (4 * step + 2 * pair + k) + a) % 16
                    obuf[step // 2, pl.ds(line, 64, stride=16), :] = woven[
                        64 * a : 64 * (a + 1), 128 * k : 128 * k + 128
                    ]

    def inner_rows():
        for h0 in (3, 5, 7, 9):
            conv_group(h0, 2)
        conv_before(3, 6)
        for h0 in (11, 13, 15):
            conv_group(h0, 2)
        conv_before(9, 6)
        conv_up(1)
        conv_up(2)

    def out_half(half):
        ostage[half] = obuf[half].reshape(64, 16, 128).astype(BF16)

    def end_rows():
        conv_group(0, 2)
        conv_group(2, 1)
        conv_group(17, 2)
        conv_before(0, 3)
        conv_group(19, 1)
        conv_before(15, 3)
        conv_up(0)
        conv_up(3)
        out_half(0)

    ybuf[:, 18 * GP :, :] = jnp.zeros((2, 8, 128), F32)
    wait_recv(every[k] for k in (0, 5))
    side_mixed()
    inner_rows()
    stores = [
        pltpu.make_async_copy(ostage.at[half], out.at[:, 16 * half : 16 * half + 16], osem.at[half])
        for half in range(2)
    ]
    wait_recv(every[k] for k in (1, 2, 3, 4, 6, 7, 8, 9, 10, 11, 12, 13))
    top_mixed()
    bottom_mixed()
    end_rows()
    stores[0].start()
    out_half(1)
    stores[1].start()
    for store in stores:
        store.wait()
    wait_send(fcopies + every)


def on_device(
    nr, nc, features, gain_one, qkv_weight, bias_table, proj_weight, gain_two,
    hidden_weight, output_weight, group_conv, before_conv, upsample_conv,
):
    selector = jnp.asarray(table_selector(), BF16)
    operands = (
        features, gain_one, qkv_weight, bias_table.T, proj_weight, gain_two, hidden_weight,
        output_weight.T, group_conv, before_conv.transpose(0, 1, 3, 2),
        upsample_conv.reshape(3, 192, 256), selector,
    )
    any_space = pl.BlockSpec(memory_space=pl.ANY)
    staged = [pltpu.VMEM(x.shape, x.dtype) for x in operands]
    staged[10] = pltpu.VMEM((3, 256, 256), BF16)
    scratch = staged + [
        pltpu.VMEM((2, 192, 128), BF16), pltpu.VMEM((2, 192, 128), BF16),
        pltpu.VMEM((192, 128), BF16), pltpu.VMEM((192, 128), BF16), pltpu.VMEM((4, 48, 128), BF16),
        pltpu.VMEM((2, 192, 128), BF16), pltpu.VMEM((2, 192, 128), BF16),
        pltpu.VMEM((192, 128), BF16), pltpu.VMEM((192, 128), BF16), pltpu.VMEM((4, 48, 128), BF16),
        pltpu.VMEM((3, TW, 256), BF16), pltpu.VMEM((3, TW, 256), BF16),
        pltpu.VMEM((192, 128), BF16), pltpu.VMEM((192, 128), BF16), pltpu.VMEM((4, 48, 128), BF16),
        pltpu.VMEM((192, 128), BF16), pltpu.VMEM((192, 128), BF16), pltpu.VMEM((4, 48, 128), BF16),
        pltpu.VMEM((TH, TW, 256), BF16),
        pltpu.VMEM((2, 24 * PITCH, 128), F32), pltpu.VMEM((2, 24 * PITCH, 128), F32),
        pltpu.VMEM((2, 22 * PITCH, 128), F32), pltpu.VMEM((2, 20 * GP, 128), F32),
        pltpu.VMEM((2, 18 * GP + 8, 128), F32), pltpu.VMEM((18 * GP + 8, 128), F32),
        pltpu.VMEM((18, TW, 256), BF16),
        pltpu.VMEM((256, 640), BF16), pltpu.VMEM((256, 256), BF16), pltpu.VMEM((256, 256), BF16),
        pltpu.VMEM((192, 256), BF16), pltpu.VMEM((256, 256), BF16), pltpu.VMEM((256, 256), BF16),
        pltpu.VMEM((256, 384), BF16), pltpu.VMEM((256, 384), BF16), pltpu.VMEM((384, 256), BF16),
        pltpu.VMEM((9, 256, 256), BF16), pltpu.VMEM((3, 256, 256), BF16),
        pltpu.VMEM((3, 256, 256), BF16), pltpu.VMEM((3, 256, 256), BF16),
        pltpu.VMEM((HEADS, KWIN * KWIN, 256), F32), pltpu.VMEM((4, KWIN * KWIN, 256), BF16),
        pltpu.VMEM((4, KWIN * KWIN, 256), BF16), pltpu.VMEM((4, 192, KWIN * KWIN), BF16),
        pltpu.VMEM((4, 256, 256), F32), pltpu.VMEM((14, KWIN * KWIN, 256), F32),
        pltpu.VMEM((2, KWIN * KWIN, 256), BF16), pltpu.VMEM((4, 192, 256), BF16),
        pltpu.VMEM((256, 256), F32), pltpu.VMEM((256, 256), BF16), pltpu.VMEM((256, 384), BF16),
        pltpu.VMEM((2, 64 * 16, 128), F32), pltpu.VMEM((2, 64, 16, 128), BF16),
        pltpu.SemaphoreType.DMA((2,)),
        pltpu.SemaphoreType.DMA((12,)), pltpu.SemaphoreType.DMA((10,)), pltpu.SemaphoreType.DMA((10,)),
        pltpu.SemaphoreType.DMA((14,)), pltpu.SemaphoreType.DMA((14,)),
    ]
    result = pl.pallas_call(
        functools.partial(kernel, nr, nc),
        out_shape=pltpu.VMEM((64, 2 * TH, 2 * TW), BF16),
        in_specs=[any_space] * len(operands),
        out_specs=pl.BlockSpec(memory_space=pl.ANY),
        scratch_shapes=scratch,
        compiler_params=pltpu.CompilerParams(
            collective_id=0, has_side_effects=True, vmem_limit_bytes=62 * 1024 * 1024
        ),
    )(*operands)
    return result


def solution(mesh):
    placed = (P("rows", "cols", None),) + (P(),) * 10
    body = functools.partial(on_device, mesh.shape["rows"], mesh.shape["cols"])
    return jax.shard_map(
        body, mesh=mesh, in_specs=placed, out_specs=P(None, "rows", "cols"), check_vma=False
    )
```

```python
import functools
import math

import jax
import jax.numpy as jnp
import numpy as np
from jax import lax
from jax.experimental import pallas as pl
from jax.experimental.pallas import tpu as pltpu
from jax.sharding import PartitionSpec as P

HEADS = 6
HEAD = 30
SLOT = 32
CH = 180
WIN = 16
KWIN = 24
SIDE = WIN + KWIN - 1
TABLE = SIDE * SIDE
TH = 16
TW = 64
PITCH = 80
GP = 72
QSCALE = math.log2(math.e) / math.sqrt(HEAD)
LOG2E = math.log2(math.e)
F32 = jnp.float32
BF16 = jnp.bfloat16
MESH = pl.DeviceIdType.MESH
NT = (((1,), (1,)), ((), ()))


def table_selector():
    out = np.zeros((384, 384), np.float32)
    for lane in range(128):
        for part in range(3):
            entry = 16 * part + lane % 16
            if entry < SIDE:
                out[SIDE * (7 - lane // 16) + SIDE - 1 - entry, 128 * part + lane] = 1.0
    return out


def mm(a, b):
    return jnp.dot(a, b, preferred_element_type=F32)


def mm_nt(a, b):
    return lax.dot_general(a, b, NT, preferred_element_type=F32)


def iota(shape, dim):
    return lax.broadcasted_iota(jnp.int32, shape, dim)


def one_hot(mask):
    return jnp.where(mask, 1.0, 0.0).astype(BF16)


def normalize(x, gain):
    lane = iota(x[1].shape, 1)
    mean = jnp.sum(x[0] + x[1], axis=-1, keepdims=True) * (1.0 / CH)
    low = x[0] - mean
    high = jnp.where(lane < CH - 128, x[1] - mean, 0.0)
    spread = jnp.sum(low * low + high * high, axis=-1, keepdims=True) * (1.0 / CH)
    scale = lax.rsqrt(spread + 1e-05)
    return low * scale * gain[:, 0:128], high * scale * gain[:, 128:256]


def pack_pixels(low, high):
    half = low.shape[0] // 2
    lane = iota((half, 128), 1)
    joined = jnp.where(lane < 64, high[:half], pltpu.roll(high[half:], 64, 1))
    return jnp.concatenate([low, joined], axis=0).astype(BF16)


def unpack_pixels(packed, valid):
    count = packed.shape[0] * 2 // 3
    x = jnp.where(valid, packed.astype(F32), 0.0)
    joined = x[count:]
    high = jnp.concatenate([joined, pltpu.roll(joined, 64, 1)], axis=0)
    return x[:count], jnp.where(iota(high.shape, 1) < CH - 128, high, 0.0)


def kernel(
    nr, nc,
    feat, gain1, qkv, table, proj, gain2, hid, outw, gconv, bconv, uconv, selector,
    out,
    feat_v, gain1_v, qkv_v, table_v, proj_v, gain2_v, hid_v, outw_v, gconv_v, bconv_v, upad, sel_v,
    send_t, send_b, send_l, send_r, send_c, halo_t, halo_b, halo_l, halo_r, halo_c,
    mix_t, mix_b, mix_l, mix_r, mix_c, mix_sl, mix_sr, mix_sc, mix_own,
    fpad, npad, mixpad, gbuf, ybuf, lbuf, l3,
    qpad, wqt, wk, wvt, ppad, pw, hpad, opad, wout, gpad, bpad, w2, w3, bias, xwin, kwin, vwin, qwin, sbuf, pbuf, attt, fbuf, second, inner, obuf, ostage, osem,
    local_sem, fsend, frecv, msend, mrecv,
):
    row = lax.axis_index("rows")
    col = lax.axis_index("cols")
    up = lax.rem(row + nr - 1, nr)
    down = lax.rem(row + 1, nr)
    left = lax.rem(col + nc - 1, nc)
    right = lax.rem(col + 1, nc)
    has_up = row > 0
    has_down = row < nr - 1
    has_left = col > 0
    has_right = col < nc - 1
    place = {
        "u": ((up, col), has_up), "d": ((down, col), has_down),
        "l": ((row, left), has_left), "r": ((row, right), has_right),
        "ul": ((up, left), has_up & has_left), "ur": ((up, right), has_up & has_right),
        "dl": ((down, left), has_down & has_left), "dr": ((down, right), has_down & has_right),
    }
    opposite = {"u": "d", "d": "u", "l": "r", "r": "l", "ul": "dr", "dr": "ul", "ur": "dl", "dl": "ur"}
    barrier = pltpu.get_barrier_semaphore()
    expected = 0
    for device, exists in place.values():
        expected = expected + jnp.where(exists, 1, 0)

        @pl.when(exists)
        def _(device=device):
            pl.semaphore_signal(barrier, inc=1, device_id=device, device_id_type=MESH)

    local = {}
    pairs = [
        ("feat", feat, feat_v), ("gain1", gain1, gain1_v), ("table", table, table_v),
        ("selector", selector, sel_v), ("qkv", qkv, qkv_v), ("proj", proj, proj_v),
        ("gain2", gain2, gain2_v), ("hid", hid, hid_v), ("outw", outw, outw_v),
        ("gconv", gconv, gconv_v), ("bconv", bconv, bconv_v), ("uconv", uconv, upad.at[:, 0:192, :]),
    ]
    for number, (name, source, target) in enumerate(pairs):
        local[name] = pltpu.make_async_copy(source, target, local_sem.at[number])
    for name in ("feat", "gain1", "table", "selector"):
        local[name].start()

    def arrive(*names):
        for name in names:
            local[name].wait()

    def exchange(specs, send_sem, recv_sem):
        copies = []
        for number, (source, target, way) in enumerate(specs):
            copy = pltpu.make_async_remote_copy(
                src_ref=source, dst_ref=target, send_sem=send_sem.at[number],
                recv_sem=recv_sem.at[number], device_id=place[way][0], device_id_type=MESH,
            )
            copies.append((copy, place[way][1], place[opposite[way]][1]))
        return copies

    def start(copies):
        for copy, sends, _ in copies:
            pl.when(sends)(copy.start)

    def wait_recv(copies):
        for copy, _, receives in copies:
            pl.when(receives)(copy.wait_recv)

    def wait_send(copies):
        for copy, sends, _ in copies:
            pl.when(sends)(copy.wait_send)

    fcopies = exchange(
        [
            (send_r, halo_l, "r"),
            (send_t.at[0], halo_b.at[0], "u"),
            (send_b.at[0], halo_t.at[0], "d"),
            (send_c.at[3], halo_c.at[0], "dr"),
            (send_c.at[1], halo_c.at[2], "ur"),
            (send_l, halo_r, "l"),
            (send_t.at[1], halo_b.at[1], "u"),
            (send_b.at[1], halo_t.at[1], "d"),
            (send_c.at[0], halo_c.at[3], "ul"),
            (send_c.at[2], halo_c.at[1], "dl"),
        ],
        fsend, frecv,
    )

    fpad[1] = jnp.zeros(fpad.shape[1:], F32)
    arrive("feat", "gain1")
    for h in range(0, TH, 4):
        x = feat_v[h : h + 4].astype(F32).reshape(4 * TW, CH)
        for k in range(4):
            rows = pl.ds((h + k + 4) * PITCH + 8, TW)
            fpad[0, rows, :] = x[k * TW : (k + 1) * TW, 0:128]
            fpad[1, rows, 0 : CH - 128] = x[k * TW : (k + 1) * TW, 128:CH]

    def region(ref, first_row, count_rows, first_col, count_cols):
        return [
            jnp.concatenate(
                [
                    ref[half, pl.ds((first_row + k) * PITCH + first_col, count_cols), :]
                    for k in range(count_rows)
                ],
                axis=0,
            )
            for half in range(2)
        ]

    corner_place = ((4, 8), (4, 64), (16, 8), (16, 64))
    pl.semaphore_wait(barrier, expected)
    for part, corners in ((0, (3, 1)), (1, (0, 2))):
        if part == 0:
            send_r[...] = pack_pixels(*region(fpad, 4, TH, 64, 8))
        else:
            send_l[...] = pack_pixels(*region(fpad, 4, TH, 8, 8))
        send_t[part] = pack_pixels(*region(fpad, 4, 4, 8 + 32 * part, 32))
        send_b[part] = pack_pixels(*region(fpad, 16, 4, 8 + 32 * part, 32))
        start(fcopies[5 * part : 5 * part + 3])
        for corner in corners:
            first_row, first_col = corner_place[corner]
            send_c[corner] = pack_pixels(*region(fpad, first_row, 4, first_col, 8))
        start(fcopies[5 * part + 3 : 5 * part + 5])
    for name in ("qkv", "proj", "gain2", "hid", "outw", "gconv", "bconv", "uconv"):
        local[name].start()

    def lanes256(ref):
        return jnp.concatenate([ref[...].reshape(1, CH), jnp.zeros((1, 256 - CH), F32)], axis=1)

    g1 = lanes256(gain1_v)

    def store_normed(x, starts):
        n = normalize(x, g1)
        width = x[0].shape[0] // len(starts)
        for k, start in enumerate(starts):
            for half in range(2):
                npad[half, pl.ds(start, width), :] = n[half][k * width : (k + 1) * width]

    def own_pixels():
        for h in range(0, TH, 4):
            store_normed(
                region(fpad, h + 4, 4, 8, TW), [(h + k + 4) * PITCH + 8 for k in range(4)]
            )

    own_pixels()
    for ref in (qpad, ppad, hpad, opad):
        ref[...] = jnp.zeros(ref.shape, ref.dtype)

    r = iota((256, 256), 0)
    c = iota((256, 256), 1)
    identity = one_hot(r == c)

    def select_bias():
        whole = jnp.concatenate(
            [table_v[...] * LOG2E, jnp.zeros((HEADS, 1536 - TABLE), F32)], axis=1
        )
        whole = jnp.concatenate([whole, jnp.zeros((2, 1536), F32)], axis=0)
        pieces = []
        for tile in range(5):
            first = SIDE * (SIDE - 8 - 8 * tile)
            pieces.append(pltpu.roll(whole, (1536 - first) % 1536, 1)[:, 0:384])
        rows = jnp.concatenate(pieces, axis=0)
        hi = rows.astype(BF16)
        rest = rows - hi.astype(F32)
        mid = rest.astype(BF16)
        low = (rest - mid.astype(F32)).astype(BF16)
        picked = mm(hi, sel_v[...]) + mm(mid, sel_v[...]) + mm(low, sel_v[...])
        return picked

    lane8 = iota((8, 128), 1)
    sub8 = iota((8, 128), 0)
    lane24 = iota((KWIN, 128), 1)

    def head_bias(picked, head):
        tiles = []
        for tile in range(5):
            z = picked[8 * tile + head : 8 * tile + head + 1, :]
            blocks = []
            for part, base in ((1, 7), (0, 15), (0, 7)):
                first = jnp.broadcast_to(z[:, 128 * part : 128 * part + 128], (8, 128))
                second = jnp.broadcast_to(z[:, 128 * part + 128 : 128 * part + 256], (8, 128))
                first = pltpu.roll(first, 128 - base, 1, stride=1, stride_axis=0)
                second = pltpu.roll(second, 16 - base, 1, stride=1, stride_axis=0)
                blocks.append(jnp.where((lane8 & 15) + base - sub8 < 16, first, second))
            tiles.append(jnp.concatenate(blocks, axis=0))
        for shift in range(8):
            amount = 16 * shift
            if shift:
                rolled = [pltpu.roll(t, 128 - amount, 1) for t in tiles]
                joined = [
                    jnp.where(lane24 < 128 - amount, rolled[k], rolled[k + 1]) for k in range(4)
                ]
            else:
                joined = tiles
            for block in range(3):
                p = KWIN - 1 - 8 * block - shift
                for half in range(2):
                    bias[head, KWIN * p : KWIN * (p + 1), 128 * half : 128 * half + 128] = (
                        joined[block + half]
                    )

    def prepare_weights():
        qpad[0:CH, 0 : 3 * CH] = qkv_v[...]
        wqt[...] = mm_nt(one_hot((r == c) & (r < CH)), qpad[:, 0:256]).astype(BF16)
        wk[...] = mm(qpad[:, 128:384], one_hot((r == c + 52) & (c < CH))).astype(BF16)
        rv = iota((192, 384), 0)
        cv = iota((192, 384), 1)
        source = HEAD * lax.shift_right_logical(rv, 5) + (rv & 31)
        wvt[...] = mm_nt(one_hot((cv == source + 104) & ((rv & 31) < HEAD)), qpad[:, 256:640]).astype(BF16)

    def proj_weights():
        ppad[0:CH, 0:CH] = proj_v[...]
        source = HEAD * lax.shift_right_logical(r, 5) + (r & 31)
        pw[...] = mm(one_hot((c == source) & ((r & 31) < HEAD) & (r < 192)), ppad[...]).astype(BF16)
        hpad[0:CH, 0 : 2 * CH] = hid_v[...]

    def out_weights():
        opad[0:CH, 0 : 2 * CH] = outw_v[...]
        wout[...] = mm_nt(one_hot(iota((384, 384), 0) == iota((384, 384), 1)), opad[...]).astype(BF16)

    def conv_weights(a):
        for b in range(3):
            tap = 3 * a + b
            gpad[tap] = jnp.zeros((256, 256), BF16)
            gpad[tap, 0:CH, 0:CH] = gconv_v[a, b]
        bpad[a] = jnp.zeros((256, 256), BF16)
        upad[a, 192:256, :] = jnp.zeros((64, 256), BF16)
        order = 4 * (r & 63) + 2 * (lax.shift_right_logical(r, 6) & 1) + lax.shift_right_logical(r, 7)
        for b in range(3):
            bpad[a, 64 * b : 64 * (b + 1), 0:CH] = bconv_v[a, b]
        w2[a] = mm_nt(identity, bpad[a]).astype(BF16)
        w3[a] = mm_nt(one_hot(c == order), upad[a]).astype(BF16)

    late_weights = [
        proj_weights, out_weights, functools.partial(conv_weights, 0),
        functools.partial(conv_weights, 1), functools.partial(conv_weights, 2),
    ]
    arrive("qkv")
    prepare_weights()

    def halo_pixels(part):
        side, rim, has_side = ((halo_l, 0, has_left), (halo_r, 72, has_right))[part]
        groups = [
            (halo_t[part], has_up, [h * PITCH + 8 + 32 * part for h in range(4)]),
            (halo_b[part], has_down, [(20 + h) * PITCH + 8 + 32 * part for h in range(4)]),
            (side[...], has_side, [(4 + h) * PITCH + rim for h in range(TH)]),
            (halo_c[part], has_up & has_side, [h * PITCH + rim for h in range(4)]),
            (halo_c[2 + part], has_down & has_side, [(20 + h) * PITCH + rim for h in range(4)]),
        ]
        for packed, valid, starts in groups:
            x = unpack_pixels(packed, valid)
            width = x[0].shape[0] // len(starts)
            for k, start in enumerate(starts):
                for half in range(2):
                    fpad[half, pl.ds(start, width), :] = x[half][k * width : (k + 1) * width]
            store_normed(x, starts)

    inside = c < CH
    ones_row = (iota((192, KWIN * KWIN), 0) & 31) == HEAD
    tops = {}

    def pixels(ref, half, w, first_row, count_rows, first_col, count_cols):
        return jnp.concatenate(
            [
                ref[half, pl.ds((first_row + p) * PITCH + first_col + w * WIN, count_cols), :]
                for p in range(count_rows)
            ],
            axis=0,
        )

    def project_keys(w, spans):
        for first, count in spans:
            keys_in = jnp.concatenate(
                [pixels(npad, half, w, first, count, 4, KWIN).astype(BF16) for half in range(2)],
                axis=1,
            )
            rows = slice(KWIN * first, KWIN * (first + count))
            xwin[w, rows, :] = keys_in
            kwin[w, rows, :] = mm(keys_in, wk[...]).astype(BF16)

    def project_values(w):
        vwin[w] = jnp.where(ones_row, 1.0, mm_nt(wvt[...], xwin[w])).astype(BF16)

    def project_queries(w):
        query_in = jnp.concatenate(
            [pixels(npad, half, w, 4, WIN, 8, WIN).astype(BF16) for half in range(2)], axis=1
        )
        qwin[w] = mm_nt(wqt[...], query_in) * QSCALE

    whole_keys = ((0, 288), (288, 576))
    own_keys = ((96, 288), (288, 480))
    halo_keys = ((0, 96), (480, 576))
    inner_from = 2 * HEADS

    def slot(number):
        return number % 2 if number < inner_from else 2 + number - inner_from

    def score(number, w, head, spans):
        mine = (r >= HEAD * head) & (r < HEAD * (head + 1))
        q = jnp.where(mine, qwin[w], 0.0).astype(BF16)
        top = tops.get(number)
        for first, last in spans:
            scores = mm(kwin[w, first:last, :], q) + bias[head, first:last, :]
            sbuf[slot(number), first:last, :] = scores
            best = jnp.max(scores, axis=0, keepdims=True)
            top = best if top is None else jnp.maximum(top, best)
        tops[number] = top

    def exponent(number):
        pbuf[number % 2] = jnp.exp2(sbuf[slot(number)] - tops[number]).astype(BF16)

    def combine(number, w, head):
        rows = slice(SLOT * head, SLOT * (head + 1))
        mixed_values = mm(vwin[w, rows, :], pbuf[number % 2])
        attt[w, rows, :] = (mixed_values / mixed_values[HEAD : HEAD + 1, :]).astype(BF16)

    def merge_heads(w):
        attended = mm_nt(identity, attt[w]).astype(BF16)
        base = jnp.concatenate([pixels(fpad, half, w, 4, WIN, 8, WIN) for half in range(2)], axis=1)
        first = base + mm(attended, pw[0:192, :])
        fbuf[...] = first
        center = first - jnp.sum(first, axis=-1, keepdims=True) * (1.0 / CH)
        center = jnp.where(inside, center, 0.0)
        spread = jnp.sum(center * center, axis=-1, keepdims=True) * (1.0 / CH)
        second[...] = (center * lax.rsqrt(spread + 1e-05) * g2).astype(BF16)

    def hidden(part):
        lanes = slice(128 * part, 128 * part + 128)
        value = mm(second[...], hpad[:, lanes])
        inner[:, lanes] = (0.5 * value * (1.0 + lax.erf(value * math.sqrt(0.5)))).astype(BF16)

    def finish_window(w):
        mixed = fbuf[...] + mm(inner[...], wout[...])
        for i in range(WIN):
            block = mixed[WIN * i : WIN * (i + 1), :]
            rows = pl.ds((3 + i) * PITCH + 8 + w * WIN, WIN)
            mixpad[0, rows, :] = block[:, 0:128]
            mixpad[1, rows, :] = block[:, 128:256]
            mix_own[i, w * WIN : (w + 1) * WIN, :] = block.astype(BF16)
        if w == 0:
            mix_sl[...] = pack_pixels(*region(mixpad, 3, TH, 8, 8))
            mix_sc[0] = pack_pixels(*region(mixpad, 3, 4, 8, 8))
            mix_sc[2] = pack_pixels(*region(mixpad, 15, 4, 8, 8))
        if w == 3:
            mix_sr[...] = pack_pixels(*region(mixpad, 3, TH, 64, 8))
            mix_sc[1] = pack_pixels(*region(mixpad, 3, 4, 64, 8))
            mix_sc[3] = pack_pixels(*region(mixpad, 15, 4, 64, 8))
        start(mcopies[w])

    def strip(w):
        cols = slice(w * WIN, (w + 1) * WIN)
        return [
            (mix_own.at[0:3, cols], mix_b.at[:, cols], "u"),
            (mix_own.at[13:16, cols], mix_t.at[:, cols], "d"),
        ]

    specs = {
        0: [
            (mix_sl, mix_r, "l"),
            (mix_sc.at[0], mix_c.at[3], "ul"),
            (mix_sc.at[2], mix_c.at[1], "dl"),
        ] + strip(0),
        3: [
            (mix_sr, mix_l, "r"),
            (mix_sc.at[1], mix_c.at[2], "ur"),
            (mix_sc.at[3], mix_c.at[0], "dr"),
        ] + strip(3),
        1: strip(1),
        2: strip(2),
    }
    windows = (0, 3, 1, 2)
    every = exchange([item for w in windows for item in specs[w]], msend, mrecv)
    mcopies = {0: every[0:5], 3: every[5:10], 1: every[10:12], 2: every[12:14]}
    steps = [(w, head) for w in windows for head in range(HEADS)]

    def first_half():
        halo_pixels(0)
        project_keys(0, ((0, KWIN),))
        project_values(0)
        attend(0, 3)

    def second_half():
        halo_pixels(1)
        attend(3, len(steps) + 2)
        merge_heads(windows[-1])
        for part in range(3):
            hidden(part)
        finish_window(windows[-1])

    def attend(begin, end):
        for number in range(begin, end):
            turn, head = divmod(number, HEADS)
            if number < len(steps):
                inner_window = number >= inner_from
                score(number, windows[turn], head, halo_keys if inner_window else whole_keys)
            if 0 <= number - 1 < len(steps):
                exponent(number - 1)
            if 0 <= number - 2:
                combine(number - 2, *steps[number - 2])
            if turn + 1 < len(windows) and head == 3:
                project_keys(windows[turn + 1], ((0, 4), (20, 4)) if turn else ((0, KWIN),))
            if turn + 1 < len(windows) and head == 4:
                project_values(windows[turn + 1])
            if 0 < turn < len(windows):
                if head == 1:
                    merge_heads(windows[turn - 1])
                elif 2 <= head <= 4:
                    hidden(head - 2)
                elif head == 5:
                    finish_window(windows[turn - 1])

    def all_queries():
        for w in windows:
            project_queries(w)

    def own_scores():
        for w in windows[2:]:
            project_keys(w, ((4, TH),))
        picked = select_bias()
        head_bias(picked, 0)
        for head in range(HEADS):
            score(inner_from + head, windows[2], head, own_keys)
            if head + 1 < HEADS:
                head_bias(picked, head + 1)
            score(inner_from + HEADS + head, windows[3], head, own_keys)

    all_queries()
    arrive("table", "selector")
    own_scores()
    arrive("proj", "gain2", "hid", "outw", "gconv", "bconv", "uconv")
    g2 = lanes256(gain2_v)
    for prepare in late_weights:
        prepare()
    wait_recv(fcopies[k] for k in (0, 1, 2, 3, 4))
    first_half()
    wait_recv(fcopies[k] for k in (5, 6, 7, 8, 9))
    second_half()

    def store_mixed(start, count, values, valid):
        x = jnp.where(valid, values, 0.0)
        rows = pl.ds(start, count)
        mixpad[0, rows, :] = x[:, 0:128]
        mixpad[1, rows, :] = x[:, 128:256]

    def store_packed(packed, valid, starts, skip=0):
        x = unpack_pixels(packed, valid)
        for k, start in enumerate(starts):
            part = slice((k + skip) * 8, (k + skip + 1) * 8)
            for half in range(2):
                mixpad[half, pl.ds(start, 8), :] = x[half][part]

    def side_mixed():
        store_packed(mix_l[...], has_left, [(3 + h) * PITCH for h in range(TH)])
        store_packed(mix_r[...], has_right, [(3 + h) * PITCH + 72 for h in range(TH)])

    def top_mixed():
        for h in range(3):
            store_mixed(h * PITCH + 8, TW, mix_t[h].astype(F32), has_up)
        store_packed(mix_c[0], has_up & has_left, [h * PITCH for h in range(3)], 1)
        store_packed(mix_c[1], has_up & has_right, [h * PITCH + 72 for h in range(3)], 1)

    def bottom_mixed():
        for h in range(3):
            store_mixed((19 + h) * PITCH + 8, TW, mix_b[h].astype(F32), has_down)
        store_packed(mix_c[2], has_down & has_left, [(19 + h) * PITCH for h in range(3)])
        store_packed(mix_c[3], has_down & has_right, [(19 + h) * PITCH + 72 for h in range(3)])

    cols72 = iota((GP, 128), 0)
    gcols = ((cols72 >= 2) | has_left) & ((cols72 < 66) | has_right)
    lcols = ((cols72 >= 1) | has_left) & ((cols72 < 65) | has_right)

    def conv_group(h0, count):
        acc = None
        for a in range(3):
            for b in range(3):
                halves = []
                for half in range(2):
                    rows = [
                        mixpad[half, pl.ds((h0 + k + a) * PITCH + 5 + b, GP), :] for k in range(count)
                    ]
                    halves.append(jnp.concatenate(rows, axis=0).astype(BF16))
                term = mm(jnp.concatenate(halves, axis=1), gpad[3 * a + b])
                acc = term if acc is None else acc + term
        for k in range(count):
            h = h0 + k
            keep = gcols & has_up if h < 2 else gcols & has_down if h >= 18 else gcols
            for half in range(2):
                base = fpad[half, pl.ds((h + 2) * PITCH + 6, GP), :]
                value = base + acc[GP * k : GP * (k + 1), 128 * half : 128 * half + 128]
                gbuf[half, pl.ds(h * GP, GP), :] = jnp.where(keep, value, 0.0)

    low_lanes = iota((GP, 128), 1) < 64
    low64 = iota((TW, 128), 1) < 64

    def conv_before(first, count):
        start = first * GP
        acc = None
        for a in range(3):
            rows = pl.ds(start + a * GP, count * GP)
            lhs = jnp.concatenate([gbuf[half, rows, :].astype(BF16) for half in range(2)], axis=1)
            term = mm(lhs, w2[a])
            acc = term if acc is None else acc + term
        rows = pl.ds(start, count * GP)
        ybuf[0, rows, :] = acc[:, 0:128]
        ybuf[1, rows, :] = acc[:, 128:256]
        for h in range(first, first + count):
            start = h * GP
            value = (
                ybuf[0, pl.ds(start, GP), :]
                + pltpu.roll(ybuf[0, pl.ds(start + 1, GP), :], 64, 1)
                + ybuf[1, pl.ds(start + 2, GP), :]
            )
            value = jnp.where(value >= 0, value, 0.01 * value)
            keep = lcols & has_up if h < 1 else lcols & has_down if h >= 17 else lcols
            value = jnp.where(keep, value, 0.0)
            lbuf[pl.ds(start, GP), :] = jnp.where(low_lanes, value, pltpu.roll(value, 64, 1))
        for h in range(first, first + count):
            start = h * GP
            zero = lbuf[pl.ds(start, TW), :]
            one = lbuf[pl.ds(start + 1, TW), :]
            two = lbuf[pl.ds(start + 2, TW), :]
            l3[h, :, 0:128] = jnp.where(low64, zero, one).astype(BF16)
            l3[h, :, 128:256] = jnp.where(low64, two, 0.0).astype(BF16)

    target = 128 * (lax.shift_right_logical(r, 6) & 1) + 2 * (r & 63) + lax.shift_right_logical(r, 7)
    weave = one_hot(c == target)

    def conv_up(step):
        acc = None
        for a in range(3):
            rhs = jnp.concatenate([l3[4 * step + a + k] for k in range(4)], axis=0)
            term = mm_nt(w3[a], rhs)
            acc = term if acc is None else acc + term
        acc = acc.astype(BF16)
        for pair in range(2):
            lanes = slice(128 * pair, 128 * pair + 128)
            both = jnp.concatenate([acc[0:128, lanes], acc[128:256, lanes]], axis=1)
            woven = mm(both, weave)
            for k in range(2):
                for a in range(2):
                    line = (2 * (4 * step + 2 * pair + k) + a) % 16
                    obuf[step // 2, pl.ds(line, 64, stride=16), :] = woven[
                        64 * a : 64 * (a + 1), 128 * k : 128 * k + 128
                    ]

    def inner_rows():
        for h0 in (3, 5, 7, 9):
            conv_group(h0, 2)
        conv_before(3, 6)
        for h0 in (11, 13, 15):
            conv_group(h0, 2)
        conv_before(9, 6)
        conv_up(1)
        conv_up(2)

    def out_half(half):
        ostage[half] = obuf[half].reshape(64, 16, 128).astype(BF16)

    def end_rows():
        conv_group(0, 2)
        conv_group(2, 1)
        conv_group(17, 2)
        conv_before(0, 3)
        conv_group(19, 1)
        conv_before(15, 3)
        conv_up(0)
        conv_up(3)
        out_half(0)

    ybuf[:, 18 * GP :, :] = jnp.zeros((2, 8, 128), F32)
    wait_recv(every[k] for k in (0, 5))
    side_mixed()
    inner_rows()
    stores = [
        pltpu.make_async_copy(ostage.at[half], out.at[:, 16 * half : 16 * half + 16], osem.at[half])
        for half in range(2)
    ]
    wait_recv(every[k] for k in (1, 2, 3, 4, 6, 7, 8, 9, 10, 11, 12, 13))
    top_mixed()
    bottom_mixed()
    end_rows()
    stores[0].start()
    out_half(1)
    stores[1].start()
    for store in stores:
        store.wait()
    wait_send(fcopies + every)


def on_device(
    nr, nc, features, gain_one, qkv_weight, bias_table, proj_weight, gain_two,
    hidden_weight, output_weight, group_conv, before_conv, upsample_conv,
):
    selector = jnp.asarray(table_selector(), BF16)
    operands = (
        features, gain_one, qkv_weight, bias_table.T, proj_weight, gain_two, hidden_weight,
        output_weight.T, group_conv, before_conv.transpose(0, 1, 3, 2),
        upsample_conv.reshape(3, 192, 256), selector,
    )
    any_space = pl.BlockSpec(memory_space=pl.ANY)
    staged = [pltpu.VMEM(x.shape, x.dtype) for x in operands]
    staged[10] = pltpu.VMEM((3, 256, 256), BF16)
    scratch = staged + [
        pltpu.VMEM((2, 192, 128), BF16), pltpu.VMEM((2, 192, 128), BF16),
        pltpu.VMEM((192, 128), BF16), pltpu.VMEM((192, 128), BF16), pltpu.VMEM((4, 48, 128), BF16),
        pltpu.VMEM((2, 192, 128), BF16), pltpu.VMEM((2, 192, 128), BF16),
        pltpu.VMEM((192, 128), BF16), pltpu.VMEM((192, 128), BF16), pltpu.VMEM((4, 48, 128), BF16),
        pltpu.VMEM((3, TW, 256), BF16), pltpu.VMEM((3, TW, 256), BF16),
        pltpu.VMEM((192, 128), BF16), pltpu.VMEM((192, 128), BF16), pltpu.VMEM((4, 48, 128), BF16),
        pltpu.VMEM((192, 128), BF16), pltpu.VMEM((192, 128), BF16), pltpu.VMEM((4, 48, 128), BF16),
        pltpu.VMEM((TH, TW, 256), BF16),
        pltpu.VMEM((2, 24 * PITCH, 128), F32), pltpu.VMEM((2, 24 * PITCH, 128), F32),
        pltpu.VMEM((2, 22 * PITCH, 128), F32), pltpu.VMEM((2, 20 * GP, 128), F32),
        pltpu.VMEM((2, 18 * GP + 8, 128), F32), pltpu.VMEM((18 * GP + 8, 128), F32),
        pltpu.VMEM((18, TW, 256), BF16),
        pltpu.VMEM((256, 640), BF16), pltpu.VMEM((256, 256), BF16), pltpu.VMEM((256, 256), BF16),
        pltpu.VMEM((192, 256), BF16), pltpu.VMEM((256, 256), BF16), pltpu.VMEM((256, 256), BF16),
        pltpu.VMEM((256, 384), BF16), pltpu.VMEM((256, 384), BF16), pltpu.VMEM((384, 256), BF16),
        pltpu.VMEM((9, 256, 256), BF16), pltpu.VMEM((3, 256, 256), BF16),
        pltpu.VMEM((3, 256, 256), BF16), pltpu.VMEM((3, 256, 256), BF16),
        pltpu.VMEM((HEADS, KWIN * KWIN, 256), F32), pltpu.VMEM((4, KWIN * KWIN, 256), BF16),
        pltpu.VMEM((4, KWIN * KWIN, 256), BF16), pltpu.VMEM((4, 192, KWIN * KWIN), BF16),
        pltpu.VMEM((4, 256, 256), F32), pltpu.VMEM((14, KWIN * KWIN, 256), F32),
        pltpu.VMEM((2, KWIN * KWIN, 256), BF16), pltpu.VMEM((4, 192, 256), BF16),
        pltpu.VMEM((256, 256), F32), pltpu.VMEM((256, 256), BF16), pltpu.VMEM((256, 384), BF16),
        pltpu.VMEM((2, 64 * 16, 128), F32), pltpu.VMEM((2, 64, 16, 128), BF16),
        pltpu.SemaphoreType.DMA((2,)),
        pltpu.SemaphoreType.DMA((12,)), pltpu.SemaphoreType.DMA((10,)), pltpu.SemaphoreType.DMA((10,)),
        pltpu.SemaphoreType.DMA((14,)), pltpu.SemaphoreType.DMA((14,)),
    ]
    result = pl.pallas_call(
        functools.partial(kernel, nr, nc),
        out_shape=pltpu.VMEM((64, 2 * TH, 2 * TW), BF16),
        in_specs=[any_space] * len(operands),
        out_specs=pl.BlockSpec(memory_space=pl.ANY),
        scratch_shapes=scratch,
        compiler_params=pltpu.CompilerParams(
            collective_id=0, has_side_effects=True, vmem_limit_bytes=62 * 1024 * 1024
        ),
    )(*operands)
    return result


def solution(mesh):
    placed = (P("rows", "cols", None),) + (P(),) * 10
    body = functools.partial(on_device, mesh.shape["rows"], mesh.shape["cols"])
    return jax.shard_map(
        body, mesh=mesh, in_specs=placed, out_specs=P(None, "rows", "cols"), check_vma=False
    )
```

```python
import functools
import math

import jax
import jax.numpy as jnp
import numpy as np
from jax import lax
from jax.experimental import pallas as pl
from jax.experimental.pallas import tpu as pltpu
from jax.sharding import PartitionSpec as P

HEADS = 6
HEAD = 30
SLOT = 32
CH = 180
WIN = 16
KWIN = 24
SIDE = WIN + KWIN - 1
TABLE = SIDE * SIDE
TH = 16
TW = 64
PITCH = 80
GP = 72
QSCALE = math.log2(math.e) / math.sqrt(HEAD)
LOG2E = math.log2(math.e)
F32 = jnp.float32
BF16 = jnp.bfloat16
MESH = pl.DeviceIdType.MESH
NT = (((1,), (1,)), ((), ()))


def table_selector():
    out = np.zeros((384, 384), np.float32)
    for lane in range(128):
        for part in range(3):
            entry = 16 * part + lane % 16
            if entry < SIDE:
                out[SIDE * (7 - lane // 16) + SIDE - 1 - entry, 128 * part + lane] = 1.0
    return out


def mm(a, b):
    return jnp.dot(a, b, preferred_element_type=F32)


def mm_nt(a, b):
    return lax.dot_general(a, b, NT, preferred_element_type=F32)


def iota(shape, dim):
    return lax.broadcasted_iota(jnp.int32, shape, dim)


def one_hot(mask):
    return jnp.where(mask, 1.0, 0.0).astype(BF16)


def normalize(x, gain):
    lane = iota(x[1].shape, 1)
    mean = jnp.sum(x[0] + x[1], axis=-1, keepdims=True) * (1.0 / CH)
    low = x[0] - mean
    high = jnp.where(lane < CH - 128, x[1] - mean, 0.0)
    spread = jnp.sum(low * low + high * high, axis=-1, keepdims=True) * (1.0 / CH)
    scale = lax.rsqrt(spread + 1e-05)
    return low * scale * gain[:, 0:128], high * scale * gain[:, 128:256]


def pack_pixels(low, high):
    half = low.shape[0] // 2
    lane = iota((half, 128), 1)
    joined = jnp.where(lane < 64, high[:half], pltpu.roll(high[half:], 64, 1))
    return jnp.concatenate([low, joined], axis=0).astype(BF16)


def unpack_pixels(packed, valid):
    count = packed.shape[0] * 2 // 3
    x = jnp.where(valid, packed.astype(F32), 0.0)
    joined = x[count:]
    high = jnp.concatenate([joined, pltpu.roll(joined, 64, 1)], axis=0)
    return x[:count], jnp.where(iota(high.shape, 1) < CH - 128, high, 0.0)


def kernel(
    nr, nc,
    feat, gain1, qkv, table, proj, gain2, hid, outw, gconv, bconv, uconv, selector,
    out,
    feat_v, gain1_v, qkv_v, table_v, proj_v, gain2_v, hid_v, outw_v, gconv_v, bconv_v, upad, sel_v,
    send_t, send_b, send_l, send_r, send_c, halo_t, halo_b, halo_l, halo_r, halo_c,
    mix_t, mix_b, mix_l, mix_r, mix_c, mix_sl, mix_sr, mix_sc, mix_own,
    fpad, npad, mixpad, gbuf, ybuf, lbuf, l3,
    qpad, wqt, wk, wvt, ppad, pw, hpad, opad, wout, gpad, bpad, w2, w3, bias, xwin, kwin, vwin, qwin, sbuf, pbuf, attt, fbuf, second, inner, obuf, ostage, osem,
    local_sem, fsend, frecv, msend, mrecv,
):
    row = lax.axis_index("rows")
    col = lax.axis_index("cols")
    up = lax.rem(row + nr - 1, nr)
    down = lax.rem(row + 1, nr)
    left = lax.rem(col + nc - 1, nc)
    right = lax.rem(col + 1, nc)
    has_up = row > 0
    has_down = row < nr - 1
    has_left = col > 0
    has_right = col < nc - 1
    place = {
        "u": ((up, col), has_up), "d": ((down, col), has_down),
        "l": ((row, left), has_left), "r": ((row, right), has_right),
        "ul": ((up, left), has_up & has_left), "ur": ((up, right), has_up & has_right),
        "dl": ((down, left), has_down & has_left), "dr": ((down, right), has_down & has_right),
    }
    opposite = {"u": "d", "d": "u", "l": "r", "r": "l", "ul": "dr", "dr": "ul", "ur": "dl", "dl": "ur"}
    barrier = pltpu.get_barrier_semaphore()
    expected = 0
    for device, exists in place.values():
        expected = expected + jnp.where(exists, 1, 0)

        @pl.when(exists)
        def _(device=device):
            pl.semaphore_signal(barrier, inc=1, device_id=device, device_id_type=MESH)

    local = {}
    pairs = [
        ("feat", feat, feat_v), ("gain1", gain1, gain1_v), ("table", table, table_v),
        ("selector", selector, sel_v), ("qkv", qkv, qkv_v), ("proj", proj, proj_v),
        ("gain2", gain2, gain2_v), ("hid", hid, hid_v), ("outw", outw, outw_v),
        ("gconv", gconv, gconv_v), ("bconv", bconv, bconv_v), ("uconv", uconv, upad.at[:, 0:192, :]),
    ]
    for number, (name, source, target) in enumerate(pairs):
        local[name] = pltpu.make_async_copy(source, target, local_sem.at[number])
    for name in ("feat", "gain1", "table", "selector"):
        local[name].start()

    def arrive(*names):
        for name in names:
            local[name].wait()

    def exchange(specs, send_sem, recv_sem):
        copies = []
        for number, (source, target, way) in enumerate(specs):
            copy = pltpu.make_async_remote_copy(
                src_ref=source, dst_ref=target, send_sem=send_sem.at[number],
                recv_sem=recv_sem.at[number], device_id=place[way][0], device_id_type=MESH,
            )
            copies.append((copy, place[way][1], place[opposite[way]][1]))
        return copies

    def start(copies):
        for copy, sends, _ in copies:
            pl.when(sends)(copy.start)

    def wait_recv(copies):
        for copy, _, receives in copies:
            pl.when(receives)(copy.wait_recv)

    def wait_send(copies):
        for copy, sends, _ in copies:
            pl.when(sends)(copy.wait_send)

    fcopies = exchange(
        [
            (send_b.at[0], halo_t.at[0], "d"),
            (send_r, halo_l, "r"),
            (send_t.at[0], halo_b.at[0], "u"),
            (send_c.at[3], halo_c.at[0], "dr"),
            (send_c.at[1], halo_c.at[2], "ur"),
            (send_b.at[1], halo_t.at[1], "d"),
            (send_l, halo_r, "l"),
            (send_t.at[1], halo_b.at[1], "u"),
            (send_c.at[0], halo_c.at[3], "ul"),
            (send_c.at[2], halo_c.at[1], "dl"),
        ],
        fsend, frecv,
    )

    fpad[1] = jnp.zeros(fpad.shape[1:], F32)
    arrive("feat", "gain1")
    for h in range(0, TH, 4):
        x = feat_v[h : h + 4].astype(F32).reshape(4 * TW, CH)
        for k in range(4):
            rows = pl.ds((h + k + 4) * PITCH + 8, TW)
            fpad[0, rows, :] = x[k * TW : (k + 1) * TW, 0:128]
            fpad[1, rows, 0 : CH - 128] = x[k * TW : (k + 1) * TW, 128:CH]

    def region(ref, first_row, count_rows, first_col, count_cols):
        return [
            jnp.concatenate(
                [
                    ref[half, pl.ds((first_row + k) * PITCH + first_col, count_cols), :]
                    for k in range(count_rows)
                ],
                axis=0,
            )
            for half in range(2)
        ]

    corner_place = ((4, 8), (4, 64), (16, 8), (16, 64))
    pl.semaphore_wait(barrier, expected)
    for part, corners in ((0, (3, 1)), (1, (0, 2))):
        send_b[part] = pack_pixels(*region(fpad, 16, 4, 8 + 32 * part, 32))
        start(fcopies[5 * part : 5 * part + 1])
        if part == 0:
            send_r[...] = pack_pixels(*region(fpad, 4, TH, 64, 8))
        else:
            send_l[...] = pack_pixels(*region(fpad, 4, TH, 8, 8))
        send_t[part] = pack_pixels(*region(fpad, 4, 4, 8 + 32 * part, 32))
        start(fcopies[5 * part + 1 : 5 * part + 3])
        for corner in corners:
            first_row, first_col = corner_place[corner]
            send_c[corner] = pack_pixels(*region(fpad, first_row, 4, first_col, 8))
        start(fcopies[5 * part + 3 : 5 * part + 5])
    for name in ("qkv", "proj", "gain2", "hid", "outw", "gconv", "bconv", "uconv"):
        local[name].start()

    def lanes256(ref):
        return jnp.concatenate([ref[...].reshape(1, CH), jnp.zeros((1, 256 - CH), F32)], axis=1)

    g1 = lanes256(gain1_v)

    def store_normed(x, starts):
        n = normalize(x, g1)
        width = x[0].shape[0] // len(starts)
        for k, start in enumerate(starts):
            for half in range(2):
                npad[half, pl.ds(start, width), :] = n[half][k * width : (k + 1) * width]

    def own_pixels():
        for h in range(0, TH, 4):
            store_normed(
                region(fpad, h + 4, 4, 8, TW), [(h + k + 4) * PITCH + 8 for k in range(4)]
            )

    own_pixels()
    for ref in (qpad, ppad, hpad, opad):
        ref[...] = jnp.zeros(ref.shape, ref.dtype)

    r = iota((256, 256), 0)
    c = iota((256, 256), 1)
    identity = one_hot(r == c)

    def select_bias():
        whole = jnp.concatenate(
            [table_v[...] * LOG2E, jnp.zeros((HEADS, 1536 - TABLE), F32)], axis=1
        )
        whole = jnp.concatenate([whole, jnp.zeros((2, 1536), F32)], axis=0)
        pieces = []
        for tile in range(5):
            first = SIDE * (SIDE - 8 - 8 * tile)
            pieces.append(pltpu.roll(whole, (1536 - first) % 1536, 1)[:, 0:384])
        rows = jnp.concatenate(pieces, axis=0)
        hi = rows.astype(BF16)
        rest = rows - hi.astype(F32)
        mid = rest.astype(BF16)
        low = (rest - mid.astype(F32)).astype(BF16)
        picked = mm(hi, sel_v[...]) + mm(mid, sel_v[...]) + mm(low, sel_v[...])
        return picked

    lane8 = iota((8, 128), 1)
    sub8 = iota((8, 128), 0)
    lane24 = iota((KWIN, 128), 1)

    def head_bias(picked, head):
        tiles = []
        for tile in range(5):
            z = picked[8 * tile + head : 8 * tile + head + 1, :]
            blocks = []
            for part, base in ((1, 7), (0, 15), (0, 7)):
                first = jnp.broadcast_to(z[:, 128 * part : 128 * part + 128], (8, 128))
                second = jnp.broadcast_to(z[:, 128 * part + 128 : 128 * part + 256], (8, 128))
                first = pltpu.roll(first, 128 - base, 1, stride=1, stride_axis=0)
                second = pltpu.roll(second, 16 - base, 1, stride=1, stride_axis=0)
                blocks.append(jnp.where((lane8 & 15) + base - sub8 < 16, first, second))
            tiles.append(jnp.concatenate(blocks, axis=0))
        for shift in range(8):
            amount = 16 * shift
            if shift:
                rolled = [pltpu.roll(t, 128 - amount, 1) for t in tiles]
                joined = [
                    jnp.where(lane24 < 128 - amount, rolled[k], rolled[k + 1]) for k in range(4)
                ]
            else:
                joined = tiles
            for block in range(3):
                p = KWIN - 1 - 8 * block - shift
                for half in range(2):
                    bias[head, KWIN * p : KWIN * (p + 1), 128 * half : 128 * half + 128] = (
                        joined[block + half]
                    )

    def prepare_weights():
        qpad[0:CH, 0 : 3 * CH] = qkv_v[...]
        wqt[...] = mm_nt(one_hot((r == c) & (r < CH)), qpad[:, 0:256]).astype(BF16)
        wk[...] = mm(qpad[:, 128:384], one_hot((r == c + 52) & (c < CH))).astype(BF16)
        rv = iota((192, 384), 0)
        cv = iota((192, 384), 1)
        source = HEAD * lax.shift_right_logical(rv, 5) + (rv & 31)
        wvt[...] = mm_nt(one_hot((cv == source + 104) & ((rv & 31) < HEAD)), qpad[:, 256:640]).astype(BF16)

    def proj_weights():
        ppad[0:CH, 0:CH] = proj_v[...]
        source = HEAD * lax.shift_right_logical(r, 5) + (r & 31)
        pw[...] = mm(one_hot((c == source) & ((r & 31) < HEAD) & (r < 192)), ppad[...]).astype(BF16)
        hpad[0:CH, 0 : 2 * CH] = hid_v[...]

    def out_weights():
        opad[0:CH, 0 : 2 * CH] = outw_v[...]
        wout[...] = mm_nt(one_hot(iota((384, 384), 0) == iota((384, 384), 1)), opad[...]).astype(BF16)

    def conv_weights(a):
        for b in range(3):
            tap = 3 * a + b
            gpad[tap] = jnp.zeros((256, 256), BF16)
            gpad[tap, 0:CH, 0:CH] = gconv_v[a, b]
        bpad[a] = jnp.zeros((256, 256), BF16)
        upad[a, 192:256, :] = jnp.zeros((64, 256), BF16)
        order = 4 * (r & 63) + 2 * (lax.shift_right_logical(r, 6) & 1) + lax.shift_right_logical(r, 7)
        for b in range(3):
            bpad[a, 64 * b : 64 * (b + 1), 0:CH] = bconv_v[a, b]
        w2[a] = mm_nt(identity, bpad[a]).astype(BF16)
        w3[a] = mm_nt(one_hot(c == order), upad[a]).astype(BF16)

    late_weights = [
        proj_weights, out_weights, functools.partial(conv_weights, 0),
        functools.partial(conv_weights, 1), functools.partial(conv_weights, 2),
    ]
    arrive("qkv")
    prepare_weights()

    def halo_pixels(part):
        side, rim, has_side = ((halo_l, 0, has_left), (halo_r, 72, has_right))[part]
        groups = [
            (halo_t[part], has_up, [h * PITCH + 8 + 32 * part for h in range(4)]),
            (halo_b[part], has_down, [(20 + h) * PITCH + 8 + 32 * part for h in range(4)]),
            (side[...], has_side, [(4 + h) * PITCH + rim for h in range(TH)]),
            (halo_c[part], has_up & has_side, [h * PITCH + rim for h in range(4)]),
            (halo_c[2 + part], has_down & has_side, [(20 + h) * PITCH + rim for h in range(4)]),
        ]
        for packed, valid, starts in groups:
            x = unpack_pixels(packed, valid)
            width = x[0].shape[0] // len(starts)
            for k, start in enumerate(starts):
                for half in range(2):
                    fpad[half, pl.ds(start, width), :] = x[half][k * width : (k + 1) * width]
            store_normed(x, starts)

    inside = c < CH
    ones_row = (iota((192, KWIN * KWIN), 0) & 31) == HEAD
    tops = {}

    def pixels(ref, half, w, first_row, count_rows, first_col, count_cols):
        return jnp.concatenate(
            [
                ref[half, pl.ds((first_row + p) * PITCH + first_col + w * WIN, count_cols), :]
                for p in range(count_rows)
            ],
            axis=0,
        )

    def project_keys(w, spans):
        for first, count in spans:
            keys_in = jnp.concatenate(
                [pixels(npad, half, w, first, count, 4, KWIN).astype(BF16) for half in range(2)],
                axis=1,
            )
            rows = slice(KWIN * first, KWIN * (first + count))
            xwin[w, rows, :] = keys_in
            kwin[w, rows, :] = mm(keys_in, wk[...]).astype(BF16)

    def project_values(w):
        vwin[w] = jnp.where(ones_row, 1.0, mm_nt(wvt[...], xwin[w])).astype(BF16)

    def project_queries(w):
        query_in = jnp.concatenate(
            [pixels(npad, half, w, 4, WIN, 8, WIN).astype(BF16) for half in range(2)], axis=1
        )
        qwin[w] = mm_nt(wqt[...], query_in) * QSCALE

    whole_keys = ((0, 288), (288, 576))
    own_keys = ((96, 288), (288, 480))
    halo_keys = ((0, 96), (480, 576))
    inner_from = 2 * HEADS

    def slot(number):
        return number % 2 if number < inner_from else 2 + number - inner_from

    def score(number, w, head, spans):
        mine = (r >= HEAD * head) & (r < HEAD * (head + 1))
        q = jnp.where(mine, qwin[w], 0.0).astype(BF16)
        top = tops.get(number)
        for first, last in spans:
            scores = mm(kwin[w, first:last, :], q) + bias[head, first:last, :]
            sbuf[slot(number), first:last, :] = scores
            best = jnp.max(scores, axis=0, keepdims=True)
            top = best if top is None else jnp.maximum(top, best)
        tops[number] = top

    def exponent(number):
        pbuf[number % 2] = jnp.exp2(sbuf[slot(number)] - tops[number]).astype(BF16)

    def combine(number, w, head):
        rows = slice(SLOT * head, SLOT * (head + 1))
        mixed_values = mm(vwin[w, rows, :], pbuf[number % 2])
        attt[w, rows, :] = (mixed_values / mixed_values[HEAD : HEAD + 1, :]).astype(BF16)

    def merge_heads(w):
        attended = mm_nt(identity, attt[w]).astype(BF16)
        base = jnp.concatenate([pixels(fpad, half, w, 4, WIN, 8, WIN) for half in range(2)], axis=1)
        first = base + mm(attended, pw[0:192, :])
        fbuf[...] = first
        center = first - jnp.sum(first, axis=-1, keepdims=True) * (1.0 / CH)
        center = jnp.where(inside, center, 0.0)
        spread = jnp.sum(center * center, axis=-1, keepdims=True) * (1.0 / CH)
        second[...] = (center * lax.rsqrt(spread + 1e-05) * g2).astype(BF16)

    def hidden(part):
        lanes = slice(128 * part, 128 * part + 128)
        value = mm(second[...], hpad[:, lanes])
        inner[:, lanes] = (0.5 * value * (1.0 + lax.erf(value * math.sqrt(0.5)))).astype(BF16)

    def finish_window(w):
        mixed = fbuf[...] + mm(inner[...], wout[...])
        for i in range(WIN):
            block = mixed[WIN * i : WIN * (i + 1), :]
            rows = pl.ds((3 + i) * PITCH + 8 + w * WIN, WIN)
            mixpad[0, rows, :] = block[:, 0:128]
            mixpad[1, rows, :] = block[:, 128:256]
            mix_own[i, w * WIN : (w + 1) * WIN, :] = block.astype(BF16)
        if w == 0:
            mix_sl[...] = pack_pixels(*region(mixpad, 3, TH, 8, 8))
            mix_sc[0] = pack_pixels(*region(mixpad, 3, 4, 8, 8))
            mix_sc[2] = pack_pixels(*region(mixpad, 15, 4, 8, 8))
        if w == 3:
            mix_sr[...] = pack_pixels(*region(mixpad, 3, TH, 64, 8))
            mix_sc[1] = pack_pixels(*region(mixpad, 3, 4, 64, 8))
            mix_sc[3] = pack_pixels(*region(mixpad, 15, 4, 64, 8))
        start(mcopies[w] if w in (0, 3) else mcopies[w][::-1])

    def strip(w):
        cols = slice(w * WIN, (w + 1) * WIN)
        return [
            (mix_own.at[0:3, cols], mix_b.at[:, cols], "u"),
            (mix_own.at[13:16, cols], mix_t.at[:, cols], "d"),
        ]

    specs = {
        0: [
            (mix_sl, mix_r, "l"),
            (mix_sc.at[0], mix_c.at[3], "ul"),
            (mix_sc.at[2], mix_c.at[1], "dl"),
        ] + strip(0),
        3: [
            (mix_sr, mix_l, "r"),
            (mix_sc.at[1], mix_c.at[2], "ur"),
            (mix_sc.at[3], mix_c.at[0], "dr"),
        ] + strip(3),
        1: strip(1),
        2: strip(2),
    }
    windows = (0, 3, 1, 2)
    every = exchange([item for w in windows for item in specs[w]], msend, mrecv)
    mcopies = {0: every[0:5], 3: every[5:10], 1: every[10:12], 2: every[12:14]}
    steps = [(w, head) for w in windows for head in range(HEADS)]

    def first_half():
        halo_pixels(0)
        project_keys(0, ((0, KWIN),))
        project_values(0)
        attend(0, 3)

    def second_half():
        halo_pixels(1)
        attend(3, len(steps) + 2)
        merge_heads(windows[-1])
        for part in range(3):
            hidden(part)
        finish_window(windows[-1])

    def attend(begin, end):
        for number in range(begin, end):
            turn, head = divmod(number, HEADS)
            if number < len(steps):
                inner_window = number >= inner_from
                score(number, windows[turn], head, halo_keys if inner_window else whole_keys)
            if 0 <= number - 1 < len(steps):
                exponent(number - 1)
            if 0 <= number - 2:
                combine(number - 2, *steps[number - 2])
            if turn + 1 < len(windows) and head == 3:
                project_keys(windows[turn + 1], ((0, 4), (20, 4)) if turn else ((0, KWIN),))
            if turn + 1 < len(windows) and head == 4:
                project_values(windows[turn + 1])
            if 0 < turn < len(windows):
                if head == 1:
                    merge_heads(windows[turn - 1])
                elif 2 <= head <= 4:
                    hidden(head - 2)
                elif head == 5:
                    finish_window(windows[turn - 1])

    def all_queries():
        for w in windows:
            project_queries(w)

    def own_scores():
        for w in windows[2:]:
            project_keys(w, ((4, TH),))
        picked = select_bias()
        head_bias(picked, 0)
        for head in range(HEADS):
            score(inner_from + head, windows[2], head, own_keys)
            if head + 1 < HEADS:
                head_bias(picked, head + 1)
            score(inner_from + HEADS + head, windows[3], head, own_keys)

    all_queries()
    arrive("table", "selector")
    own_scores()
    arrive("proj", "gain2", "hid", "outw", "gconv", "bconv", "uconv")
    g2 = lanes256(gain2_v)
    for prepare in late_weights:
        prepare()
    wait_recv(fcopies[k] for k in (0, 1, 2, 3, 4))
    first_half()
    wait_recv(fcopies[k] for k in (5, 6, 7, 8, 9))
    second_half()

    def store_mixed(start, count, values, valid):
        x = jnp.where(valid, values, 0.0)
        rows = pl.ds(start, count)
        mixpad[0, rows, :] = x[:, 0:128]
        mixpad[1, rows, :] = x[:, 128:256]

    def store_packed(packed, valid, starts, skip=0):
        x = unpack_pixels(packed, valid)
        for k, start in enumerate(starts):
            part = slice((k + skip) * 8, (k + skip + 1) * 8)
            for half in range(2):
                mixpad[half, pl.ds(start, 8), :] = x[half][part]

    def side_mixed():
        store_packed(mix_l[...], has_left, [(3 + h) * PITCH for h in range(TH)])
        store_packed(mix_r[...], has_right, [(3 + h) * PITCH + 72 for h in range(TH)])

    def top_mixed():
        for h in range(3):
            store_mixed(h * PITCH + 8, TW, mix_t[h].astype(F32), has_up)
        store_packed(mix_c[0], has_up & has_left, [h * PITCH for h in range(3)], 1)
        store_packed(mix_c[1], has_up & has_right, [h * PITCH + 72 for h in range(3)], 1)

    def bottom_mixed():
        for h in range(3):
            store_mixed((19 + h) * PITCH + 8, TW, mix_b[h].astype(F32), has_down)
        store_packed(mix_c[2], has_down & has_left, [(19 + h) * PITCH for h in range(3)])
        store_packed(mix_c[3], has_down & has_right, [(19 + h) * PITCH + 72 for h in range(3)])

    cols72 = iota((GP, 128), 0)
    gcols = ((cols72 >= 2) | has_left) & ((cols72 < 66) | has_right)
    lcols = ((cols72 >= 1) | has_left) & ((cols72 < 65) | has_right)

    def conv_group(h0, count):
        acc = None
        for a in range(3):
            for b in range(3):
                halves = []
                for half in range(2):
                    rows = [
                        mixpad[half, pl.ds((h0 + k + a) * PITCH + 5 + b, GP), :] for k in range(count)
                    ]
                    halves.append(jnp.concatenate(rows, axis=0).astype(BF16))
                term = mm(jnp.concatenate(halves, axis=1), gpad[3 * a + b])
                acc = term if acc is None else acc + term
        for k in range(count):
            h = h0 + k
            keep = gcols & has_up if h < 2 else gcols & has_down if h >= 18 else gcols
            for half in range(2):
                base = fpad[half, pl.ds((h + 2) * PITCH + 6, GP), :]
                value = base + acc[GP * k : GP * (k + 1), 128 * half : 128 * half + 128]
                gbuf[half, pl.ds(h * GP, GP), :] = jnp.where(keep, value, 0.0)

    low_lanes = iota((GP, 128), 1) < 64
    low64 = iota((TW, 128), 1) < 64

    def conv_before(first, count):
        start = first * GP
        acc = None
        for a in range(3):
            rows = pl.ds(start + a * GP, count * GP)
            lhs = jnp.concatenate([gbuf[half, rows, :].astype(BF16) for half in range(2)], axis=1)
            term = mm(lhs, w2[a])
            acc = term if acc is None else acc + term
        rows = pl.ds(start, count * GP)
        ybuf[0, rows, :] = acc[:, 0:128]
        ybuf[1, rows, :] = acc[:, 128:256]
        for h in range(first, first + count):
            start = h * GP
            value = (
                ybuf[0, pl.ds(start, GP), :]
                + pltpu.roll(ybuf[0, pl.ds(start + 1, GP), :], 64, 1)
                + ybuf[1, pl.ds(start + 2, GP), :]
            )
            value = jnp.where(value >= 0, value, 0.01 * value)
            keep = lcols & has_up if h < 1 else lcols & has_down if h >= 17 else lcols
            value = jnp.where(keep, value, 0.0)
            lbuf[pl.ds(start, GP), :] = jnp.where(low_lanes, value, pltpu.roll(value, 64, 1))
        for h in range(first, first + count):
            start = h * GP
            zero = lbuf[pl.ds(start, TW), :]
            one = lbuf[pl.ds(start + 1, TW), :]
            two = lbuf[pl.ds(start + 2, TW), :]
            l3[h, :, 0:128] = jnp.where(low64, zero, one).astype(BF16)
            l3[h, :, 128:256] = jnp.where(low64, two, 0.0).astype(BF16)

    target = 128 * (lax.shift_right_logical(r, 6) & 1) + 2 * (r & 63) + lax.shift_right_logical(r, 7)
    weave = one_hot(c == target)

    def conv_up(step):
        acc = None
        for a in range(3):
            rhs = jnp.concatenate([l3[4 * step + a + k] for k in range(4)], axis=0)
            term = mm_nt(w3[a], rhs)
            acc = term if acc is None else acc + term
        acc = acc.astype(BF16)
        for pair in range(2):
            lanes = slice(128 * pair, 128 * pair + 128)
            both = jnp.concatenate([acc[0:128, lanes], acc[128:256, lanes]], axis=1)
            woven = mm(both, weave)
            for k in range(2):
                for a in range(2):
                    line = (2 * (4 * step + 2 * pair + k) + a) % 16
                    obuf[step // 2, pl.ds(line, 64, stride=16), :] = woven[
                        64 * a : 64 * (a + 1), 128 * k : 128 * k + 128
                    ]

    def inner_rows():
        for h0 in (3, 5, 7, 9):
            conv_group(h0, 2)
        conv_before(3, 6)
        for h0 in (11, 13, 15):
            conv_group(h0, 2)
        conv_before(9, 6)
        conv_up(1)
        conv_up(2)

    def out_half(half):
        ostage[half] = obuf[half].reshape(64, 16, 128).astype(BF16)

    def end_rows():
        conv_group(0, 2)
        conv_group(2, 1)
        conv_group(17, 2)
        conv_before(0, 3)
        conv_group(19, 1)
        conv_before(15, 3)
        conv_up(0)
        conv_up(3)
        out_half(0)

    ybuf[:, 18 * GP :, :] = jnp.zeros((2, 8, 128), F32)
    wait_recv(every[k] for k in (0, 5))
    side_mixed()
    inner_rows()
    stores = [
        pltpu.make_async_copy(ostage.at[half], out.at[:, 16 * half : 16 * half + 16], osem.at[half])
        for half in range(2)
    ]
    wait_recv(every[k] for k in (1, 2, 3, 4, 6, 7, 8, 9, 10, 11, 12, 13))
    top_mixed()
    bottom_mixed()
    end_rows()
    stores[0].start()
    out_half(1)
    stores[1].start()
    for store in stores:
        store.wait()
    wait_send(fcopies + every)


def on_device(
    nr, nc, features, gain_one, qkv_weight, bias_table, proj_weight, gain_two,
    hidden_weight, output_weight, group_conv, before_conv, upsample_conv,
):
    selector = jnp.asarray(table_selector(), BF16)
    operands = (
        features, gain_one, qkv_weight, bias_table.T, proj_weight, gain_two, hidden_weight,
        output_weight.T, group_conv, before_conv.transpose(0, 1, 3, 2),
        upsample_conv.reshape(3, 192, 256), selector,
    )
    any_space = pl.BlockSpec(memory_space=pl.ANY)
    staged = [pltpu.VMEM(x.shape, x.dtype) for x in operands]
    staged[10] = pltpu.VMEM((3, 256, 256), BF16)
    scratch = staged + [
        pltpu.VMEM((2, 192, 128), BF16), pltpu.VMEM((2, 192, 128), BF16),
        pltpu.VMEM((192, 128), BF16), pltpu.VMEM((192, 128), BF16), pltpu.VMEM((4, 48, 128), BF16),
        pltpu.VMEM((2, 192, 128), BF16), pltpu.VMEM((2, 192, 128), BF16),
        pltpu.VMEM((192, 128), BF16), pltpu.VMEM((192, 128), BF16), pltpu.VMEM((4, 48, 128), BF16),
        pltpu.VMEM((3, TW, 256), BF16), pltpu.VMEM((3, TW, 256), BF16),
        pltpu.VMEM((192, 128), BF16), pltpu.VMEM((192, 128), BF16), pltpu.VMEM((4, 48, 128), BF16),
        pltpu.VMEM((192, 128), BF16), pltpu.VMEM((192, 128), BF16), pltpu.VMEM((4, 48, 128), BF16),
        pltpu.VMEM((TH, TW, 256), BF16),
        pltpu.VMEM((2, 24 * PITCH, 128), F32), pltpu.VMEM((2, 24 * PITCH, 128), F32),
        pltpu.VMEM((2, 22 * PITCH, 128), F32), pltpu.VMEM((2, 20 * GP, 128), F32),
        pltpu.VMEM((2, 18 * GP + 8, 128), F32), pltpu.VMEM((18 * GP + 8, 128), F32),
        pltpu.VMEM((18, TW, 256), BF16),
        pltpu.VMEM((256, 640), BF16), pltpu.VMEM((256, 256), BF16), pltpu.VMEM((256, 256), BF16),
        pltpu.VMEM((192, 256), BF16), pltpu.VMEM((256, 256), BF16), pltpu.VMEM((256, 256), BF16),
        pltpu.VMEM((256, 384), BF16), pltpu.VMEM((256, 384), BF16), pltpu.VMEM((384, 256), BF16),
        pltpu.VMEM((9, 256, 256), BF16), pltpu.VMEM((3, 256, 256), BF16),
        pltpu.VMEM((3, 256, 256), BF16), pltpu.VMEM((3, 256, 256), BF16),
        pltpu.VMEM((HEADS, KWIN * KWIN, 256), F32), pltpu.VMEM((4, KWIN * KWIN, 256), BF16),
        pltpu.VMEM((4, KWIN * KWIN, 256), BF16), pltpu.VMEM((4, 192, KWIN * KWIN), BF16),
        pltpu.VMEM((4, 256, 256), F32), pltpu.VMEM((14, KWIN * KWIN, 256), F32),
        pltpu.VMEM((2, KWIN * KWIN, 256), BF16), pltpu.VMEM((4, 192, 256), BF16),
        pltpu.VMEM((256, 256), F32), pltpu.VMEM((256, 256), BF16), pltpu.VMEM((256, 384), BF16),
        pltpu.VMEM((2, 64 * 16, 128), F32), pltpu.VMEM((2, 64, 16, 128), BF16),
        pltpu.SemaphoreType.DMA((2,)),
        pltpu.SemaphoreType.DMA((12,)), pltpu.SemaphoreType.DMA((10,)), pltpu.SemaphoreType.DMA((10,)),
        pltpu.SemaphoreType.DMA((14,)), pltpu.SemaphoreType.DMA((14,)),
    ]
    result = pl.pallas_call(
        functools.partial(kernel, nr, nc),
        out_shape=pltpu.VMEM((64, 2 * TH, 2 * TW), BF16),
        in_specs=[any_space] * len(operands),
        out_specs=pl.BlockSpec(memory_space=pl.ANY),
        scratch_shapes=scratch,
        compiler_params=pltpu.CompilerParams(
            collective_id=0, has_side_effects=True, vmem_limit_bytes=62 * 1024 * 1024
        ),
    )(*operands)
    return result


def solution(mesh):
    placed = (P("rows", "cols", None),) + (P(),) * 10
    body = functools.partial(on_device, mesh.shape["rows"], mesh.shape["cols"])
    return jax.shard_map(
        body, mesh=mesh, in_specs=placed, out_specs=P(None, "rows", "cols"), check_vma=False
    )
```
